32 devices in a mesh: noise: 4 (over y, x), row: 8 (over z, core).
Axes of the slice: x: 2, y: 2, z: 4, core: 2. Of those that a mesh axis runs over, the one named last changes fastest.
Arguments:
- activations: bfloat16 [16, 512, 768], P('noise', 'row'), may hold values from -6 to 6
- cond_scale: bfloat16 [16, 512, 768], P('noise', 'row'), may hold values from 0.25 to 16
- cond_shift: bfloat16 [16, 512, 768], P('noise', 'row'), may hold values from -4 to 4
- output_gate: bfloat16 [16, 512, 768], P('noise', 'row'), may hold values from -8 to 8
- pair_repr: bfloat16 [512, 512, 128], P('row', 'noise'), may hold values from -6 to 6
- bias_weight: bfloat16 [128, 8], replicated, may hold values from -1.5 to 1.5
- query_weight: bfloat16 [768, 384], P('noise'), may hold values from -0.21875 to 0.21875
- query_bias: bfloat16 [384], replicated, may hold values from -4 to 4
- key_weight: bfloat16 [768, 384], P('noise'), may hold values from -0.21875 to 0.21875
- value_weight: bfloat16 [768, 384], P('noise'), may hold values from -0.21875 to 0.21875
- output_weight: bfloat16 [384, 768], P('noise'), may hold values from -0.3125 to 0.3125
- token_mask: int32 [16, 512], P('noise', 'row'), may hold values from 0 to 1, as said below
Outputs:
- updated: bfloat16 [16, 512, 768], P('noise', 'row')
The draws below stay inside these ranges and needn't reach their ends.
Inputs may be any that keep to these rules, and one draw needn't show every extreme that they name: `token_mask`: in each sample the tokens with mask 1 form a prefix of half of 512 tokens or more, and some sample has all 512 tokens.
All inputs are finite; a program needn't handle non-finite values.
Results may differ from the reference program's by a relative error of at most 0.012.
The reference program's roundings to bfloat16 on the way count: a program that leaves them out, or rounds other values in their place, can miss the bound.
Values may be sent and summed in bfloat16 or wider, within the bound.
No kernel may reach another device: no remote copies, remote signals or barrier semaphores. Data moves between devices by JAX's collectives and lax.ppermute only.
A program may use at most 128 MiB of HBM per device.

```python
import math
import jax
import jax.numpy as jnp
from jax import lax

D = 768
HEADS = 8
HEAD_DIM = 48
PAIR_C = 128
ROW_TOKENS = 64
TOKENS = 512
SAMPLES = 16


def draw_cond_scale(key, part):
    key = jax.random.fold_in(key, 11)
    key_scales = jax.random.fold_in(key, 0)
    scales = jnp.exp(jax.random.uniform(key_scales, (SAMPLES, TOKENS, D), jnp.float32, math.log(0.5), math.log(2.0)))
    return scales.astype(jnp.bfloat16)


def draw_token_mask(key, part):
    key = jax.random.fold_in(key, 23)
    key_lengths, key_full = jax.random.split(key)
    lengths = jax.random.randint(key_lengths, (SAMPLES,), TOKENS // 2, TOKENS + 1)
    full_sample = jax.random.randint(key_full, (), 0, SAMPLES)
    lengths = jnp.where(jnp.arange(SAMPLES) == full_sample, TOKENS, lengths)
    return (jnp.arange(TOKENS)[None, :] < lengths[:, None]).astype(jnp.int32)


def levels(key, extent, cuts, low, high):
    def one(dim, parts):
        draws = jax.random.uniform(jax.random.fold_in(jax.random.fold_in(key, 6), dim), (parts,), jnp.float32, low / len(cuts), high / len(cuts))
        return jnp.repeat(jnp.exp(draws), extent[dim] // parts).reshape((-1,) + (1,) * (len(extent) - dim - 1))

    factor_of = one(*cuts[0])
    for cut in cuts[1:]:
        factor_of = factor_of * one(*cut)
    return factor_of


def normal_values(own_key, shape, scale, most, shards=(), held_as=jnp.bfloat16):
    result = scale * jax.random.normal(own_key, shape, jnp.float32)
    if shards:
        result = result * levels(own_key, shape, shards, -0.22, 0.18)
    return jnp.clip(result, -most, most).astype(held_as)


def setup_inputs(seed: int = 0) -> dict:
    seeds = jax.random.split(jax.random.key(seed), 13)
    return {
        "activations": normal_values(seeds[0], (SAMPLES, TOKENS, D), 1.0, 6.0, ((0, 4), (1, 8))),
        "cond_scale": draw_cond_scale(jax.random.fold_in(seeds[12], 71), 0),
        "cond_shift": normal_values(seeds[2], (SAMPLES, TOKENS, D), 0.5, 4.0, ((0, 4), (1, 8))),
        "output_gate": normal_values(seeds[3], (SAMPLES, TOKENS, D), 1.5, 8.0, ((0, 4), (1, 8))),
        "pair_repr": normal_values(seeds[4], (TOKENS, TOKENS, PAIR_C), 1.0, 6.0, ((0, 8), (1, 4))),
        "bias_weight": normal_values(seeds[5], (PAIR_C, HEADS), 0.25, 1.5),
        "query_weight": normal_values(seeds[6], (D, HEADS * HEAD_DIM), D ** -0.5, 0.21875, ((0, 4),)),
        "query_bias": normal_values(seeds[7], (HEADS * HEAD_DIM,), 1.0, 4.0),
        "key_weight": normal_values(seeds[8], (D, HEADS * HEAD_DIM), D ** -0.5, 0.21875, ((0, 4),)),
        "value_weight": normal_values(seeds[9], (D, HEADS * HEAD_DIM), D ** -0.5, 0.21875, ((0, 4),)),
        "output_weight": normal_values(seeds[10], (HEADS * HEAD_DIM, D), (HEADS * HEAD_DIM) ** -0.5, 0.3125, ((0, 4),)),
        "token_mask": draw_token_mask(jax.random.fold_in(seeds[12], 71), 0),
    }


epsilon = 1e-05
masked_score = -1e+30

def layer_norm(tensor):
    average = lax.optimization_barrier(jnp.mean(tensor, axis=-1, keepdims=True))
    centred = tensor - average
    variance = lax.optimization_barrier(jnp.mean(centred * centred, axis=-1, keepdims=True))
    return centred * lax.rsqrt(variance + epsilon)

def reference(activations, cond_scale, cond_shift, output_gate, pair_repr, bias_weight, query_weight, query_bias, key_weight, value_weight, output_weight, token_mask):
    head_features = HEADS * HEAD_DIM
    normed = layer_norm(activations.astype(jnp.float32))
    shifted = (cond_scale.astype(jnp.float32) * normed + cond_shift.astype(jnp.float32)).astype(jnp.bfloat16)
    flat_rows = shifted.reshape(SAMPLES * TOKENS, D)
    queries = (jnp.dot(flat_rows, query_weight, preferred_element_type=jnp.float32) + query_bias.astype(jnp.float32)).astype(jnp.bfloat16)
    key_rows = jnp.dot(flat_rows, key_weight, preferred_element_type=jnp.float32).astype(jnp.bfloat16)
    value_rows = jnp.dot(flat_rows, value_weight, preferred_element_type=jnp.float32).astype(jnp.bfloat16)

    def bias_block(block_rows):
        return jnp.einsum('ijc,ch->hij', layer_norm(block_rows.astype(jnp.float32)), bias_weight.astype(jnp.float32), precision=lax.Precision.HIGHEST).astype(jnp.bfloat16)
    blocks = lax.map(bias_block, pair_repr.reshape(TOKENS // ROW_TOKENS, ROW_TOKENS, TOKENS, PAIR_C))
    pair_bias = blocks.transpose(1, 0, 2, 3).reshape(HEADS, TOKENS, TOKENS)
    score_factor = 1.0 / math.sqrt(HEAD_DIM)

    def one_sample(inputs):
        query_one, key_one, value_one, valid_one = inputs
        query_heads = query_one.reshape(TOKENS, HEADS, HEAD_DIM).astype(jnp.float32)
        key_heads = key_one.reshape(TOKENS, HEADS, HEAD_DIM).astype(jnp.float32)
        value_heads = value_one.reshape(TOKENS, HEADS, HEAD_DIM).astype(jnp.float32)
        scores = jnp.einsum('ihd,jhd->hij', query_heads, key_heads, precision=lax.Precision.HIGHEST) * score_factor + pair_bias.astype(jnp.float32)
        scores = jnp.where(valid_one[None, None, :] > 0, scores, masked_score)
        highest = lax.optimization_barrier(jnp.max(scores, axis=-1, keepdims=True))
        weights = jnp.exp(scores - highest)
        summed = lax.optimization_barrier(jnp.sum(weights, axis=-1, keepdims=True))
        rounded = lax.optimization_barrier(weights.astype(jnp.bfloat16))
        mixture = jnp.einsum('hij,jhd->hid', rounded.astype(jnp.float32), value_heads, precision=lax.Precision.HIGHEST) / summed
        return mixture.transpose(1, 0, 2).reshape(TOKENS, head_features).astype(jnp.bfloat16)
    attended = lax.map(one_sample, (queries.reshape(SAMPLES, TOKENS, head_features), key_rows.reshape(SAMPLES, TOKENS, head_features), value_rows.reshape(SAMPLES, TOKENS, head_features), token_mask))
    projected = jnp.dot(attended.reshape(SAMPLES * TOKENS, head_features), output_weight, preferred_element_type=jnp.float32).reshape(SAMPLES, TOKENS, D)
    return (activations.astype(jnp.float32) + jax.nn.sigmoid(output_gate.astype(jnp.float32)) * projected).astype(jnp.bfloat16)
```

```python
import functools
import math

import jax
import jax.numpy as jnp
from jax import lax
from jax.experimental import pallas as pl
from jax.experimental.pallas import tpu as pltpu
from jax.sharding import PartitionSpec as P

epsilon = 1e-05
masked_score = -1e30
absent = 32768.0
log2_e = math.log2(math.e)


def layer_norm(tensor):
    average = jnp.mean(tensor, axis=-1, keepdims=True)
    centred = tensor - average
    variance = jnp.mean(centred * centred, axis=-1, keepdims=True)
    return centred * lax.rsqrt(variance + epsilon)


def shift_kernel(activations, cond_scale, cond_shift, token_mask, shifted, sent):
    samples, rows, features = activations.shape
    diagonal = lax.broadcasted_iota(jnp.int32, (rows, rows), 0) == lax.broadcasted_iota(
        jnp.int32, (rows, rows), 1
    )
    for s in range(samples):
        normed = layer_norm(activations[s].astype(jnp.float32))
        result = cond_scale[s].astype(jnp.float32) * normed + cond_shift[s].astype(jnp.float32)
        flags = jnp.where(diagonal, token_mask[s : s + 1, :].astype(jnp.float32), 0.0)
        valid = jnp.sum(flags, axis=1, keepdims=True) > 0.0
        shifted[s] = result.astype(jnp.bfloat16)
        sent[s] = jnp.where(valid, result, absent).astype(jnp.bfloat16)


def attend_kernel(noise_size, heads, *refs):
    (mine, other, weights_mine, weights_other, query_bias, shifted, activations, output_gate) = refs[:8]
    bias_parts = refs[8 : 8 + noise_size]
    updated, full_weights, full_output, full_bias, keys, values, spread = refs[8 + noise_size :]
    groups, _, rows, features = mine.shape
    head_features = query_bias.shape[1]
    width = head_features // heads
    tokens = keys.shape[0]
    core = lax.rem(lax.axis_index("row"), 2)
    place = lax.axis_index("noise")
    lane = lax.broadcasted_iota(jnp.int32, (1, head_features), 1)

    @pl.when(pl.program_id(0) == 0)
    def _():
        depth, breadth = weights_mine.shape[2:]
        out_rows = depth // 2

        def take(of_keys, of_queries):
            for k in range(noise_size):
                block = place ^ k
                down = pl.ds(pl.multiple_of(block * depth, math.gcd(depth, 64)), depth)
                full_weights[down, 0:breadth] = of_queries[k, 0]
                full_weights[down, breadth : 2 * breadth] = of_keys[k, 0]
                full_weights[down, 2 * breadth : 3 * breadth] = of_keys[k, 1]
                across = pl.ds(pl.multiple_of(block * out_rows, math.gcd(out_rows, 32)), out_rows)
                halves = of_queries[k, 1].astype(full_output.dtype)
                full_output[across, 0:breadth] = halves[0:out_rows]
                full_output[across, breadth : 2 * breadth] = halves[out_rows:depth]

        @pl.when(core == 0)
        def _():
            take(weights_mine, weights_other)

        @pl.when(core != 0)
        def _():
            take(weights_other, weights_mine)

        for k in range(noise_size):
            part = bias_parts[k]
            columns = part.shape[2]
            along = pl.ds(pl.multiple_of((place ^ k) * columns, 128), columns)
            full_bias[:, along] = part[...].reshape(heads * rows, columns).astype(jnp.float32) * log2_e

    for source, parity in ((mine, core), (other, 1 - core)):
        block = source[...].reshape(groups * rows, features)
        projected = jnp.dot(
            block, full_weights[:, head_features:], preferred_element_type=jnp.float32
        ).astype(jnp.bfloat16)
        penalty = jnp.where(block[:, 0:1].astype(jnp.float32) > absent / 2, masked_score, 0.0)
        penalty = jnp.broadcast_to(penalty, (groups * rows, 128)).astype(jnp.bfloat16)
        for g in range(groups):
            here = slice(g * rows, (g + 1) * rows)
            down = pl.ds(pl.multiple_of((2 * g + parity) * rows, rows), rows)
            keys[down, 0:head_features] = projected[here, 0:head_features]
            keys[down, head_features:] = penalty[here]
            values[down, :] = projected[here, head_features:]

    queries = (
        jnp.dot(shifted[0], full_weights[:, 0:head_features], preferred_element_type=jnp.float32)
        + query_bias[...].astype(jnp.float32)
    ).astype(jnp.bfloat16)
    one = (lax.broadcasted_iota(jnp.int32, (rows, 128), 1) == 0).astype(jnp.bfloat16)
    for h in range(heads):
        inside = ((lane >= h * width) & (lane < (h + 1) * width)).astype(jnp.bfloat16)
        spread[h * rows : (h + 1) * rows, 0:head_features] = queries * inside
        spread[h * rows : (h + 1) * rows, head_features:] = one
    scores = lax.dot_general(
        spread[...], keys[...], (((1,), (1,)), ((), ())), preferred_element_type=jnp.float32
    )
    scores = scores * (log2_e / math.sqrt(width)) + full_bias[...]
    probs = jnp.exp2(scores - jnp.max(scores, axis=1, keepdims=True))
    total = jnp.sum(probs, axis=1, keepdims=True)
    mixture = jnp.dot(probs.astype(jnp.bfloat16), values[...], preferred_element_type=jnp.float32) / total
    attended = jnp.zeros((rows, head_features), jnp.float32)
    for h in range(heads):
        inside = (lane >= h * width) & (lane < (h + 1) * width)
        attended = jnp.where(inside, mixture[h * rows : (h + 1) * rows], attended)
    projected = jnp.dot(
        attended.astype(jnp.bfloat16), full_output[...].astype(jnp.bfloat16), preferred_element_type=jnp.float32
    )
    gate = jax.nn.sigmoid(output_gate[0].astype(jnp.float32))
    updated[0] = (activations[0].astype(jnp.float32) + gate * projected).astype(jnp.bfloat16)


def swap_cores(array):
    return lax.ppermute(array, "row", [(i, i ^ 1) for i in range(lax.axis_size("row"))])


def from_noise(array, k):
    if k == 0:
        return array
    return lax.ppermute(array, "noise", [(i, i ^ k) for i in range(lax.axis_size("noise"))])


def body(
    activations,
    cond_scale,
    cond_shift,
    output_gate,
    pair_repr,
    bias_weight,
    query_weight,
    query_bias,
    key_weight,
    value_weight,
    output_weight,
    token_mask,
):
    samples, rows, features = activations.shape
    heads = bias_weight.shape[1]
    head_features = query_weight.shape[1]
    row_size, noise_size = lax.axis_size("row"), lax.axis_size("noise")
    tokens = rows * row_size
    groups = row_size // 2
    core = lax.rem(lax.axis_index("row"), 2)

    shifted, sent = pl.pallas_call(
        shift_kernel,
        out_shape=[jax.ShapeDtypeStruct(activations.shape, jnp.bfloat16)] * 2,
        name="shift",
    )(activations, cond_scale, cond_shift, token_mask)
    mine = lax.all_gather(
        sent,
        "row",
        axis=0,
        axis_index_groups=[list(range(c, row_size, 2)) for c in range(2)],
    )
    other = swap_cores(mine)

    first = jnp.where(core == 0, key_weight, query_weight)
    output_halves = jnp.concatenate(
        [output_weight[:, :head_features], output_weight[:, head_features:]], axis=0
    )
    second = jnp.where(core == 0, value_weight, output_halves)
    half = jnp.stack([first, second])
    weights_mine = jnp.stack([from_noise(half, k) for k in range(noise_size)])
    weights_other = swap_cores(weights_mine)

    pair_normed = layer_norm(pair_repr.astype(jnp.float32))
    bias_tile = jnp.einsum(
        "ijc,ch->hij", pair_normed, bias_weight.astype(jnp.float32), precision=lax.Precision.HIGHEST
    ).astype(jnp.bfloat16)
    bias_parts = [from_noise(bias_tile, k) for k in range(noise_size)]

    whole = lambda array: pl.BlockSpec(array.shape, lambda s: (0,) * array.ndim)
    per_sample = pl.BlockSpec((1, rows, features), lambda s: (s, 0, 0))
    gathered = pl.BlockSpec((groups, 1, rows, features), lambda s: (0, s, 0, 0))
    bias_row = query_bias.reshape(1, head_features)
    padded = head_features + 128
    output_type = jnp.float32 if output_weight.shape[0] % 16 else jnp.bfloat16
    return pl.pallas_call(
        functools.partial(attend_kernel, noise_size, heads),
        grid=(samples,),
        in_specs=[
            gathered,
            gathered,
            whole(weights_mine),
            whole(weights_other),
            whole(bias_row),
            per_sample,
            per_sample,
            per_sample,
        ]
        + [whole(bias_tile)] * noise_size,
        out_specs=per_sample,
        out_shape=jax.ShapeDtypeStruct(activations.shape, jnp.bfloat16),
        scratch_shapes=[
            pltpu.VMEM((features, 3 * head_features), jnp.bfloat16),
            pltpu.VMEM((head_features, features), output_type),
            pltpu.VMEM((heads * rows, tokens), jnp.float32),
            pltpu.VMEM((tokens, padded), jnp.bfloat16),
            pltpu.VMEM((tokens, head_features), jnp.bfloat16),
            pltpu.VMEM((heads * rows, padded), jnp.bfloat16),
        ],
        compiler_params=pltpu.CompilerParams(vmem_limit_bytes=56 * 2**20),
        name="attend",
    )(
        mine,
        other,
        weights_mine,
        weights_other,
        bias_row,
        shifted,
        activations,
        output_gate,
        *bias_parts,
    )


def solution(mesh):
    return jax.shard_map(
        body,
        mesh=mesh,
        in_specs=(
            P("noise", "row", None),
            P("noise", "row", None),
            P("noise", "row", None),
            P("noise", "row", None),
            P("row", "noise", None),
            P(),
            P("noise", None),
            P(),
            P("noise", None),
            P("noise", None),
            P("noise", None),
            P("noise", "row"),
        ),
        out_specs=P("noise", "row", None),
        check_vma=False,
    )
```

```python
import functools
import math

import jax
import jax.numpy as jnp
from jax import lax
from jax.experimental import pallas as pl
from jax.experimental.pallas import tpu as pltpu
from jax.sharding import PartitionSpec as P

epsilon = 1e-05
masked_score = -1e30
absent = 32768.0
log2_e = math.log2(math.e)
vmem_bytes = 40 * 2**20


def layer_norm(tensor):
    average = jnp.mean(tensor, axis=-1, keepdims=True)
    centred = tensor - average
    variance = jnp.mean(centred * centred, axis=-1, keepdims=True)
    return centred * lax.rsqrt(variance + epsilon)


def shift_kernel(activations, cond_scale, cond_shift, token_mask, shifted, sent):
    samples, rows, features = activations.shape
    diagonal = lax.broadcasted_iota(jnp.int32, (rows, rows), 0) == lax.broadcasted_iota(
        jnp.int32, (rows, rows), 1
    )
    for s in range(samples):
        normed = layer_norm(activations[s].astype(jnp.float32))
        result = cond_scale[s].astype(jnp.float32) * normed + cond_shift[s].astype(jnp.float32)
        flags = jnp.where(diagonal, token_mask[s : s + 1, :].astype(jnp.float32), 0.0)
        valid = jnp.sum(flags, axis=1, keepdims=True) > 0.0
        shifted[s] = result.astype(jnp.bfloat16)
        sent[s] = jnp.where(valid, result, absent).astype(jnp.bfloat16)


def attend_blocks(heads, s, blocks, bias_of, queries, key_weight, value_weight, spread):
    head_features = key_weight.shape[1]
    width = head_features // heads
    count = queries.shape[1]
    lane = lax.broadcasted_iota(jnp.int32, (1, head_features), 1)
    tokens = jnp.concatenate([block[s] for block in blocks], axis=0)
    rows = blocks[0].shape[1]
    keys = jnp.dot(tokens, key_weight[...], preferred_element_type=jnp.float32).astype(jnp.bfloat16)
    penalty = jnp.where(tokens[:, 0:1].astype(jnp.float32) > absent / 2, masked_score, 0.0)
    penalty = jnp.broadcast_to(penalty, (tokens.shape[0], 128)).astype(jnp.bfloat16)
    keys = jnp.concatenate([keys, penalty], axis=1)
    values = lax.dot_general(
        value_weight[...], tokens, (((1,), (1,)), ((), ())), preferred_element_type=jnp.float32
    ).astype(jnp.bfloat16)
    one = (lax.broadcasted_iota(jnp.int32, (count, 128), 1) == 0).astype(jnp.bfloat16)
    own = queries[s]
    for h in range(heads):
        inside = ((lane >= h * width) & (lane < (h + 1) * width)).astype(jnp.bfloat16)
        spread[h * count : (h + 1) * count, 0:head_features] = own * inside
        spread[h * count : (h + 1) * count, head_features:] = one
    scores = lax.dot_general(
        keys, spread[...], (((1,), (1,)), ((), ())), preferred_element_type=jnp.float32
    ) * (log2_e / math.sqrt(width))
    sums, highs, totals = [], [], []
    for h in range(heads):
        bias = jnp.concatenate([bias_of(b, h) for b in range(len(blocks))], axis=0)
        score = scores[:, h * count : (h + 1) * count] + bias.astype(jnp.float32) * log2_e
        high = jnp.max(score, axis=0, keepdims=True)
        probs = jnp.exp2(score - high)
        totals.append(jnp.sum(probs, axis=0, keepdims=True))
        highs.append(high)
        sums.append(
            jnp.dot(
                values[h * width : (h + 1) * width],
                probs.astype(jnp.bfloat16),
                preferred_element_type=jnp.float32,
            )
        )
    return sums, highs, totals


def bias_picker(bias_parts, steps, first):
    chip = lax.axis_index("row") // 2
    place = lax.axis_index("noise")

    def pick(b, h):
        origin = lax.rem(chip - (first + b) + steps, steps)
        return bias_parts[origin ^ place, h]

    return pick


def early_kernel(steps, heads, weights_mine, weights_other, query_bias, shifted, shifted_other, bias_parts, *refs):
    blocks = refs[: steps - 1]
    partial, queries, key_weight, value_weight, output_weight, query_weight, spread, stage = refs[steps - 1 :]
    noise_size, _, depth, breadth = weights_mine.shape
    samples, rows, features = shifted.shape
    width = breadth // heads
    out_rows = depth // 2
    core = lax.rem(lax.axis_index("row"), 2)
    place = lax.axis_index("noise")

    def take(of_keys, of_queries):
        for k in range(noise_size):
            block = place ^ k
            down = pl.ds(pl.multiple_of(block * depth, math.gcd(depth, 64)), depth)
            query_weight[down, :] = of_queries[k, 0]
            key_weight[down, :] = of_keys[k, 0]
            stage[down, :] = of_keys[k, 1].astype(jnp.float32)
            across = pl.ds(pl.multiple_of(block * out_rows, math.gcd(out_rows, 32)), out_rows)
            halves = of_queries[k, 1].astype(output_weight.dtype)
            output_weight[across, 0:breadth] = halves[0:out_rows]
            output_weight[across, breadth : 2 * breadth] = halves[out_rows:depth]

    @pl.when(core == 0)
    def _():
        take(weights_mine, weights_other)
        queries[:, 0:rows] = shifted_queries(shifted, query_weight, query_bias)
        queries[:, rows : 2 * rows] = shifted_queries(shifted_other, query_weight, query_bias)

    @pl.when(core != 0)
    def _():
        take(weights_other, weights_mine)
        queries[:, 0:rows] = shifted_queries(shifted_other, query_weight, query_bias)
        queries[:, rows : 2 * rows] = shifted_queries(shifted, query_weight, query_bias)

    value_weight[...] = stage[...].T.astype(jnp.bfloat16)
    pick = bias_picker(bias_parts, steps, 0)
    for s in range(samples):
        sums, highs, totals = attend_blocks(
            heads, s, blocks, pick, queries, key_weight, value_weight, spread
        )
        for h in range(heads):
            partial[s, h * width : (h + 1) * width] = sums[h]
            partial[s, breadth + h : breadth + h + 1] = highs[h]
            partial[s, breadth + heads + h : breadth + heads + h + 1] = totals[h]


def shifted_queries(shifted, query_weight, query_bias):
    samples, rows, features = shifted.shape
    result = jnp.dot(
        shifted[...].reshape(samples * rows, features),
        query_weight[...],
        preferred_element_type=jnp.float32,
    ) + query_bias[...].astype(jnp.float32)
    return result.astype(jnp.bfloat16).reshape(samples, rows, -1)


def late_kernel(steps, heads, partial, queries, key_weight, value_weight, bias_parts, block, keep, give, merged, spread):
    samples = block.shape[0]
    breadth = key_weight.shape[1]
    width = breadth // heads
    core = lax.rem(lax.axis_index("row"), 2)
    pick = bias_picker(bias_parts, steps, steps - 1)
    for s in range(samples):
        sums, highs, totals = attend_blocks(
            heads, s, [block], pick, queries, key_weight, value_weight, spread
        )
        for h in range(heads):
            at_high = slice(breadth + h, breadth + h + 1)
            at_total = slice(breadth + heads + h, breadth + heads + h + 1)
            before = partial[s, at_high]
            high = jnp.maximum(before, highs[h])
            old, new = jnp.exp2(before - high), jnp.exp2(highs[h] - high)
            across = slice(h * width, (h + 1) * width)
            merged[s, across] = partial[s, across] * old + sums[h] * new
            merged[s, at_high] = high
            merged[s, at_total] = partial[s, at_total] * old + totals[h] * new
    half = merged.shape[2] // 2
    left = lax.broadcasted_iota(jnp.int32, (1, 2 * half), 1) < half
    for pair in range(samples // 2):
        a, b = merged[2 * pair], merged[2 * pair + 1]
        turned_a, turned_b = pltpu.roll(a, half, 1), pltpu.roll(b, half, 1)
        of_first, of_second = jnp.where(left, a, turned_b), jnp.where(left, turned_a, b)
        keep[pair] = jnp.where(core == 0, of_first, of_second)
        give[pair] = jnp.where(core == 0, of_second, of_first)


def finish_kernel(heads, keep, got, output_weight, activations, output_gate, updated):
    pairs = keep.shape[0]
    breadth = output_weight.shape[0]
    width = breadth // heads
    rows, features = updated.shape[1:]
    for pair in range(pairs):
        parts = []
        for h in range(heads):
            at_high = slice(breadth + h, breadth + h + 1)
            at_total = slice(breadth + heads + h, breadth + heads + h + 1)
            across = slice(h * width, (h + 1) * width)
            high = jnp.maximum(keep[pair, at_high], got[pair, at_high])
            mine, theirs = jnp.exp2(keep[pair, at_high] - high), jnp.exp2(got[pair, at_high] - high)
            total = keep[pair, at_total] * mine + got[pair, at_total] * theirs
            parts.append((keep[pair, across] * mine + got[pair, across] * theirs) / total)
        attended = jnp.concatenate(parts, axis=0).T.astype(jnp.bfloat16)
        projected = jnp.dot(
            attended, output_weight[...].astype(jnp.bfloat16), preferred_element_type=jnp.float32
        )
        for side in range(2):
            s = 2 * pair + side
            gate = jax.nn.sigmoid(output_gate[s].astype(jnp.float32))
            updated[s] = (
                activations[s].astype(jnp.float32) + gate * projected[side * rows : (side + 1) * rows]
            ).astype(jnp.bfloat16)


def swap_cores(array):
    return lax.ppermute(array, "row", [(i, i ^ 1) for i in range(lax.axis_size("row"))])


def next_chip(array):
    size = lax.axis_size("row")
    return lax.ppermute(array, "row", [(i, (i + 2) % size) for i in range(size)])


def from_noise(array, k):
    if k == 0:
        return array
    return lax.ppermute(array, "noise", [(i, i ^ k) for i in range(lax.axis_size("noise"))])


def body(
    activations,
    cond_scale,
    cond_shift,
    output_gate,
    pair_repr,
    bias_weight,
    query_weight,
    query_bias,
    key_weight,
    value_weight,
    output_weight,
    token_mask,
):
    samples, rows, features = activations.shape
    heads = bias_weight.shape[1]
    head_features = query_weight.shape[1]
    noise_size = lax.axis_size("noise")
    steps = lax.axis_size("row") // 2
    assert noise_size == steps and pair_repr.shape[1] == 2 * rows
    core = lax.rem(lax.axis_index("row"), 2)
    bf16, f32 = jnp.bfloat16, jnp.float32
    params = pltpu.CompilerParams(vmem_limit_bytes=vmem_bytes)
    struct = jax.ShapeDtypeStruct

    shifted, sent = pl.pallas_call(
        shift_kernel,
        out_shape=[struct(activations.shape, bf16)] * 2,
        name="shift",
    )(activations, cond_scale, cond_shift, token_mask)
    blocks = [sent, next_chip(sent)]
    shifted_other = swap_cores(shifted)

    first = jnp.where(core == 0, key_weight, query_weight)
    output_halves = jnp.concatenate(
        [output_weight[:, :head_features], output_weight[:, head_features:]], axis=0
    )
    second = jnp.where(core == 0, value_weight, output_halves)
    half = jnp.stack([first, second])
    weights_mine = jnp.stack([from_noise(half, k) for k in range(noise_size)])

    pair_normed = layer_norm(pair_repr.astype(f32))
    bias_tile = jnp.einsum(
        "ijc,ch->hji", pair_normed, bias_weight.astype(f32), precision=lax.Precision.HIGHEST
    ).astype(bf16)
    low, up = bias_tile[:, :rows], bias_tile[:, rows:]
    bias_mine, bias_theirs = jnp.where(core == 0, low, up), jnp.where(core == 0, up, low)
    blocks[1], bias_mine, bias_theirs = lax.optimization_barrier((blocks[1], bias_mine, bias_theirs))
    bias_got = swap_cores(bias_theirs)
    blocks.append(next_chip(blocks[1]))
    bias_chip = jnp.where(
        core == 0,
        jnp.concatenate([bias_mine, bias_got], axis=2),
        jnp.concatenate([bias_got, bias_mine], axis=2),
    )
    bias_parts = jnp.stack([from_noise(bias_chip, k) for k in range(noise_size)])
    weights_other = swap_cores(weights_mine)
    for _ in range(steps - 3):
        blocks.append(next_chip(blocks[-1]))
    last = blocks.pop()

    bias_row = query_bias.reshape(1, head_features)
    padded = head_features + 128
    spread = pltpu.VMEM((heads * 2 * rows, padded), bf16)
    record = head_features + 2 * heads
    output_type = f32 if output_weight.shape[0] % 16 else bf16
    partial, queries, key_full, value_full, output_full = pl.pallas_call(
        functools.partial(early_kernel, steps, heads),
        out_shape=[
            struct((samples, record, 2 * rows), f32),
            struct((samples, 2 * rows, head_features), bf16),
            struct((features, head_features), bf16),
            struct((head_features, features), bf16),
            struct((head_features, features), output_type),
        ],
        scratch_shapes=[
            pltpu.VMEM((features, head_features), bf16),
            spread,
            pltpu.VMEM((features, head_features), f32),
        ],
        compiler_params=params,
        name="early",
    )(weights_mine, weights_other, bias_row, shifted, shifted_other, bias_parts, *blocks)
    keep, give = pl.pallas_call(
        functools.partial(late_kernel, steps, heads),
        out_shape=[struct((samples // 2, record, 2 * rows), f32)] * 2,
        scratch_shapes=[pltpu.VMEM((samples, record, 2 * rows), f32), spread],
        compiler_params=params,
        name="late",
    )(partial, queries, key_full, value_full, bias_parts, last)
    got = swap_cores(give)
    return pl.pallas_call(
        functools.partial(finish_kernel, heads),
        out_shape=struct(activations.shape, bf16),
        compiler_params=params,
        name="finish",
    )(keep, got, output_full, activations, output_gate)


def solution(mesh):
    return jax.shard_map(
        body,
        mesh=mesh,
        in_specs=(
            P("noise", "row", None),
            P("noise", "row", None),
            P("noise", "row", None),
            P("noise", "row", None),
            P("row", "noise", None),
            P(),
            P("noise", None),
            P(),
            P("noise", None),
            P("noise", None),
            P("noise", None),
            P("noise", "row"),
        ),
        out_specs=P("noise", "row", None),
        check_vma=False,
    )
```

```python
import functools
import math

import jax
import jax.numpy as jnp
from jax import lax
from jax.experimental import pallas as pl
from jax.experimental.pallas import tpu as pltpu
from jax.sharding import PartitionSpec as P

epsilon = 1e-05
masked_score = -1e30
absent = 32768.0
log2_e = math.log2(math.e)
vmem_bytes = 40 * 2**20


def layer_norm(tensor):
    average = jnp.mean(tensor, axis=-1, keepdims=True)
    centred = tensor - average
    variance = jnp.mean(centred * centred, axis=-1, keepdims=True)
    return centred * lax.rsqrt(variance + epsilon)


def shift_kernel(
    activations, cond_scale, cond_shift, token_mask, query_weight, key_weight, value_weight, shifted, sent, packed
):
    samples, rows, features = activations.shape
    diagonal = lax.broadcasted_iota(jnp.int32, (rows, rows), 0) == lax.broadcasted_iota(
        jnp.int32, (rows, rows), 1
    )
    for s in range(samples):
        normed = layer_norm(activations[s].astype(jnp.float32))
        result = cond_scale[s].astype(jnp.float32) * normed + cond_shift[s].astype(jnp.float32)
        flags = jnp.where(diagonal, token_mask[s : s + 1, :].astype(jnp.float32), 0.0)
        valid = jnp.sum(flags, axis=1, keepdims=True) > 0.0
        shifted[s] = result.astype(jnp.bfloat16)
        sent[s] = jnp.where(valid, result, absent).astype(jnp.bfloat16)
    core = lax.rem(lax.axis_index("row"), 2)
    half, breadth = packed.shape[0], query_weight.shape[1]
    for w, weight in enumerate((query_weight, key_weight, value_weight)):
        whole = weight[...].astype(jnp.float32)
        packed[:, w * breadth : (w + 1) * breadth] = jnp.where(
            core == 0, whole[:half], whole[half:]
        ).astype(jnp.bfloat16)


def bias_kernel(pair, weights, tile, collected):
    step = pl.program_id(0)
    per, columns, channels = pair.shape
    heads = weights.shape[0]
    rows = collected.shape[0] // heads
    normed = layer_norm(pair[...].reshape(per * columns, channels).astype(jnp.float32))
    upper = normed.astype(jnp.bfloat16)
    lower = (normed - upper.astype(jnp.float32)).astype(jnp.bfloat16)
    result = lax.dot_general(
        weights[...],
        jnp.concatenate([upper, lower], axis=1),
        (((1,), (1,)), ((), ())),
        preferred_element_type=jnp.float32,
    )
    for r in range(per):
        at = pl.ds(pl.multiple_of((step * per + r) * heads, heads), heads)
        collected[at, :] = result[:, r * columns : (r + 1) * columns]

    @pl.when(step == pl.num_programs(0) - 1)
    def _():
        core = lax.rem(lax.axis_index("row"), 2)
        half = columns // 2
        for h in range(heads):
            turned = collected[pl.ds(h, rows, stride=heads), :].T
            low, up = turned[:half], turned[half:]
            both = [jnp.where(core == 0, low, up), jnp.where(core == 0, up, low)]
            tile[h] = jnp.concatenate(both, axis=1).astype(jnp.bfloat16)


def attend_blocks(heads, s, place, blocks, bias_of, queries, key_weight, value_weight, spread):
    head_features = key_weight.shape[1]
    width = head_features // heads
    count = queries.shape[1]
    lane = lax.broadcasted_iota(jnp.int32, (1, head_features), 1)
    tokens = jnp.concatenate([block[place] for block in blocks], axis=0)
    rows = blocks[0].shape[1]
    keys = jnp.dot(tokens, key_weight[...], preferred_element_type=jnp.float32).astype(jnp.bfloat16)
    penalty = jnp.where(tokens[:, 0:1].astype(jnp.float32) > absent / 2, masked_score, 0.0)
    penalty = jnp.broadcast_to(penalty, (tokens.shape[0], 128)).astype(jnp.bfloat16)
    keys = jnp.concatenate([keys, penalty], axis=1)
    values = lax.dot_general(
        value_weight[...], tokens, (((1,), (1,)), ((), ())), preferred_element_type=jnp.float32
    ).astype(jnp.bfloat16)
    one = (lax.broadcasted_iota(jnp.int32, (count, 128), 1) == 0).astype(jnp.bfloat16)
    own = queries[s]
    for h in range(heads):
        inside = ((lane >= h * width) & (lane < (h + 1) * width)).astype(jnp.bfloat16)
        spread[h * count : (h + 1) * count, 0:head_features] = own * inside
        spread[h * count : (h + 1) * count, head_features:] = one
    scores = lax.dot_general(
        keys, spread[...], (((1,), (1,)), ((), ())), preferred_element_type=jnp.float32
    ) * (log2_e / math.sqrt(width))
    sums, highs, totals = [], [], []
    for h in range(heads):
        bias = jnp.concatenate([bias_of(b, h) for b in range(len(blocks))], axis=0)
        score = scores[:, h * count : (h + 1) * count] + bias * log2_e
        high = jnp.max(score, axis=0, keepdims=True)
        probs = jnp.exp2(score - high)
        totals.append(jnp.sum(probs, axis=0, keepdims=True))
        highs.append(high)
        sums.append(
            jnp.dot(
                values[h * width : (h + 1) * width],
                probs.astype(jnp.bfloat16),
                preferred_element_type=jnp.float32,
            )
        )
    return sums, highs, totals


def bias_picker(bias_mine, bias_other, steps, first):
    chip = lax.axis_index("row") // 2
    place = lax.axis_index("noise")
    width = bias_mine.shape[3]
    own = lax.broadcasted_iota(jnp.int32, (1, width), 1) < width // 2

    def pick(b, h):
        part = lax.rem(chip - (first + b) + steps, steps) ^ place
        return jnp.where(own, bias_mine[part, h].astype(jnp.float32), bias_other[part, h].astype(jnp.float32))

    return pick


def early_kernel(steps, heads, weights_mine, weights_other, query_bias, shifted, shifted_other, bias_mine, bias_other, *refs):
    blocks = refs[: steps - 1]
    partial, queries, key_weight, value_weight, full, spread = refs[steps - 1 :]
    noise_size, half, _ = weights_mine.shape
    samples, rows, features = shifted.shape
    breadth = key_weight.shape[1]
    width = breadth // heads
    core = lax.rem(lax.axis_index("row"), 2)
    place = lax.axis_index("noise")
    for part, of_core in ((weights_mine, core), (weights_other, 1 - core)):
        for k in range(noise_size):
            start = ((place ^ k) * 2 + of_core) * half
            down = pl.ds(pl.multiple_of(start, math.gcd(half, 32)), half)
            full[down, :] = part[k].astype(full.dtype)
    key_weight[...] = full[:, breadth : 2 * breadth].astype(jnp.bfloat16)
    value_weight[...] = full[:, 2 * breadth :].astype(jnp.float32).T.astype(jnp.bfloat16)
    for side, tokens in enumerate((shifted, shifted_other)):
        result = jnp.dot(
            tokens[...].reshape(samples * rows, features),
            full[:, 0:breadth].astype(jnp.bfloat16),
            preferred_element_type=jnp.float32,
        ) + query_bias[...].astype(jnp.float32)
        queries[:, side * rows : (side + 1) * rows] = result.astype(jnp.bfloat16).reshape(
            samples, rows, breadth
        )

    pick = bias_picker(bias_mine, bias_other, steps, 0)
    for s in range(samples):
        sums, highs, totals = attend_blocks(
            heads, s, s, blocks, pick, queries, key_weight, value_weight, spread
        )
        for h in range(heads):
            partial[s, h * width : (h + 1) * width] = sums[h]
            partial[s, breadth + h : breadth + h + 1] = highs[h]
            partial[s, breadth + heads + h : breadth + heads + h + 1] = totals[h]


def late_kernel(
    steps, heads, first, partial, queries, key_weight, value_weight, bias_mine, bias_other, block, keep, give, merged, spread
):
    samples = merged.shape[0]
    breadth = key_weight.shape[1]
    width = breadth // heads
    pick = bias_picker(bias_mine, bias_other, steps, steps - 1)
    for s in range(samples):
        sums, highs, totals = attend_blocks(
            heads, first + s, first + s, [block], pick, queries, key_weight, value_weight, spread
        )
        before = partial.at[first + s]
        for h in range(heads):
            at_high = slice(breadth + h, breadth + h + 1)
            at_total = slice(breadth + heads + h, breadth + heads + h + 1)
            high = jnp.maximum(before[at_high], highs[h])
            old, new = jnp.exp2(before[at_high] - high), jnp.exp2(highs[h] - high)
            across = slice(h * width, (h + 1) * width)
            merged[s, across] = before[across] * old + sums[h] * new
            merged[s, at_high] = high
            merged[s, at_total] = before[at_total] * old + totals[h] * new
    half = merged.shape[2] // 2
    left = lax.broadcasted_iota(jnp.int32, (1, 2 * half), 1) < half
    for pair in range(samples // 2):
        a, b = merged[2 * pair], merged[2 * pair + 1]
        keep[pair] = jnp.where(left, a, pltpu.roll(b, half, 1))
        give[pair] = jnp.where(left, pltpu.roll(a, half, 1), b)


def finish_kernel(heads, chunks, weight_parts, activations, output_gate, *refs):
    keep, got = refs[:chunks], refs[chunks : 2 * chunks]
    updated, output_weight = refs[2 * chunks :]
    noise_size, part_rows, _ = weight_parts.shape
    breadth = output_weight.shape[0]
    width = breadth // heads
    rows = updated.shape[1]
    place = lax.axis_index("noise")
    for k in range(noise_size):
        down = pl.ds(pl.multiple_of((place ^ k) * part_rows, math.gcd(part_rows, 32)), part_rows)
        output_weight[down, :] = weight_parts[k].astype(output_weight.dtype)
    pairs = keep[0].shape[0]
    for pair in range(chunks * pairs):
        own, other = keep[pair // pairs].at[pair % pairs], got[pair // pairs].at[pair % pairs]
        parts = []
        for h in range(heads):
            at_high = slice(breadth + h, breadth + h + 1)
            at_total = slice(breadth + heads + h, breadth + heads + h + 1)
            across = slice(h * width, (h + 1) * width)
            high = jnp.maximum(own[at_high], other[at_high])
            mine, theirs = jnp.exp2(own[at_high] - high), jnp.exp2(other[at_high] - high)
            total = own[at_total] * mine + other[at_total] * theirs
            parts.append((own[across] * mine + other[across] * theirs) / total)
        attended = jnp.concatenate(parts, axis=0).T.astype(jnp.bfloat16)
        projected = jnp.dot(
            attended, output_weight[...].astype(jnp.bfloat16), preferred_element_type=jnp.float32
        )
        for side in range(2):
            s = 2 * pair + side
            gate = jax.nn.sigmoid(output_gate[s].astype(jnp.float32))
            updated[s] = (
                activations[s].astype(jnp.float32) + gate * projected[side * rows : (side + 1) * rows]
            ).astype(jnp.bfloat16)


def swap_cores(array):
    return lax.ppermute(array, "row", [(i, i ^ 1) for i in range(lax.axis_size("row"))])


def next_chip(array):
    size = lax.axis_size("row")
    return lax.ppermute(array, "row", [(i, (i + 2) % size) for i in range(size)])


def from_noise(array, k):
    if k == 0:
        return array
    return lax.ppermute(array, "noise", [(i, i ^ k) for i in range(lax.axis_size("noise"))])


def body(
    activations,
    cond_scale,
    cond_shift,
    output_gate,
    pair_repr,
    bias_weight,
    query_weight,
    query_bias,
    key_weight,
    value_weight,
    output_weight,
    token_mask,
):
    samples, rows, features = activations.shape
    heads = bias_weight.shape[1]
    head_features = query_weight.shape[1]
    noise_size = lax.axis_size("noise")
    steps = lax.axis_size("row") // 2
    assert noise_size == steps and pair_repr.shape[1] == 2 * rows
    bf16, f32 = jnp.bfloat16, jnp.float32
    params = pltpu.CompilerParams(vmem_limit_bytes=vmem_bytes)
    struct = jax.ShapeDtypeStruct
    after = lax.optimization_barrier
    half = query_weight.shape[0] // 2

    shifted, sent, packed = pl.pallas_call(
        shift_kernel,
        out_shape=[struct(activations.shape, bf16)] * 2 + [struct((half, 3 * head_features), bf16)],
        compiler_params=params,
        name="shift",
    )(activations, cond_scale, cond_shift, token_mask, query_weight, key_weight, value_weight)

    ring = [sent, next_chip(sent)]
    weights_mine = jnp.stack([from_noise(packed, k) for k in range(noise_size)])
    shifted_other = swap_cores(shifted)
    pair_repr, _ = after((pair_repr, packed))
    per = 8
    columns, channels = pair_repr.shape[1:]
    twice = jnp.concatenate([bias_weight.T, bias_weight.T], axis=1)
    bias_tile = pl.pallas_call(
        bias_kernel,
        grid=(rows // per,),
        in_specs=[
            pl.BlockSpec((per, columns, channels), lambda i: (i, 0, 0)),
            pl.BlockSpec((heads, 2 * channels), lambda i: (0, 0)),
        ],
        out_specs=pl.BlockSpec((heads, rows, columns), lambda i: (0, 0, 0)),
        out_shape=struct((heads, rows, columns), bf16),
        scratch_shapes=[pltpu.VMEM((rows * heads, columns), f32)],
        compiler_params=params,
        name="bias",
    )(pair_repr, twice)

    ring[1], weights_mine, shifted_other, bias_tile = after((ring[1], weights_mine, shifted_other, bias_tile))
    ring.append(next_chip(ring[1]))
    bias_mine = jnp.stack([from_noise(bias_tile, k) for k in range(noise_size)])
    weights_other = swap_cores(weights_mine)

    ring[2], bias_mine, weights_other, output_weight = after((ring[2], bias_mine, weights_other, output_weight))
    for _ in range(steps - 3):
        ring.append(next_chip(ring[-1]))
    last = ring.pop()
    bias_other = swap_cores(bias_mine)
    output_parts = jnp.stack([from_noise(output_weight, k) for k in range(noise_size)])

    bias_row = query_bias.reshape(1, head_features)
    spread = pltpu.VMEM((heads * 2 * rows, head_features + 128), bf16)
    record = head_features + 2 * heads
    full_type = f32 if half % 16 else bf16
    output_type = f32 if output_weight.shape[0] % 16 else bf16
    partial, queries, key_full, value_full = pl.pallas_call(
        functools.partial(early_kernel, steps, heads),
        out_shape=[
            struct((samples, record, 2 * rows), f32),
            struct((samples, 2 * rows, head_features), bf16),
            struct((features, head_features), bf16),
            struct((head_features, features), bf16),
        ],
        scratch_shapes=[pltpu.VMEM((features, 3 * head_features), full_type), spread],
        compiler_params=params,
        name="early",
    )(weights_mine, weights_other, bias_row, shifted, shifted_other, bias_mine, bias_other, *ring)
    keep, got = [], []
    chunks = 2
    each = samples // chunks
    for c in range(chunks):
        kept, give = pl.pallas_call(
            functools.partial(late_kernel, steps, heads, c * each),
            out_shape=[struct((each // 2, record, 2 * rows), f32)] * 2,
            scratch_shapes=[pltpu.VMEM((each, record, 2 * rows), f32), spread],
            compiler_params=params,
            name="late",
        )(partial, queries, key_full, value_full, bias_mine, bias_other, last)
        keep.append(kept)
        got.append(swap_cores(give))
    return pl.pallas_call(
        functools.partial(finish_kernel, heads, chunks),
        out_shape=struct(activations.shape, bf16),
        scratch_shapes=[pltpu.VMEM((head_features, features), output_type)],
        compiler_params=params,
        name="finish",
    )(output_parts, activations, output_gate, *keep, *got)


def solution(mesh):
    return jax.shard_map(
        body,
        mesh=mesh,
        in_specs=(
            P("noise", "row", None),
            P("noise", "row", None),
            P("noise", "row", None),
            P("noise", "row", None),
            P("row", "noise", None),
            P(),
            P("noise", None),
            P(),
            P("noise", None),
            P("noise", None),
            P("noise", None),
            P("noise", "row"),
        ),
        out_specs=P("noise", "row", None),
        check_vma=False,
    )
```

```python
import functools
import math

import jax
import jax.numpy as jnp
from jax import lax
from jax.experimental import pallas as pl
from jax.experimental.pallas import tpu as pltpu
from jax.sharding import PartitionSpec as P

epsilon = 1e-05
masked_score = -1e30
absent = 32768.0
log2_e = math.log2(math.e)
vmem_bytes = 40 * 2**20
wide_bytes = 60 * 2**20


def layer_norm(tensor):
    average = jnp.mean(tensor, axis=-1, keepdims=True)
    centred = tensor - average
    variance = jnp.mean(centred * centred, axis=-1, keepdims=True)
    return centred * lax.rsqrt(variance + epsilon)


def shift_kernel(
    activations_hbm,
    scale_hbm,
    shift_hbm,
    mask_hbm,
    query_hbm,
    key_hbm,
    shifted,
    sent,
    packed,
    activations,
    cond_scale,
    cond_shift,
    token_mask,
    query_weight,
    key_weight,
    sems,
):
    samples, rows, features = activations.shape
    copies = [pltpu.make_async_copy(mask_hbm, token_mask, sems.at[0])]
    for s in range(samples):
        for t, (source, target) in enumerate(
            ((activations_hbm, activations), (scale_hbm, cond_scale), (shift_hbm, cond_shift))
        ):
            copies.append(pltpu.make_async_copy(source.at[s], target.at[s], sems.at[1 + 3 * s + t]))
    copies.append(pltpu.make_async_copy(query_hbm, query_weight, sems.at[1 + 3 * samples]))
    copies.append(pltpu.make_async_copy(key_hbm, key_weight, sems.at[2 + 3 * samples]))
    for copy in copies:
        copy.start()
    diagonal = lax.broadcasted_iota(jnp.int32, (rows, rows), 0) == lax.broadcasted_iota(
        jnp.int32, (rows, rows), 1
    )
    copies[0].wait()
    for s in range(samples):
        for copy in copies[1 + 3 * s : 4 + 3 * s]:
            copy.wait()
        normed = layer_norm(activations[s].astype(jnp.float32))
        result = cond_scale[s].astype(jnp.float32) * normed + cond_shift[s].astype(jnp.float32)
        flags = jnp.where(diagonal, token_mask[s : s + 1, :].astype(jnp.float32), 0.0)
        valid = jnp.sum(flags, axis=1, keepdims=True) > 0.0
        shifted[s] = result.astype(jnp.bfloat16)
        sent[s] = jnp.where(valid, result, absent).astype(jnp.bfloat16)
    core = lax.rem(lax.axis_index("row"), 2)
    half, breadth = packed.shape[0], query_weight.shape[1]
    for w, weight in enumerate((query_weight, key_weight)):
        copies[1 + 3 * samples + w].wait()
        whole = weight[...].astype(jnp.float32)
        packed[:, w * breadth : (w + 1) * breadth] = jnp.where(
            core == 0, whole[:half], whole[half:]
        ).astype(jnp.bfloat16)


def bias_kernel(pair_hbm, value_hbm, weights, parcel, pair, value_weight, collected, sems):
    pieces, per, columns, channels = pair.shape
    heads = weights.shape[0]
    rows = pieces * per
    copies = [
        pltpu.make_async_copy(pair_hbm.at[pl.ds(i * per, per)], pair.at[i], sems.at[i]) for i in range(pieces)
    ]
    copies.append(pltpu.make_async_copy(value_hbm, value_weight, sems.at[pieces]))
    for copy in copies:
        copy.start()
    twice = jnp.concatenate([weights[...], weights[...]], axis=1)
    for i in range(pieces):
        copies[i].wait()
        normed = layer_norm(pair[i].reshape(per * columns, channels).astype(jnp.float32))
        upper = normed.astype(jnp.bfloat16)
        lower = (normed - upper.astype(jnp.float32)).astype(jnp.bfloat16)
        result = lax.dot_general(
            twice,
            jnp.concatenate([upper, lower], axis=1),
            (((1,), (1,)), ((), ())),
            preferred_element_type=jnp.float32,
        )
        for r in range(per):
            at = (i * per + r) * heads
            collected[at : at + heads, :] = result[:, r * columns : (r + 1) * columns]
    core = lax.rem(lax.axis_index("row"), 2)
    half = columns // 2
    for h in range(heads):
        turned = collected[pl.ds(h, rows, stride=heads), :].T
        low, up = turned[:half], turned[half:]
        both = [jnp.where(core == 0, low, up), jnp.where(core == 0, up, low)]
        parcel[h * half : (h + 1) * half, :] = jnp.concatenate(both, axis=1).astype(jnp.bfloat16)
    copies[pieces].wait()
    depth, breadth = value_weight.shape
    whole = value_weight[...].astype(jnp.float32)
    kept = jnp.where(core == 0, whole[: depth // 2], whole[depth // 2 :]).astype(jnp.bfloat16)
    for t in range(breadth // columns):
        at = heads * half + t * (depth // 2)
        parcel[at : at + depth // 2, :] = kept[:, t * columns : (t + 1) * columns]


def attend_keys(heads, keys, values, penalty, bias_of, queries):
    width = queries.shape[0] // heads
    sums, highs, totals = [], [], []
    for h in range(heads):
        across = slice(h * width, (h + 1) * width)
        score = jnp.dot(keys[:, across], queries[across, :], preferred_element_type=jnp.float32)
        score = score * (log2_e / math.sqrt(width)) + (bias_of(h) * log2_e + penalty)
        high = jnp.max(score, axis=0, keepdims=True)
        probs = jnp.exp2(score - high)
        totals.append(jnp.sum(probs, axis=0, keepdims=True))
        highs.append(high)
        sums.append(
            jnp.dot(values[across, :], probs.astype(jnp.bfloat16), preferred_element_type=jnp.float32)
        )
    return sums, highs, totals


def absent_penalty(tokens):
    return jnp.where(tokens[:, 0:1].astype(jnp.float32) > absent / 2, masked_score, 0.0)


def bias_picker(parcel_mine, parcel_other, steps, first, rows):
    chip = lax.axis_index("row") // 2
    place = lax.axis_index("noise")
    own = lax.broadcasted_iota(jnp.int32, (1, 2 * rows), 1) < rows

    def pick(b, h):
        part = lax.rem(chip - (first + b) + steps, steps) ^ place
        at = slice(h * rows, (h + 1) * rows)
        return jnp.where(own, parcel_mine[part, at].astype(jnp.float32), parcel_other[part, at].astype(jnp.float32))

    return pick


def early_kernel(
    steps, heads, weights_mine, weights_other, query_bias, shifted, shifted_other, parcel_mine, parcel_other, *refs
):
    blocks = refs[: steps - 1]
    partial, queries, key_weight, value_weight, full, full_value = refs[steps - 1 :]
    noise_size, half, _ = weights_mine.shape
    samples, rows, features = shifted.shape
    breadth = key_weight.shape[1]
    width = breadth // heads
    core = lax.rem(lax.axis_index("row"), 2)
    place = lax.axis_index("noise")
    for part, parcel, of_core in (
        (weights_mine, parcel_mine, core),
        (weights_other, parcel_other, 1 - core),
    ):
        for k in range(noise_size):
            start = ((place ^ k) * 2 + of_core) * half
            down = pl.ds(pl.multiple_of(start, math.gcd(half, 32)), half)
            full[down, :] = part[k].astype(full.dtype)
            for t in range(breadth // 128):
                at = heads * rows + t * half
                full_value[down, t * 128 : (t + 1) * 128] = parcel[k, at : at + half].astype(full.dtype)
    key_weight[...] = full[:, breadth : 2 * breadth].astype(jnp.bfloat16)
    value_weight[...] = full_value[...].astype(jnp.float32).T.astype(jnp.bfloat16)
    sides = []
    for tokens in (shifted, shifted_other):
        result = jnp.dot(
            tokens[...].reshape(samples * rows, features),
            full[:, 0:breadth].astype(jnp.bfloat16),
            preferred_element_type=jnp.float32,
        ) + query_bias[...].astype(jnp.float32)
        sides.append(result.astype(jnp.bfloat16).astype(jnp.float32))
    pick = bias_picker(parcel_mine, parcel_other, steps, 0, rows)
    for s in range(samples):
        both = [side[s * rows : (s + 1) * rows] for side in sides]
        queries[s] = jnp.concatenate(both, axis=0).T.astype(jnp.bfloat16)
        tokens = jnp.concatenate([block[s] for block in blocks], axis=0)
        keys = jnp.dot(tokens, key_weight[...], preferred_element_type=jnp.float32).astype(jnp.bfloat16)
        values = lax.dot_general(
            value_weight[...], tokens, (((1,), (1,)), ((), ())), preferred_element_type=jnp.float32
        ).astype(jnp.bfloat16)
        sums, highs, totals = attend_keys(
            heads,
            keys,
            values,
            absent_penalty(tokens),
            lambda h: jnp.concatenate([pick(b, h) for b in range(steps - 1)], axis=0),
            queries.at[s],
        )
        for h in range(heads):
            partial[s, h * width : (h + 1) * width] = sums[h]
            partial[s, breadth + h : breadth + h + 1] = highs[h]
            partial[s, breadth + heads + h : breadth + heads + h + 1] = totals[h]


def late_kernel(
    steps, heads, first, partial, queries, key_weight, value_weight, parcel_mine, parcel_other, block, keep, give, merged
):
    samples = merged.shape[0]
    _, rows, features = block.shape
    breadth = key_weight.shape[1]
    width = breadth // heads
    pick = bias_picker(parcel_mine, parcel_other, steps, steps - 1, rows)
    tokens = block[first : first + samples].reshape(samples * rows, features)
    all_keys = jnp.dot(tokens, key_weight[...], preferred_element_type=jnp.float32).astype(jnp.bfloat16)
    all_values = lax.dot_general(
        value_weight[...], tokens, (((1,), (1,)), ((), ())), preferred_element_type=jnp.float32
    ).astype(jnp.bfloat16)
    penalty = absent_penalty(tokens)
    for s in range(samples):
        here = slice(s * rows, (s + 1) * rows)
        sums, highs, totals = attend_keys(
            heads,
            all_keys[here],
            all_values[:, here],
            penalty[here],
            lambda h: pick(0, h),
            queries.at[first + s],
        )
        before = partial.at[first + s]
        for h in range(heads):
            at_high = slice(breadth + h, breadth + h + 1)
            at_total = slice(breadth + heads + h, breadth + heads + h + 1)
            high = jnp.maximum(before[at_high], highs[h])
            old, new = jnp.exp2(before[at_high] - high), jnp.exp2(highs[h] - high)
            across = slice(h * width, (h + 1) * width)
            merged[s, across] = before[across] * old + sums[h] * new
            merged[s, at_high] = high
            merged[s, at_total] = before[at_total] * old + totals[h] * new
    half = merged.shape[2] // 2
    left = lax.broadcasted_iota(jnp.int32, (1, 2 * half), 1) < half
    for pair in range(samples // 2):
        a, b = merged[2 * pair], merged[2 * pair + 1]
        keep[pair] = jnp.where(left, a, pltpu.roll(b, half, 1))
        give[pair] = jnp.where(left, pltpu.roll(a, half, 1), b)


def finish_kernel(heads, chunks, weight_parts, activations, output_gate, *refs):
    keep, got = refs[:chunks], refs[chunks : 2 * chunks]
    updated, output_weight = refs[2 * chunks :]
    noise_size, part_rows, _ = weight_parts.shape
    breadth = output_weight.shape[0]
    width = breadth // heads
    rows = updated.shape[1]
    place = lax.axis_index("noise")
    for k in range(noise_size):
        down = pl.ds(pl.multiple_of((place ^ k) * part_rows, math.gcd(part_rows, 32)), part_rows)
        output_weight[down, :] = weight_parts[k].astype(output_weight.dtype)
    pairs = keep[0].shape[0]
    for pair in range(chunks * pairs):
        own, other = keep[pair // pairs].at[pair % pairs], got[pair // pairs].at[pair % pairs]
        parts = []
        for h in range(heads):
            at_high = slice(breadth + h, breadth + h + 1)
            at_total = slice(breadth + heads + h, breadth + heads + h + 1)
            across = slice(h * width, (h + 1) * width)
            high = jnp.maximum(own[at_high], other[at_high])
            mine, theirs = jnp.exp2(own[at_high] - high), jnp.exp2(other[at_high] - high)
            total = own[at_total] * mine + other[at_total] * theirs
            parts.append((own[across] * mine + other[across] * theirs) / total)
        attended = jnp.concatenate(parts, axis=0).T.astype(jnp.bfloat16)
        projected = jnp.dot(
            attended, output_weight[...].astype(jnp.bfloat16), preferred_element_type=jnp.float32
        )
        for side in range(2):
            s = 2 * pair + side
            gate = jax.nn.sigmoid(output_gate[s].astype(jnp.float32))
            updated[s] = (
                activations[s].astype(jnp.float32) + gate * projected[side * rows : (side + 1) * rows]
            ).astype(jnp.bfloat16)


def swap_cores(array):
    return lax.ppermute(array, "row", [(i, i ^ 1) for i in range(lax.axis_size("row"))])


def next_chip(array):
    size = lax.axis_size("row")
    return lax.ppermute(array, "row", [(i, (i + 2) % size) for i in range(size)])


def from_noise(array, k):
    if k == 0:
        return array
    return lax.ppermute(array, "noise", [(i, i ^ k) for i in range(lax.axis_size("noise"))])


def body(
    activations,
    cond_scale,
    cond_shift,
    output_gate,
    pair_repr,
    bias_weight,
    query_weight,
    query_bias,
    key_weight,
    value_weight,
    output_weight,
    token_mask,
):
    samples, rows, features = activations.shape
    heads = bias_weight.shape[1]
    head_features = query_weight.shape[1]
    noise_size = lax.axis_size("noise")
    steps = lax.axis_size("row") // 2
    assert noise_size == steps and pair_repr.shape[1] == 2 * rows
    bf16, f32 = jnp.bfloat16, jnp.float32
    params = pltpu.CompilerParams(vmem_limit_bytes=vmem_bytes)
    struct = jax.ShapeDtypeStruct
    after = lax.optimization_barrier
    half = query_weight.shape[0] // 2

    in_hbm = pl.BlockSpec(memory_space=pltpu.HBM)
    shifted, sent, packed = pl.pallas_call(
        shift_kernel,
        in_specs=[in_hbm] * 6,
        out_shape=[struct(activations.shape, bf16)] * 2 + [struct((half, 2 * head_features), bf16)],
        scratch_shapes=[pltpu.VMEM(activations.shape, bf16)] * 3
        + [pltpu.VMEM(token_mask.shape, jnp.int32)]
        + [pltpu.VMEM(query_weight.shape, bf16)] * 2
        + [pltpu.SemaphoreType.DMA((3 * samples + 3,))],
        compiler_params=pltpu.CompilerParams(vmem_limit_bytes=wide_bytes),
        name="shift",
    )(activations, cond_scale, cond_shift, token_mask, query_weight, key_weight)

    ring = [sent, next_chip(sent)]
    weights = [from_noise(packed, k) for k in range(noise_size)]
    shifted_other = swap_cores(shifted)
    pair_repr, _ = after((pair_repr, packed))
    pieces = 8
    columns, channels = pair_repr.shape[1:]
    parcel = pl.pallas_call(
        bias_kernel,
        in_specs=[in_hbm, in_hbm, pl.BlockSpec(memory_space=pltpu.VMEM)],
        out_shape=struct((heads * rows + 3 * half, columns), bf16),
        scratch_shapes=[
            pltpu.VMEM((pieces, rows // pieces, columns, channels), bf16),
            pltpu.VMEM(value_weight.shape, bf16),
            pltpu.VMEM((rows * heads, columns), f32),
            pltpu.SemaphoreType.DMA((pieces + 1,)),
        ],
        compiler_params=pltpu.CompilerParams(vmem_limit_bytes=wide_bytes),
        name="bias",
    )(pair_repr, value_weight, bias_weight.T)

    ring[1], weights, shifted_other, parcel = after((ring[1], weights, shifted_other, parcel))
    ring.append(next_chip(ring[1]))
    weights_mine = jnp.stack(weights)
    weights_other = swap_cores(weights_mine)
    parcels = [from_noise(parcel, k) for k in range(noise_size)]

    ring[2], parcels, weights_other, output_weight = after((ring[2], parcels, weights_other, output_weight))
    for _ in range(steps - 3):
        ring.append(next_chip(ring[-1]))
    last = ring.pop()
    parcel_mine = jnp.stack(parcels)
    parcel_other = swap_cores(parcel_mine)
    output_parts = jnp.stack([from_noise(output_weight, k) for k in range(noise_size)])

    bias_row = query_bias.reshape(1, head_features)
    record = head_features + 2 * heads
    full_type = f32 if half % 16 else bf16
    output_type = f32 if output_weight.shape[0] % 16 else bf16
    partial, queries, key_full, value_full = pl.pallas_call(
        functools.partial(early_kernel, steps, heads),
        out_shape=[
            struct((samples, record, 2 * rows), f32),
            struct((samples, head_features, 2 * rows), bf16),
            struct((features, head_features), bf16),
            struct((head_features, features), bf16),
        ],
        scratch_shapes=[
            pltpu.VMEM((features, 2 * head_features), full_type),
            pltpu.VMEM((features, head_features), full_type),
        ],
        compiler_params=params,
        name="early",
    )(weights_mine, weights_other, bias_row, shifted, shifted_other, parcel_mine, parcel_other, *ring)
    keep, got = [], []
    chunks = 2
    each = samples // chunks
    for c in range(chunks):
        kept, give = pl.pallas_call(
            functools.partial(late_kernel, steps, heads, c * each),
            out_shape=[struct((each // 2, record, 2 * rows), f32)] * 2,
            scratch_shapes=[pltpu.VMEM((each, record, 2 * rows), f32)],
            compiler_params=params,
            name="late",
        )(partial, queries, key_full, value_full, parcel_mine, parcel_other, last)
        keep.append(kept)
        got.append(swap_cores(give))
    return pl.pallas_call(
        functools.partial(finish_kernel, heads, chunks),
        out_shape=struct(activations.shape, bf16),
        scratch_shapes=[pltpu.VMEM((head_features, features), output_type)],
        compiler_params=params,
        name="finish",
    )(output_parts, activations, output_gate, *keep, *got)


def solution(mesh):
    return jax.shard_map(
        body,
        mesh=mesh,
        in_specs=(
            P("noise", "row", None),
            P("noise", "row", None),
            P("noise", "row", None),
            P("noise", "row", None),
            P("row", "noise", None),
            P(),
            P("noise", None),
            P(),
            P("noise", None),
            P("noise", None),
            P("noise", None),
            P("noise", "row"),
        ),
        out_specs=P("noise", "row", None),
        check_vma=False,
    )
```

```python
import functools
import math

import jax
import jax.numpy as jnp
from jax import lax
from jax.experimental import pallas as pl
from jax.experimental.pallas import tpu as pltpu
from jax.sharding import PartitionSpec as P

epsilon = 1e-05
masked_score = -1e30
absent = 32768.0
log2_e = math.log2(math.e)
vmem_bytes = 40 * 2**20
wide_bytes = 60 * 2**20


def layer_norm(tensor):
    average = jnp.mean(tensor, axis=-1, keepdims=True)
    centred = tensor - average
    variance = jnp.mean(centred * centred, axis=-1, keepdims=True)
    return centred * lax.rsqrt(variance + epsilon)


def shift_kernel(
    activations_hbm,
    scale_hbm,
    shift_hbm,
    mask_hbm,
    query_hbm,
    key_hbm,
    shifted,
    sent,
    packed,
    activations,
    cond_scale,
    cond_shift,
    token_mask,
    query_weight,
    key_weight,
    sems,
):
    samples, rows, features = activations.shape
    copies = [pltpu.make_async_copy(mask_hbm, token_mask, sems.at[0])]
    for s in range(samples):
        for t, (source, target) in enumerate(
            ((activations_hbm, activations), (scale_hbm, cond_scale), (shift_hbm, cond_shift))
        ):
            copies.append(pltpu.make_async_copy(source.at[s], target.at[s], sems.at[1 + 3 * s + t]))
    copies.append(pltpu.make_async_copy(query_hbm, query_weight, sems.at[1 + 3 * samples]))
    copies.append(pltpu.make_async_copy(key_hbm, key_weight, sems.at[2 + 3 * samples]))
    for copy in copies:
        copy.start()
    diagonal = lax.broadcasted_iota(jnp.int32, (rows, rows), 0) == lax.broadcasted_iota(
        jnp.int32, (rows, rows), 1
    )
    copies[0].wait()
    for s in range(samples):
        for copy in copies[1 + 3 * s : 4 + 3 * s]:
            copy.wait()
        normed = layer_norm(activations[s].astype(jnp.float32))
        result = cond_scale[s].astype(jnp.float32) * normed + cond_shift[s].astype(jnp.float32)
        flags = jnp.where(diagonal, token_mask[s : s + 1, :].astype(jnp.float32), 0.0)
        valid = jnp.sum(flags, axis=1, keepdims=True) > 0.0
        shifted[s] = result.astype(jnp.bfloat16)
        sent[s] = jnp.where(valid, result, absent).astype(jnp.bfloat16)
    core = lax.rem(lax.axis_index("row"), 2)
    half, breadth = packed.shape[0], query_weight.shape[1]
    for w, weight in enumerate((query_weight, key_weight)):
        copies[1 + 3 * samples + w].wait()
        whole = weight[...].astype(jnp.float32)
        packed[:, w * breadth : (w + 1) * breadth] = jnp.where(
            core == 0, whole[:half], whole[half:]
        ).astype(jnp.bfloat16)


def bias_kernel(pair_hbm, value_hbm, weights, parcel, pair, value_weight, collected, sems):
    pieces, per, columns, channels = pair.shape
    heads = weights.shape[0]
    rows = pieces * per
    copies = [
        pltpu.make_async_copy(pair_hbm.at[pl.ds(i * per, per)], pair.at[i], sems.at[i]) for i in range(pieces)
    ]
    copies.append(pltpu.make_async_copy(value_hbm, value_weight, sems.at[pieces]))
    for copy in copies:
        copy.start()
    record = 2 * heads
    extended = jnp.concatenate(
        [weights[...], jnp.full((heads, channels), 1.0 / channels, jnp.bfloat16)], axis=0
    )
    square = (channels, channels)
    diagonal = lax.broadcasted_iota(jnp.int32, square, 0) == lax.broadcasted_iota(jnp.int32, square, 1)
    centring = (jnp.where(diagonal, 1.0, 0.0) - 1.0 / channels).astype(jnp.bfloat16)
    lane = lax.broadcasted_iota(jnp.int32, (1, rows), 1)
    squares = jnp.zeros((columns, rows), jnp.float32)
    for i in range(pieces):
        copies[i].wait()
        block = pair[i].reshape(per * columns, channels)
        centred = jnp.dot(block, centring, preferred_element_type=jnp.float32)
        summed = jnp.sum(centred * centred, axis=1, keepdims=True)
        result = lax.dot_general(
            extended, block, (((1,), (1,)), ((), ())), preferred_element_type=jnp.float32
        )
        for r in range(per):
            row = i * per + r
            collected[row * record : (row + 1) * record, :] = result[:, r * columns : (r + 1) * columns]
            squares = jnp.where(lane == row, summed[r * columns : (r + 1) * columns], squares)
    core = lax.rem(lax.axis_index("row"), 2)
    half = columns // 2
    average = collected[pl.ds(heads, rows, stride=record), :].T
    inverse = lax.rsqrt(squares / channels + epsilon)
    for p in range(heads // 2):
        own, other = [], []
        for h in (2 * p, 2 * p + 1):
            summed = jnp.sum(weights[h : h + 1, :].astype(jnp.float32), axis=1, keepdims=True)
            turned = (collected[pl.ds(h, rows, stride=record), :].T - average * summed) * inverse
            low, up = turned[:half], turned[half:]
            own.append(jnp.where(core == 0, low, up))
            other.append(jnp.where(core == 0, up, low))
        at = p * half
        parcel[at : at + half, :] = jnp.concatenate(own, axis=1).astype(jnp.bfloat16)
        at += heads // 2 * half
        parcel[at : at + half, :] = jnp.concatenate(other[::-1], axis=1).astype(jnp.bfloat16)
    copies[pieces].wait()
    depth, breadth = value_weight.shape
    whole = value_weight[...].astype(jnp.float32)
    kept = jnp.where(core == 0, whole[: depth // 2], whole[depth // 2 :]).astype(jnp.bfloat16)
    for t in range(breadth // columns):
        at = heads * half + t * (depth // 2)
        parcel[at : at + depth // 2, :] = kept[:, t * columns : (t + 1) * columns]


def spread_queries(heads, queries, spread):
    count, head_features = queries.shape
    width = head_features // heads
    lane = lax.broadcasted_iota(jnp.int32, (1, head_features), 1)
    one = (lax.broadcasted_iota(jnp.int32, (count, 128), 1) == 0).astype(jnp.bfloat16)
    turned = jnp.concatenate([queries[count // 2 :], queries[: count // 2]], axis=0)
    for h in range(heads):
        inside = ((lane >= h * width) & (lane < (h + 1) * width)).astype(jnp.bfloat16)
        spread[h * count : (h + 1) * count, 0:head_features] = (turned if h % 2 else queries) * inside
        spread[h * count : (h + 1) * count, head_features:] = one


def attend_keys(heads, tokens, keys, values, bias_of, spread):
    width = values.shape[0] // heads
    count = spread.shape[0] // heads
    penalty = jnp.where(tokens[:, 0:1].astype(jnp.float32) > absent / 2, masked_score, 0.0)
    penalty = jnp.broadcast_to(penalty, (tokens.shape[0], 128)).astype(jnp.bfloat16)
    scores = lax.dot_general(
        jnp.concatenate([keys, penalty], axis=1),
        spread[...],
        (((1,), (1,)), ((), ())),
        preferred_element_type=jnp.float32,
    ) * (log2_e / math.sqrt(width))
    sums, highs, totals = [], [], []
    for h in range(heads):
        score = scores[:, h * count : (h + 1) * count] + bias_of(h) * log2_e
        high = jnp.max(score, axis=0, keepdims=True)
        probs = jnp.exp2(score - high)
        totals.append(jnp.sum(probs, axis=0, keepdims=True))
        highs.append(high)
        sums.append(
            jnp.dot(
                values[h * width : (h + 1) * width],
                probs.astype(jnp.bfloat16),
                preferred_element_type=jnp.float32,
            )
        )
    return sums, highs, totals


def bias_picker(parcel, swapped, steps, first, rows):
    chip = lax.axis_index("row") // 2
    place = lax.axis_index("noise")
    left = lax.broadcasted_iota(jnp.int32, (1, 2 * rows), 1) < rows

    def pick(b, h):
        part = lax.rem(chip - (first + b) + steps, steps) ^ place
        at = slice(h // 2 * rows, (h // 2 + 1) * rows)
        pairs = parcel[part, at].astype(jnp.float32), swapped[part, at].astype(jnp.float32)
        return jnp.where(left, pairs[h % 2], pairs[1 - h % 2])

    return pick


def early_kernel(steps, heads, weights_mine, weights_other, query_bias, shifted, parcel, swapped, swapped_value, *refs):
    blocks = refs[: steps - 1]
    partial, queries, key_weight, value_weight, full, full_value, spread = refs[steps - 1 :]
    samples, rows, features = shifted.shape
    noise_size, half = swapped_value.shape[0], weights_mine.shape[1] - rows * samples // swapped_value.shape[0]
    breadth = key_weight.shape[1]
    width = breadth // heads
    core = lax.rem(lax.axis_index("row"), 2)
    place = lax.axis_index("noise")
    below = parcel.shape[1] - breadth // 128 * half
    for part, value, skipped, of_core in (
        (weights_mine, parcel, below, core),
        (weights_other, swapped_value, 0, 1 - core),
    ):
        for k in range(noise_size):
            start = ((place ^ k) * 2 + of_core) * half
            down = pl.ds(pl.multiple_of(start, math.gcd(half, 32)), half)
            full[down, :] = part[k, 0:half].astype(full.dtype)
            for t in range(breadth // 128):
                at = skipped + t * half
                full_value[down, t * 128 : (t + 1) * 128] = value[k, at : at + half].astype(full.dtype)
    key_weight[...] = full[:, breadth : 2 * breadth].astype(jnp.bfloat16)
    value_weight[...] = full_value[...].astype(jnp.float32).T.astype(jnp.bfloat16)
    for side, tokens in enumerate((shifted[...], weights_other[:, half:])):
        result = jnp.dot(
            tokens.reshape(samples * rows, features),
            full[:, 0:breadth].astype(jnp.bfloat16),
            preferred_element_type=jnp.float32,
        ) + query_bias[...].astype(jnp.float32)
        queries[:, side * rows : (side + 1) * rows] = result.astype(jnp.bfloat16).reshape(
            samples, rows, breadth
        )
    pick = bias_picker(parcel, swapped, steps, 0, rows)
    for s in range(samples):
        tokens = jnp.concatenate([block[s] for block in blocks], axis=0)
        keys = jnp.dot(tokens, key_weight[...], preferred_element_type=jnp.float32).astype(jnp.bfloat16)
        values = lax.dot_general(
            value_weight[...], tokens, (((1,), (1,)), ((), ())), preferred_element_type=jnp.float32
        ).astype(jnp.bfloat16)
        spread_queries(heads, queries[s], spread)
        sums, highs, totals = attend_keys(
            heads,
            tokens,
            keys,
            values,
            lambda h: jnp.concatenate([pick(b, h) for b in range(steps - 1)], axis=0),
            spread,
        )
        for h in range(heads):
            partial[s, h * width : (h + 1) * width] = sums[h]
            partial[s, breadth + h : breadth + h + 1] = highs[h]
            partial[s, breadth + heads + h : breadth + heads + h + 1] = totals[h]


def late_kernel(steps, heads, first, partial, queries, key_weight, value_weight, parcel, swapped, block, keep, give, merged, spread):
    samples = merged.shape[0]
    rows = block.shape[1]
    breadth = key_weight.shape[1]
    width = breadth // heads
    pick = bias_picker(parcel, swapped, steps, steps - 1, rows)
    for s in range(samples):
        tokens = block[first + s]
        keys = jnp.dot(tokens, key_weight[...], preferred_element_type=jnp.float32).astype(jnp.bfloat16)
        values = lax.dot_general(
            value_weight[...], tokens, (((1,), (1,)), ((), ())), preferred_element_type=jnp.float32
        ).astype(jnp.bfloat16)
        spread_queries(heads, queries[first + s], spread)
        sums, highs, totals = attend_keys(heads, tokens, keys, values, lambda h: pick(0, h), spread)
        before = partial.at[first + s]
        for h in range(heads):
            at_high = slice(breadth + h, breadth + h + 1)
            at_total = slice(breadth + heads + h, breadth + heads + h + 1)
            high = jnp.maximum(before[at_high], highs[h])
            old, new = jnp.exp2(before[at_high] - high), jnp.exp2(highs[h] - high)
            across = slice(h * width, (h + 1) * width)
            merged[s, across] = before[across] * old + sums[h] * new
            merged[s, at_high] = high
            merged[s, at_total] = before[at_total] * old + totals[h] * new
    half = merged.shape[2] // 2
    left = lax.broadcasted_iota(jnp.int32, (1, 2 * half), 1) < half
    row = lax.broadcasted_iota(jnp.int32, (merged.shape[1], 1), 0)
    head = jnp.where(row < breadth, row // width, (row - breadth) % heads)
    even = head % 2 == 0
    for pair in range(samples // 2):
        a, b = merged[2 * pair], merged[2 * pair + 1]
        lefts = jnp.where(left, a, pltpu.roll(b, half, 1))
        rights = jnp.where(left, pltpu.roll(a, half, 1), b)
        keep[pair] = jnp.where(even, lefts, rights)
        give[pair] = jnp.where(even, rights, lefts)


def finish_kernel(heads, chunks, weight_parts, activations, output_gate, *refs):
    keep, got = refs[:chunks], refs[chunks : 2 * chunks]
    updated, output_weight = refs[2 * chunks :]
    noise_size, part_rows, _ = weight_parts.shape
    breadth = output_weight.shape[0]
    width = breadth // heads
    rows = updated.shape[1]
    place = lax.axis_index("noise")
    for k in range(noise_size):
        down = pl.ds(pl.multiple_of((place ^ k) * part_rows, math.gcd(part_rows, 32)), part_rows)
        output_weight[down, :] = weight_parts[k].astype(output_weight.dtype)
    pairs = keep[0].shape[0]
    for pair in range(chunks * pairs):
        own, other = keep[pair // pairs].at[pair % pairs], got[pair // pairs].at[pair % pairs]
        parts = []
        for h in range(heads):
            at_high = slice(breadth + h, breadth + h + 1)
            at_total = slice(breadth + heads + h, breadth + heads + h + 1)
            across = slice(h * width, (h + 1) * width)
            high = jnp.maximum(own[at_high], other[at_high])
            mine, theirs = jnp.exp2(own[at_high] - high), jnp.exp2(other[at_high] - high)
            total = own[at_total] * mine + other[at_total] * theirs
            parts.append((own[across] * mine + other[across] * theirs) / total)
        attended = jnp.concatenate(parts, axis=0).T.astype(jnp.bfloat16)
        projected = jnp.dot(
            attended, output_weight[...].astype(jnp.bfloat16), preferred_element_type=jnp.float32
        )
        for side in range(2):
            s = 2 * pair + side
            gate = jax.nn.sigmoid(output_gate[s].astype(jnp.float32))
            updated[s] = (
                activations[s].astype(jnp.float32) + gate * projected[side * rows : (side + 1) * rows]
            ).astype(jnp.bfloat16)


def swap_cores(array):
    return lax.ppermute(array, "row", [(i, i ^ 1) for i in range(lax.axis_size("row"))])


def next_chip(array):
    size = lax.axis_size("row")
    return lax.ppermute(array, "row", [(i, (i + 2) % size) for i in range(size)])


def from_noise(array, k):
    if k == 0:
        return array
    return lax.ppermute(array, "noise", [(i, i ^ k) for i in range(lax.axis_size("noise"))])


def body(
    activations,
    cond_scale,
    cond_shift,
    output_gate,
    pair_repr,
    bias_weight,
    query_weight,
    query_bias,
    key_weight,
    value_weight,
    output_weight,
    token_mask,
):
    samples, rows, features = activations.shape
    heads = bias_weight.shape[1]
    head_features = query_weight.shape[1]
    noise_size = lax.axis_size("noise")
    steps = lax.axis_size("row") // 2
    assert noise_size == steps and pair_repr.shape[1] == 2 * rows
    bf16, f32 = jnp.bfloat16, jnp.float32
    params = pltpu.CompilerParams(vmem_limit_bytes=vmem_bytes)
    struct = jax.ShapeDtypeStruct
    after = lax.optimization_barrier
    half = query_weight.shape[0] // 2

    in_hbm = pl.BlockSpec(memory_space=pltpu.HBM)
    shifted, sent, packed = pl.pallas_call(
        shift_kernel,
        in_specs=[in_hbm] * 6,
        out_shape=[struct(activations.shape, bf16)] * 2 + [struct((half, 2 * head_features), bf16)],
        scratch_shapes=[pltpu.VMEM(activations.shape, bf16)] * 3
        + [pltpu.VMEM(token_mask.shape, jnp.int32)]
        + [pltpu.VMEM(query_weight.shape, bf16)] * 2
        + [pltpu.SemaphoreType.DMA((3 * samples + 3,))],
        compiler_params=pltpu.CompilerParams(vmem_limit_bytes=wide_bytes),
        name="shift",
    )(activations, cond_scale, cond_shift, token_mask, query_weight, key_weight)

    ring = [sent, next_chip(sent)]
    weights = [from_noise(packed, k) for k in range(noise_size)]
    pair_repr, _ = after((pair_repr, packed))
    pieces = 8
    columns, channels = pair_repr.shape[1:]
    tile_rows = heads * rows
    parcel = pl.pallas_call(
        bias_kernel,
        in_specs=[in_hbm, in_hbm, pl.BlockSpec(memory_space=pltpu.VMEM)],
        out_shape=struct((tile_rows + 3 * half, columns), bf16),
        scratch_shapes=[
            pltpu.VMEM((pieces, rows // pieces, columns, channels), bf16),
            pltpu.VMEM(value_weight.shape, bf16),
            pltpu.VMEM((rows * 2 * heads, columns), f32),
            pltpu.SemaphoreType.DMA((pieces + 1,)),
        ],
        compiler_params=pltpu.CompilerParams(vmem_limit_bytes=wide_bytes),
        name="bias",
    )(pair_repr, value_weight, bias_weight.T)

    ring[1], weights, parcel = after((ring[1], weights, parcel))
    ring.append(next_chip(ring[1]))
    tokens = shifted.reshape(noise_size, samples * rows // noise_size, features)
    weights_mine = jnp.concatenate([jnp.stack(weights), tokens], axis=1)
    weights_other = swap_cores(weights_mine)
    parcels = [from_noise(parcel, k) for k in range(noise_size)]

    for _ in range(steps - 3):
        ring.append(next_chip(ring[-1]))
    last = ring.pop()
    parcels, _ = after((parcels, ring[2]))
    parcel_mine = jnp.stack(parcels)
    swapped = swap_cores(parcel_mine[:, tile_rows // 2 : tile_rows])
    swapped_value = swap_cores(parcel_mine[:, tile_rows:])
    output_weight, _ = after((output_weight, ring[2]))
    output_parts = [output_weight]
    for k in range(noise_size.bit_length() - 1):
        mine = jnp.stack(output_parts)
        theirs = from_noise(mine, 2**k)
        output_parts += [theirs[i] for i in range(2**k)]
    output_parts = jnp.stack(output_parts)

    bias_row = query_bias.reshape(1, head_features)
    record = head_features + 2 * heads
    full_type = f32 if half % 16 else bf16
    output_type = f32 if output_weight.shape[0] % 16 else bf16
    spread = pltpu.VMEM((heads * 2 * rows, head_features + 128), bf16)
    partial, queries, key_full, value_full = pl.pallas_call(
        functools.partial(early_kernel, steps, heads),
        out_shape=[
            struct((samples, record, 2 * rows), f32),
            struct((samples, 2 * rows, head_features), bf16),
            struct((features, head_features), bf16),
            struct((head_features, features), bf16),
        ],
        scratch_shapes=[
            pltpu.VMEM((features, 2 * head_features), full_type),
            pltpu.VMEM((features, head_features), full_type),
            spread,
        ],
        compiler_params=params,
        name="early",
    )(weights_mine, weights_other, bias_row, shifted, parcel_mine, swapped, swapped_value, *ring)
    keep, got = [], []
    chunks = 2
    each = samples // chunks
    for c in range(chunks):
        kept, give = pl.pallas_call(
            functools.partial(late_kernel, steps, heads, c * each),
            out_shape=[struct((each // 2, record, 2 * rows), f32)] * 2,
            scratch_shapes=[pltpu.VMEM((each, record, 2 * rows), f32), spread],
            compiler_params=params,
            name="late",
        )(partial, queries, key_full, value_full, parcel_mine, swapped, last)
        keep.append(kept)
        got.append(swap_cores(give))
    return pl.pallas_call(
        functools.partial(finish_kernel, heads, chunks),
        out_shape=struct(activations.shape, bf16),
        scratch_shapes=[pltpu.VMEM((head_features, features), output_type)],
        compiler_params=params,
        name="finish",
    )(output_parts, activations, output_gate, *keep, *got)


def solution(mesh):
    return jax.shard_map(
        body,
        mesh=mesh,
        in_specs=(
            P("noise", "row", None),
            P("noise", "row", None),
            P("noise", "row", None),
            P("noise", "row", None),
            P("row", "noise", None),
            P(),
            P("noise", None),
            P(),
            P("noise", None),
            P("noise", None),
            P("noise", None),
            P("noise", "row"),
        ),
        out_specs=P("noise", "row", None),
        check_vma=False,
    )
```

```python
import functools
import math

import jax
import jax.numpy as jnp
from jax import lax
from jax.experimental import pallas as pl
from jax.experimental.pallas import tpu as pltpu
from jax.sharding import PartitionSpec as P

epsilon = 1e-05
masked_score = -1e30
absent = 32768.0
log2_e = math.log2(math.e)
vmem_bytes = 40 * 2**20
wide_bytes = 60 * 2**20


def layer_norm(tensor):
    average = jnp.mean(tensor, axis=-1, keepdims=True)
    centred = tensor - average
    variance = jnp.mean(centred * centred, axis=-1, keepdims=True)
    return centred * lax.rsqrt(variance + epsilon)


def shift_kernel(
    activations_hbm,
    scale_hbm,
    shift_hbm,
    mask_hbm,
    query_hbm,
    key_hbm,
    shifted_hbm,
    sent_hbm,
    packed_hbm,
    shifted,
    sent,
    packed,
    activations,
    cond_scale,
    cond_shift,
    token_mask,
    query_weight,
    key_weight,
    sems,
    sems_out,
):
    samples, rows, features = activations.shape
    copies = [pltpu.make_async_copy(mask_hbm, token_mask, sems.at[0])]
    for s in range(samples):
        for t, (source, target) in enumerate(
            ((activations_hbm, activations), (scale_hbm, cond_scale), (shift_hbm, cond_shift))
        ):
            copies.append(pltpu.make_async_copy(source.at[s], target.at[s], sems.at[1 + 3 * s + t]))
    copies.append(pltpu.make_async_copy(query_hbm, query_weight, sems.at[1 + 3 * samples]))
    copies.append(pltpu.make_async_copy(key_hbm, key_weight, sems.at[2 + 3 * samples]))
    for copy in copies:
        copy.start()
    diagonal = lax.broadcasted_iota(jnp.int32, (rows, rows), 0) == lax.broadcasted_iota(
        jnp.int32, (rows, rows), 1
    )
    copies[0].wait()
    written = []
    for s in range(samples):
        for copy in copies[1 + 3 * s : 4 + 3 * s]:
            copy.wait()
        normed = layer_norm(activations[s].astype(jnp.float32))
        result = cond_scale[s].astype(jnp.float32) * normed + cond_shift[s].astype(jnp.float32)
        flags = jnp.where(diagonal, token_mask[s : s + 1, :].astype(jnp.float32), 0.0)
        valid = jnp.sum(flags, axis=1, keepdims=True) > 0.0
        shifted[s] = result.astype(jnp.bfloat16)
        sent[s] = jnp.where(valid, result, absent).astype(jnp.bfloat16)
        for t, (source, target) in enumerate(((sent, sent_hbm), (shifted, shifted_hbm))):
            written.append(pltpu.make_async_copy(source.at[s], target.at[s], sems_out.at[2 * s + t]))
            written[-1].start()
    core = lax.rem(lax.axis_index("row"), 2)
    half, breadth = packed.shape[0], query_weight.shape[1]
    for w, weight in enumerate((query_weight, key_weight)):
        copies[1 + 3 * samples + w].wait()
        whole = weight[...].astype(jnp.float32)
        packed[:, w * breadth : (w + 1) * breadth] = jnp.where(
            core == 0, whole[:half], whole[half:]
        ).astype(jnp.bfloat16)
    written.append(pltpu.make_async_copy(packed, packed_hbm, sems_out.at[2 * samples]))
    written[-1].start()
    for copy in written:
        copy.wait()


def bias_kernel(pair, value_weight, weights, parcel, collected):
    rows, columns, channels = pair.shape
    heads = weights.shape[0]
    per = 8
    record = 2 * heads
    extended = jnp.concatenate(
        [weights[...], jnp.full((heads, channels), 1.0 / channels, jnp.bfloat16)], axis=0
    )
    square = (channels, channels)
    diagonal = lax.broadcasted_iota(jnp.int32, square, 0) == lax.broadcasted_iota(jnp.int32, square, 1)
    centring = (jnp.where(diagonal, 1.0, 0.0) - 1.0 / channels).astype(jnp.bfloat16)
    lane = lax.broadcasted_iota(jnp.int32, (1, rows), 1)
    squares = jnp.zeros((columns, rows), jnp.float32)
    for i in range(rows // per):
        block = pair[i * per : (i + 1) * per].reshape(per * columns, channels)
        centred = jnp.dot(block, centring, preferred_element_type=jnp.float32)
        summed = jnp.sum(centred * centred, axis=1, keepdims=True)
        result = lax.dot_general(
            extended, block, (((1,), (1,)), ((), ())), preferred_element_type=jnp.float32
        )
        for r in range(per):
            row = i * per + r
            collected[row * record : (row + 1) * record, :] = result[:, r * columns : (r + 1) * columns]
            squares = jnp.where(lane == row, summed[r * columns : (r + 1) * columns], squares)
    core = lax.rem(lax.axis_index("row"), 2)
    half = columns // 2
    average = collected[pl.ds(heads, rows, stride=record), :].T
    inverse = lax.rsqrt(squares / channels + epsilon)
    for p in range(heads // 2):
        own, other = [], []
        for h in (2 * p, 2 * p + 1):
            summed = jnp.sum(weights[h : h + 1, :].astype(jnp.float32), axis=1, keepdims=True)
            turned = (collected[pl.ds(h, rows, stride=record), :].T - average * summed) * inverse
            low, up = turned[:half], turned[half:]
            own.append(jnp.where(core == 0, low, up))
            other.append(jnp.where(core == 0, up, low))
        at = p * half
        parcel[at : at + half, :] = jnp.concatenate(own, axis=1).astype(jnp.bfloat16)
        at += heads // 2 * half
        parcel[at : at + half, :] = jnp.concatenate(other[::-1], axis=1).astype(jnp.bfloat16)
    depth, breadth = value_weight.shape
    whole = value_weight[...].astype(jnp.float32)
    kept = jnp.where(core == 0, whole[: depth // 2], whole[depth // 2 :]).astype(jnp.bfloat16)
    for t in range(breadth // columns):
        at = heads * half + t * (depth // 2)
        parcel[at : at + depth // 2, :] = kept[:, t * columns : (t + 1) * columns]


def spread_queries(heads, queries, spread):
    count, head_features = queries.shape
    width = head_features // heads
    reach = spread.shape[1]
    lane = lax.broadcasted_iota(jnp.int32, (1, reach), 1)
    turned = jnp.concatenate([queries[count // 2 :], queries[: count // 2]], axis=0)
    for h in range(heads):
        start, free = (0, reach - 1) if h < heads // 2 else (head_features - reach, 0)
        inside = ((lane >= h * width - start) & (lane < (h + 1) * width - start)).astype(jnp.bfloat16)
        extra = (lane == free).astype(jnp.bfloat16)
        own = (turned if h % 2 else queries)[:, start : start + reach]
        spread[h * count : (h + 1) * count, :] = own * inside + extra


def attend_keys(heads, tokens, keys, values, bias_of, spread):
    head_features = values.shape[0]
    width = head_features // heads
    count, reach = spread.shape[0] // heads, spread.shape[1]
    used = heads // 2 * width
    penalty = jnp.where(tokens[:, 0:1].astype(jnp.float32) > absent / 2, masked_score, 0.0)
    lane = lax.broadcasted_iota(jnp.int32, (1, reach), 1)
    scores = []
    for part in range(2):
        start = part * (head_features - reach)
        inside = lane < used if part == 0 else lane >= reach - used
        extended = jnp.where(inside, keys[:, start : start + reach], penalty).astype(jnp.bfloat16)
        scores.append(
            lax.dot_general(
                extended,
                spread[part * heads // 2 * count : (part + 1) * heads // 2 * count, :],
                (((1,), (1,)), ((), ())),
                preferred_element_type=jnp.float32,
            )
        )
    sums, highs, totals = [], [], []
    for h in range(heads):
        at = h % (heads // 2) * count
        score = scores[h // (heads // 2)][:, at : at + count] * (log2_e / math.sqrt(width))
        score = score + bias_of(h) * log2_e
        high = jnp.max(score, axis=0, keepdims=True)
        probs = jnp.exp2(score - high)
        totals.append(jnp.sum(probs, axis=0, keepdims=True))
        highs.append(high)
        sums.append(
            jnp.dot(
                values[h * width : (h + 1) * width],
                probs.astype(jnp.bfloat16),
                preferred_element_type=jnp.float32,
            )
        )
    return sums, highs, totals


def bias_picker(parcel, swapped, steps, first, rows):
    chip = lax.axis_index("row") // 2
    place = lax.axis_index("noise")
    left = lax.broadcasted_iota(jnp.int32, (1, 2 * rows), 1) < rows

    def pick(b, h):
        part = lax.rem(chip - (first + b) + steps, steps) ^ place
        at = slice(h // 2 * rows, (h // 2 + 1) * rows)
        pairs = parcel[part, at].astype(jnp.float32), swapped[part, at].astype(jnp.float32)
        return jnp.where(left, pairs[h % 2], pairs[1 - h % 2])

    return pick


def early_kernel(steps, heads, weights_mine, weights_other, query_bias, shifted, parcel, swapped, swapped_value, *refs):
    blocks = refs[: steps - 1]
    partial, queries, key_weight, value_weight, full, full_value, spread = refs[steps - 1 :]
    samples, rows, features = shifted.shape
    noise_size, half = swapped_value.shape[0], weights_mine.shape[1] - rows * samples // swapped_value.shape[0]
    breadth = key_weight.shape[1]
    width = breadth // heads
    core = lax.rem(lax.axis_index("row"), 2)
    place = lax.axis_index("noise")
    below = parcel.shape[1] - breadth // 128 * half
    for part, value, skipped, of_core in (
        (weights_mine, parcel, below, core),
        (weights_other, swapped_value, 0, 1 - core),
    ):
        for k in range(noise_size):
            start = ((place ^ k) * 2 + of_core) * half
            down = pl.ds(pl.multiple_of(start, math.gcd(half, 32)), half)
            full[down, :] = part[k, 0:half].astype(full.dtype)
            for t in range(breadth // 128):
                at = skipped + t * half
                full_value[down, t * 128 : (t + 1) * 128] = value[k, at : at + half].astype(full.dtype)
    key_weight[...] = full[:, breadth : 2 * breadth].astype(jnp.bfloat16)
    value_weight[...] = full_value[...].astype(jnp.float32).T.astype(jnp.bfloat16)
    for side, tokens in enumerate((shifted[...], weights_other[:, half:])):
        result = jnp.dot(
            tokens.reshape(samples * rows, features),
            full[:, 0:breadth].astype(jnp.bfloat16),
            preferred_element_type=jnp.float32,
        ) + query_bias[...].astype(jnp.float32)
        queries[:, side * rows : (side + 1) * rows] = result.astype(jnp.bfloat16).reshape(
            samples, rows, breadth
        )
    pick = bias_picker(parcel, swapped, steps, 0, rows)
    for s in range(samples):
        tokens = jnp.concatenate([block[s] for block in blocks], axis=0)
        keys = jnp.dot(tokens, key_weight[...], preferred_element_type=jnp.float32)
        values = lax.dot_general(
            value_weight[...], tokens, (((1,), (1,)), ((), ())), preferred_element_type=jnp.float32
        ).astype(jnp.bfloat16)
        spread_queries(heads, queries[s], spread)
        sums, highs, totals = attend_keys(
            heads,
            tokens,
            keys,
            values,
            lambda h: jnp.concatenate([pick(b, h) for b in range(steps - 1)], axis=0),
            spread,
        )
        for h in range(heads):
            partial[s, h * width : (h + 1) * width] = sums[h]
            partial[s, breadth + h : breadth + h + 1] = highs[h]
            partial[s, breadth + heads + h : breadth + heads + h + 1] = totals[h]


def late_kernel(steps, heads, first, partial, queries, key_weight, value_weight, parcel, swapped, block, keep, give, merged, spread):
    samples = merged.shape[0]
    rows = block.shape[1]
    breadth = key_weight.shape[1]
    width = breadth // heads
    pick = bias_picker(parcel, swapped, steps, steps - 1, rows)
    tokens = block[first : first + samples].reshape(samples * rows, block.shape[2])
    keys = jnp.dot(tokens, key_weight[...], preferred_element_type=jnp.float32)
    values = lax.dot_general(
        value_weight[...], tokens, (((1,), (1,)), ((), ())), preferred_element_type=jnp.float32
    ).astype(jnp.bfloat16)
    for s in range(samples):
        here = slice(s * rows, (s + 1) * rows)
        spread_queries(heads, queries[first + s], spread)
        sums, highs, totals = attend_keys(
            heads, tokens[here], keys[here], values[:, here], lambda h: pick(0, h), spread
        )
        before = partial.at[first + s]
        for h in range(heads):
            at_high = slice(breadth + h, breadth + h + 1)
            at_total = slice(breadth + heads + h, breadth + heads + h + 1)
            high = jnp.maximum(before[at_high], highs[h])
            old, new = jnp.exp2(before[at_high] - high), jnp.exp2(highs[h] - high)
            across = slice(h * width, (h + 1) * width)
            merged[s, across] = before[across] * old + sums[h] * new
            merged[s, at_high] = high
            merged[s, at_total] = before[at_total] * old + totals[h] * new
    half = merged.shape[2] // 2
    left = lax.broadcasted_iota(jnp.int32, (1, 2 * half), 1) < half
    row = lax.broadcasted_iota(jnp.int32, (merged.shape[1], 1), 0)
    head = jnp.where(row < breadth, row // width, (row - breadth) % heads)
    even = head % 2 == 0
    for pair in range(samples // 2):
        a, b = merged[2 * pair], merged[2 * pair + 1]
        lefts = jnp.where(left, a, pltpu.roll(b, half, 1))
        rights = jnp.where(left, pltpu.roll(a, half, 1), b)
        keep[pair] = jnp.where(even, lefts, rights)
        give[pair] = jnp.where(even, rights, lefts)


def finish_kernel(heads, chunks, weight_parts, activations, output_gate, *refs):
    keep, got = refs[:chunks], refs[chunks : 2 * chunks]
    updated, output_weight = refs[2 * chunks :]
    noise_size, part_rows, _ = weight_parts.shape
    breadth = output_weight.shape[0]
    width = breadth // heads
    rows = updated.shape[1]
    place = lax.axis_index("noise")
    for k in range(noise_size):
        down = pl.ds(pl.multiple_of((place ^ k) * part_rows, math.gcd(part_rows, 32)), part_rows)
        output_weight[down, :] = weight_parts[k].astype(output_weight.dtype)
    pairs = keep[0].shape[0]
    for pair in range(chunks * pairs):
        own, other = keep[pair // pairs].at[pair % pairs], got[pair // pairs].at[pair % pairs]
        parts = []
        for h in range(heads):
            at_high = slice(breadth + h, breadth + h + 1)
            at_total = slice(breadth + heads + h, breadth + heads + h + 1)
            across = slice(h * width, (h + 1) * width)
            high = jnp.maximum(own[at_high], other[at_high])
            mine, theirs = jnp.exp2(own[at_high] - high), jnp.exp2(other[at_high] - high)
            total = own[at_total] * mine + other[at_total] * theirs
            parts.append((own[across] * mine + other[across] * theirs) / total)
        attended = jnp.concatenate(parts, axis=0).T.astype(jnp.bfloat16)
        projected = jnp.dot(
            attended, output_weight[...].astype(jnp.bfloat16), preferred_element_type=jnp.float32
        )
        for side in range(2):
            s = 2 * pair + side
            gate = jax.nn.sigmoid(output_gate[s].astype(jnp.float32))
            updated[s] = (
                activations[s].astype(jnp.float32) + gate * projected[side * rows : (side + 1) * rows]
            ).astype(jnp.bfloat16)


def swap_cores(array):
    return lax.ppermute(array, "row", [(i, i ^ 1) for i in range(lax.axis_size("row"))])


def next_chip(array):
    size = lax.axis_size("row")
    return lax.ppermute(array, "row", [(i, (i + 2) % size) for i in range(size)])


def from_noise(array, k):
    if k == 0:
        return array
    return lax.ppermute(array, "noise", [(i, i ^ k) for i in range(lax.axis_size("noise"))])


def body(
    activations,
    cond_scale,
    cond_shift,
    output_gate,
    pair_repr,
    bias_weight,
    query_weight,
    query_bias,
    key_weight,
    value_weight,
    output_weight,
    token_mask,
):
    samples, rows, features = activations.shape
    heads = bias_weight.shape[1]
    head_features = query_weight.shape[1]
    noise_size = lax.axis_size("noise")
    steps = lax.axis_size("row") // 2
    assert noise_size == steps and pair_repr.shape[1] == 2 * rows
    bf16, f32 = jnp.bfloat16, jnp.float32
    params = pltpu.CompilerParams(vmem_limit_bytes=vmem_bytes)
    struct = jax.ShapeDtypeStruct
    after = lax.optimization_barrier
    half = query_weight.shape[0] // 2

    in_hbm = pl.BlockSpec(memory_space=pltpu.HBM)
    packed_shape = (half, 2 * head_features)
    shifted, sent, packed = pl.pallas_call(
        shift_kernel,
        in_specs=[in_hbm] * 6,
        out_specs=[in_hbm] * 3,
        out_shape=[struct(activations.shape, bf16)] * 2 + [struct(packed_shape, bf16)],
        scratch_shapes=[pltpu.VMEM(activations.shape, bf16)] * 2
        + [pltpu.VMEM(packed_shape, bf16)]
        + [pltpu.VMEM(activations.shape, bf16)] * 3
        + [pltpu.VMEM(token_mask.shape, jnp.int32)]
        + [pltpu.VMEM(query_weight.shape, bf16)] * 2
        + [pltpu.SemaphoreType.DMA((3 * samples + 3,)), pltpu.SemaphoreType.DMA((2 * samples + 1,))],
        compiler_params=pltpu.CompilerParams(vmem_limit_bytes=wide_bytes),
        name="shift",
    )(activations, cond_scale, cond_shift, token_mask, query_weight, key_weight)

    ring = [sent, next_chip(sent)]
    weights = [from_noise(packed, k) for k in range(noise_size)]
    head_weights, _ = after((bias_weight.T, packed))
    columns = pair_repr.shape[1]
    tile_rows = heads * rows
    parcel = pl.pallas_call(
        bias_kernel,
        out_shape=struct((tile_rows + 3 * half, columns), bf16),
        scratch_shapes=[pltpu.VMEM((rows * 2 * heads, columns), f32)],
        compiler_params=params,
        name="bias",
    )(pair_repr, value_weight, head_weights)
    output_shard, _ = after((output_weight, packed))
    output_parts = jnp.stack([output_shard, from_noise(output_shard, 1)])

    ring[1], weights, parcel, output_parts = after((ring[1], weights, parcel, output_parts))
    ring.append(next_chip(ring[1]))
    tokens = shifted.reshape(noise_size, samples * rows // noise_size, features)
    weights_mine = jnp.concatenate([jnp.stack(weights), tokens], axis=1)
    weights_other = swap_cores(weights_mine)
    parcels = [from_noise(parcel, k) for k in range(noise_size)]

    for _ in range(steps - 3):
        ring.append(next_chip(ring[-1]))
    last = ring.pop()
    parcels, _ = after((parcels, ring[2]))
    parcel_mine = jnp.stack(parcels)
    swapped = swap_cores(parcel_mine[:, tile_rows // 2 : tile_rows])
    swapped_value = swap_cores(parcel_mine[:, tile_rows:])
    for k in range(1, noise_size.bit_length() - 1):
        output_parts = jnp.concatenate([output_parts, from_noise(output_parts, 2**k)], axis=0)

    bias_row = query_bias.reshape(1, head_features)
    record = head_features + 2 * heads
    full_type = f32 if half % 16 else bf16
    output_type = f32 if output_weight.shape[0] % 16 else bf16
    spread = pltpu.VMEM((heads * 2 * rows, 256), bf16)
    partial, queries, key_full, value_full = pl.pallas_call(
        functools.partial(early_kernel, steps, heads),
        out_shape=[
            struct((samples, record, 2 * rows), f32),
            struct((samples, 2 * rows, head_features), bf16),
            struct((features, head_features), bf16),
            struct((head_features, features), bf16),
        ],
        scratch_shapes=[
            pltpu.VMEM((features, 2 * head_features), full_type),
            pltpu.VMEM((features, head_features), full_type),
            spread,
        ],
        compiler_params=params,
        name="early",
    )(weights_mine, weights_other, bias_row, shifted, parcel_mine, swapped, swapped_value, *ring)
    keep, got = [], []
    chunks = 2
    each = samples // chunks
    for c in range(chunks):
        kept, give = pl.pallas_call(
            functools.partial(late_kernel, steps, heads, c * each),
            out_shape=[struct((each // 2, record, 2 * rows), f32)] * 2,
            scratch_shapes=[pltpu.VMEM((each, record, 2 * rows), f32), spread],
            compiler_params=params,
            name="late",
        )(partial, queries, key_full, value_full, parcel_mine, swapped, last)
        keep.append(kept)
        got.append(swap_cores(give))
    return pl.pallas_call(
        functools.partial(finish_kernel, heads, chunks),
        out_shape=struct(activations.shape, bf16),
        scratch_shapes=[pltpu.VMEM((head_features, features), output_type)],
        compiler_params=params,
        name="finish",
    )(output_parts, activations, output_gate, *keep, *got)


def solution(mesh):
    return jax.shard_map(
        body,
        mesh=mesh,
        in_specs=(
            P("noise", "row", None),
            P("noise", "row", None),
            P("noise", "row", None),
            P("noise", "row", None),
            P("row", "noise", None),
            P(),
            P("noise", None),
            P(),
            P("noise", None),
            P("noise", None),
            P("noise", None),
            P("noise", "row"),
        ),
        out_specs=P("noise", "row", None),
        check_vma=False,
    )
```

```python
import functools
import math

import jax
import jax.numpy as jnp
from jax import lax
from jax.experimental import pallas as pl
from jax.experimental.pallas import tpu as pltpu
from jax.sharding import PartitionSpec as P

epsilon = 1e-05
masked_score = -1e30
absent = 32768.0
log2_e = math.log2(math.e)
vmem_bytes = 40 * 2**20
wide_bytes = 60 * 2**20


def layer_norm(tensor):
    average = jnp.mean(tensor, axis=-1, keepdims=True)
    centred = tensor - average
    variance = jnp.mean(centred * centred, axis=-1, keepdims=True)
    return centred * lax.rsqrt(variance + epsilon)


def shift_kernel(
    activations_hbm,
    scale_hbm,
    shift_hbm,
    mask_hbm,
    query_hbm,
    key_hbm,
    output_hbm,
    shifted_hbm,
    sent_hbm,
    packed_hbm,
    columns_hbm,
    shifted,
    sent,
    packed,
    columns,
    activations,
    cond_scale,
    cond_shift,
    token_mask,
    query_weight,
    key_weight,
    output_weight,
    sems,
    sems_out,
):
    samples, rows, features = activations.shape
    copies = [pltpu.make_async_copy(mask_hbm, token_mask, sems.at[0])]
    for s in range(samples):
        for t, (source, target) in enumerate(
            ((activations_hbm, activations), (scale_hbm, cond_scale), (shift_hbm, cond_shift))
        ):
            copies.append(pltpu.make_async_copy(source.at[s], target.at[s], sems.at[1 + 3 * s + t]))
    copies.append(pltpu.make_async_copy(query_hbm, query_weight, sems.at[1 + 3 * samples]))
    copies.append(pltpu.make_async_copy(key_hbm, key_weight, sems.at[2 + 3 * samples]))
    copies.append(pltpu.make_async_copy(output_hbm, output_weight, sems.at[3 + 3 * samples]))
    for copy in copies:
        copy.start()
    diagonal = lax.broadcasted_iota(jnp.int32, (rows, rows), 0) == lax.broadcasted_iota(
        jnp.int32, (rows, rows), 1
    )
    copies[0].wait()
    written = []
    for s in range(samples):
        for copy in copies[1 + 3 * s : 4 + 3 * s]:
            copy.wait()
        normed = layer_norm(activations[s].astype(jnp.float32))
        result = cond_scale[s].astype(jnp.float32) * normed + cond_shift[s].astype(jnp.float32)
        flags = jnp.where(diagonal, token_mask[s : s + 1, :].astype(jnp.float32), 0.0)
        valid = jnp.sum(flags, axis=1, keepdims=True) > 0.0
        shifted[s] = result.astype(jnp.bfloat16)
        sent[s] = jnp.where(valid, result, absent).astype(jnp.bfloat16)
        for t, (source, target) in enumerate(((sent, sent_hbm), (shifted, shifted_hbm))):
            written.append(pltpu.make_async_copy(source.at[s], target.at[s], sems_out.at[2 * s + t]))
            written[-1].start()
    core = lax.rem(lax.axis_index("row"), 2)
    half, breadth = packed.shape[0], query_weight.shape[1]
    for w, weight in enumerate((query_weight, key_weight)):
        copies[1 + 3 * samples + w].wait()
        whole = weight[...].astype(jnp.float32)
        packed[:, w * breadth : (w + 1) * breadth] = jnp.where(
            core == 0, whole[:half], whole[half:]
        ).astype(jnp.bfloat16)
    written.append(pltpu.make_async_copy(packed, packed_hbm, sems_out.at[2 * samples]))
    written[-1].start()
    copies[-1].wait()
    columns[...] = jnp.where(core == 0, output_weight[:, :breadth], output_weight[:, breadth:])
    written.append(pltpu.make_async_copy(columns, columns_hbm, sems_out.at[2 * samples + 1]))
    written[-1].start()
    for copy in written:
        copy.wait()


def bias_kernel(pair, value_weight, weights, parcel, collected):
    rows, columns, channels = pair.shape
    heads = weights.shape[0]
    per = 8
    record = 2 * heads
    extended = jnp.concatenate(
        [weights[...], jnp.full((heads, channels), 1.0 / channels, jnp.bfloat16)], axis=0
    )
    square = (channels, channels)
    diagonal = lax.broadcasted_iota(jnp.int32, square, 0) == lax.broadcasted_iota(jnp.int32, square, 1)
    centring = (jnp.where(diagonal, 1.0, 0.0) - 1.0 / channels).astype(jnp.bfloat16)
    lane = lax.broadcasted_iota(jnp.int32, (1, rows), 1)
    squares = jnp.zeros((columns, rows), jnp.float32)
    for i in range(rows // per):
        block = pair[i * per : (i + 1) * per].reshape(per * columns, channels)
        centred = jnp.dot(block, centring, preferred_element_type=jnp.float32)
        summed = jnp.sum(centred * centred, axis=1, keepdims=True)
        result = lax.dot_general(
            extended, block, (((1,), (1,)), ((), ())), preferred_element_type=jnp.float32
        )
        for r in range(per):
            row = i * per + r
            collected[row * record : (row + 1) * record, :] = result[:, r * columns : (r + 1) * columns]
            squares = jnp.where(lane == row, summed[r * columns : (r + 1) * columns], squares)
    core = lax.rem(lax.axis_index("row"), 2)
    half = columns // 2
    average = collected[pl.ds(heads, rows, stride=record), :].T
    inverse = lax.rsqrt(squares / channels + epsilon)
    for p in range(heads // 2):
        own, other = [], []
        for h in (2 * p, 2 * p + 1):
            summed = jnp.sum(weights[h : h + 1, :].astype(jnp.float32), axis=1, keepdims=True)
            turned = (collected[pl.ds(h, rows, stride=record), :].T - average * summed) * inverse
            low, up = turned[:half], turned[half:]
            own.append(jnp.where(core == 0, low, up))
            other.append(jnp.where(core == 0, up, low))
        at = p * half
        parcel[at : at + half, :] = jnp.concatenate(own, axis=1).astype(jnp.bfloat16)
        at += heads // 2 * half
        parcel[at : at + half, :] = jnp.concatenate(other[::-1], axis=1).astype(jnp.bfloat16)
    depth, breadth = value_weight.shape
    whole = value_weight[...].astype(jnp.float32)
    kept = jnp.where(core == 0, whole[: depth // 2], whole[depth // 2 :]).astype(jnp.bfloat16)
    for t in range(breadth // columns):
        at = heads * half + t * (depth // 2)
        parcel[at : at + depth // 2, :] = kept[:, t * columns : (t + 1) * columns]


def spread_queries(heads, queries, spread):
    count, head_features = queries.shape
    width = head_features // heads
    reach = spread.shape[1]
    lane = lax.broadcasted_iota(jnp.int32, (1, reach), 1)
    turned = jnp.concatenate([queries[count // 2 :], queries[: count // 2]], axis=0)
    for h in range(heads):
        start, free = (0, reach - 1) if h < heads // 2 else (head_features - reach, 0)
        inside = ((lane >= h * width - start) & (lane < (h + 1) * width - start)).astype(jnp.bfloat16)
        extra = (lane == free).astype(jnp.bfloat16)
        own = (turned if h % 2 else queries)[:, start : start + reach]
        spread[h * count : (h + 1) * count, :] = own * inside + extra


def attend_keys(heads, tokens, keys, values, bias_of, spread):
    head_features = values.shape[0]
    width = head_features // heads
    count, reach = spread.shape[0] // heads, spread.shape[1]
    used = heads // 2 * width
    penalty = jnp.where(tokens[:, 0:1].astype(jnp.float32) > absent / 2, masked_score, 0.0)
    lane = lax.broadcasted_iota(jnp.int32, (1, reach), 1)
    scores = []
    for part in range(2):
        start = part * (head_features - reach)
        inside = lane < used if part == 0 else lane >= reach - used
        extended = jnp.where(inside, keys[:, start : start + reach], penalty).astype(jnp.bfloat16)
        scores.append(
            lax.dot_general(
                extended,
                spread[part * heads // 2 * count : (part + 1) * heads // 2 * count, :],
                (((1,), (1,)), ((), ())),
                preferred_element_type=jnp.float32,
            )
        )
    sums, highs, totals = [], [], []
    for h in range(heads):
        at = h % (heads // 2) * count
        score = scores[h // (heads // 2)][:, at : at + count] * (log2_e / math.sqrt(width))
        score = score + bias_of(h) * log2_e
        high = jnp.max(score, axis=0, keepdims=True)
        probs = jnp.exp2(score - high)
        totals.append(jnp.sum(probs, axis=0, keepdims=True))
        highs.append(high)
        sums.append(
            jnp.dot(
                values[h * width : (h + 1) * width],
                probs.astype(jnp.bfloat16),
                preferred_element_type=jnp.float32,
            )
        )
    return sums, highs, totals


def bias_picker(parcel, swapped, steps, first, rows):
    chip = lax.axis_index("row") // 2
    place = lax.axis_index("noise")
    left = lax.broadcasted_iota(jnp.int32, (1, 2 * rows), 1) < rows

    def pick(b, h):
        part = lax.rem(chip - (first + b) + steps, steps) ^ place
        at = slice(h // 2 * rows, (h // 2 + 1) * rows)
        pairs = parcel[part, at].astype(jnp.float32), swapped[part, at].astype(jnp.float32)
        return jnp.where(left, pairs[h % 2], pairs[1 - h % 2])

    return pick


def early_kernel(steps, heads, weights_mine, weights_other, query_bias, shifted, parcel, swapped, swapped_value, *refs):
    blocks = refs[: steps - 1]
    partial, queries, key_weight, value_weight, full, full_value, spread = refs[steps - 1 :]
    samples, rows, features = shifted.shape
    noise_size, half = swapped_value.shape[0], weights_mine.shape[1] - rows * samples // swapped_value.shape[0]
    breadth = key_weight.shape[1]
    width = breadth // heads
    core = lax.rem(lax.axis_index("row"), 2)
    place = lax.axis_index("noise")
    below = parcel.shape[1] - breadth // 128 * half
    for part, value, skipped, of_core in (
        (weights_mine, parcel, below, core),
        (weights_other, swapped_value, 0, 1 - core),
    ):
        for k in range(noise_size):
            start = ((place ^ k) * 2 + of_core) * half
            down = pl.ds(pl.multiple_of(start, math.gcd(half, 32)), half)
            full[down, :] = part[k, 0:half].astype(full.dtype)
            for t in range(breadth // 128):
                at = skipped + t * half
                full_value[down, t * 128 : (t + 1) * 128] = value[k, at : at + half].astype(full.dtype)
    key_weight[...] = full[:, breadth : 2 * breadth].astype(jnp.bfloat16)
    value_weight[...] = full_value[...].astype(jnp.float32).T.astype(jnp.bfloat16)
    for side, tokens in enumerate((shifted[...], weights_other[:, half:])):
        result = jnp.dot(
            tokens.reshape(samples * rows, features),
            full[:, 0:breadth].astype(jnp.bfloat16),
            preferred_element_type=jnp.float32,
        ) + query_bias[...].astype(jnp.float32)
        queries[:, side * rows : (side + 1) * rows] = result.astype(jnp.bfloat16).reshape(
            samples, rows, breadth
        )
    pick = bias_picker(parcel, swapped, steps, 0, rows)
    for s in range(samples):
        tokens = jnp.concatenate([block[s] for block in blocks], axis=0)
        keys = jnp.dot(tokens, key_weight[...], preferred_element_type=jnp.float32)
        values = lax.dot_general(
            value_weight[...], tokens, (((1,), (1,)), ((), ())), preferred_element_type=jnp.float32
        ).astype(jnp.bfloat16)
        spread_queries(heads, queries[s], spread)
        sums, highs, totals = attend_keys(
            heads,
            tokens,
            keys,
            values,
            lambda h: jnp.concatenate([pick(b, h) for b in range(steps - 1)], axis=0),
            spread,
        )
        for h in range(heads):
            partial[s, h * width : (h + 1) * width] = sums[h]
            partial[s, breadth + h : breadth + h + 1] = highs[h]
            partial[s, breadth + heads + h : breadth + heads + h + 1] = totals[h]


def late_kernel(steps, heads, first, partial, queries, key_weight, value_weight, parcel, swapped, block, keep, give, merged, spread):
    samples = merged.shape[0]
    rows = block.shape[1]
    breadth = key_weight.shape[1]
    width = breadth // heads
    pick = bias_picker(parcel, swapped, steps, steps - 1, rows)
    tokens = block[first : first + samples].reshape(samples * rows, block.shape[2])
    keys = jnp.dot(tokens, key_weight[...], preferred_element_type=jnp.float32)
    values = lax.dot_general(
        value_weight[...], tokens, (((1,), (1,)), ((), ())), preferred_element_type=jnp.float32
    ).astype(jnp.bfloat16)
    for s in range(samples):
        here = slice(s * rows, (s + 1) * rows)
        spread_queries(heads, queries[first + s], spread)
        sums, highs, totals = attend_keys(
            heads, tokens[here], keys[here], values[:, here], lambda h: pick(0, h), spread
        )
        before = partial.at[first + s]
        for h in range(heads):
            at_high = slice(breadth + h, breadth + h + 1)
            at_total = slice(breadth + heads + h, breadth + heads + h + 1)
            high = jnp.maximum(before[at_high], highs[h])
            old, new = jnp.exp2(before[at_high] - high), jnp.exp2(highs[h] - high)
            across = slice(h * width, (h + 1) * width)
            merged[s, across] = before[across] * old + sums[h] * new
            merged[s, at_high] = high
            merged[s, at_total] = before[at_total] * old + totals[h] * new
    half = merged.shape[2] // 2
    left = lax.broadcasted_iota(jnp.int32, (1, 2 * half), 1) < half
    row = lax.broadcasted_iota(jnp.int32, (merged.shape[1], 1), 0)
    head = jnp.where(row < breadth, row // width, (row - breadth) % heads)
    even = head % 2 == 0
    for pair in range(samples // 2):
        a, b = merged[2 * pair], merged[2 * pair + 1]
        lefts = jnp.where(left, a, pltpu.roll(b, half, 1))
        rights = jnp.where(left, pltpu.roll(a, half, 1), b)
        keep[pair] = jnp.where(even, lefts, rights)
        give[pair] = jnp.where(even, rights, lefts)


def finish_kernel(heads, chunks, output_mine, output_other, activations, output_gate, *refs):
    keep, got = refs[:chunks], refs[chunks : 2 * chunks]
    updated, output_weight = refs[2 * chunks :]
    noise_size, part_rows, part_columns = output_mine.shape
    core = lax.rem(lax.axis_index("row"), 2)
    breadth = output_weight.shape[0]
    width = breadth // heads
    rows = updated.shape[1]
    place = lax.axis_index("noise")
    for k in range(noise_size):
        down = pl.ds(pl.multiple_of((place ^ k) * part_rows, math.gcd(part_rows, 32)), part_rows)
        for part, of_core in ((output_mine, core), (output_other, 1 - core)):
            along = pl.ds(pl.multiple_of(of_core * part_columns, 128), part_columns)
            output_weight[down, along] = part[k].astype(output_weight.dtype)
    pairs = keep[0].shape[0]
    for pair in range(chunks * pairs):
        own, other = keep[pair // pairs].at[pair % pairs], got[pair // pairs].at[pair % pairs]
        parts = []
        for h in range(heads):
            at_high = slice(breadth + h, breadth + h + 1)
            at_total = slice(breadth + heads + h, breadth + heads + h + 1)
            across = slice(h * width, (h + 1) * width)
            high = jnp.maximum(own[at_high], other[at_high])
            mine, theirs = jnp.exp2(own[at_high] - high), jnp.exp2(other[at_high] - high)
            total = own[at_total] * mine + other[at_total] * theirs
            parts.append((own[across] * mine + other[across] * theirs) / total)
        attended = jnp.concatenate(parts, axis=0).T.astype(jnp.bfloat16)
        projected = jnp.dot(
            attended, output_weight[...].astype(jnp.bfloat16), preferred_element_type=jnp.float32
        )
        for side in range(2):
            s = 2 * pair + side
            gate = jax.nn.sigmoid(output_gate[s].astype(jnp.float32))
            updated[s] = (
                activations[s].astype(jnp.float32) + gate * projected[side * rows : (side + 1) * rows]
            ).astype(jnp.bfloat16)


def swap_cores(array):
    return lax.ppermute(array, "row", [(i, i ^ 1) for i in range(lax.axis_size("row"))])


def next_chip(array):
    size = lax.axis_size("row")
    return lax.ppermute(array, "row", [(i, (i + 2) % size) for i in range(size)])


def from_noise(array, k):
    if k == 0:
        return array
    return lax.ppermute(array, "noise", [(i, i ^ k) for i in range(lax.axis_size("noise"))])


def body(
    activations,
    cond_scale,
    cond_shift,
    output_gate,
    pair_repr,
    bias_weight,
    query_weight,
    query_bias,
    key_weight,
    value_weight,
    output_weight,
    token_mask,
):
    samples, rows, features = activations.shape
    heads = bias_weight.shape[1]
    head_features = query_weight.shape[1]
    noise_size = lax.axis_size("noise")
    steps = lax.axis_size("row") // 2
    assert noise_size == steps and pair_repr.shape[1] == 2 * rows
    bf16, f32 = jnp.bfloat16, jnp.float32
    params = pltpu.CompilerParams(vmem_limit_bytes=vmem_bytes)
    struct = jax.ShapeDtypeStruct
    after = lax.optimization_barrier
    half = query_weight.shape[0] // 2

    in_hbm = pl.BlockSpec(memory_space=pltpu.HBM)
    packed_shape, columns_shape = (half, 2 * head_features), (output_weight.shape[0], features // 2)
    shifted, sent, packed, output_columns = pl.pallas_call(
        shift_kernel,
        in_specs=[in_hbm] * 7,
        out_specs=[in_hbm] * 4,
        out_shape=[struct(activations.shape, bf16)] * 2
        + [struct(packed_shape, bf16), struct(columns_shape, bf16)],
        scratch_shapes=[pltpu.VMEM(activations.shape, bf16)] * 2
        + [pltpu.VMEM(packed_shape, bf16), pltpu.VMEM(columns_shape, bf16)]
        + [pltpu.VMEM(activations.shape, bf16)] * 3
        + [pltpu.VMEM(token_mask.shape, jnp.int32)]
        + [pltpu.VMEM(query_weight.shape, bf16)] * 2
        + [pltpu.VMEM(output_weight.shape, bf16)]
        + [pltpu.SemaphoreType.DMA((3 * samples + 4,)), pltpu.SemaphoreType.DMA((2 * samples + 2,))],
        compiler_params=pltpu.CompilerParams(vmem_limit_bytes=wide_bytes),
        name="shift",
    )(activations, cond_scale, cond_shift, token_mask, query_weight, key_weight, output_weight)

    ring = [sent, next_chip(sent)]
    weights = [from_noise(packed, k) for k in range(noise_size)]
    head_weights, _ = after((bias_weight.T, packed))
    columns = pair_repr.shape[1]
    tile_rows = heads * rows
    parcel = pl.pallas_call(
        bias_kernel,
        out_shape=struct((tile_rows + 3 * half, columns), bf16),
        scratch_shapes=[pltpu.VMEM((rows * 2 * heads, columns), f32)],
        compiler_params=params,
        name="bias",
    )(pair_repr, value_weight, head_weights)
    output_next = from_noise(output_columns, 1)
    ring[1], weights, parcel, output_next = after((ring[1], weights, parcel, output_next))
    output_mine = jnp.stack([output_columns, output_next])
    ring.append(next_chip(ring[1]))
    tokens = shifted.reshape(noise_size, samples * rows // noise_size, features)
    weights_mine = jnp.concatenate([jnp.stack(weights), tokens], axis=1)
    weights_other = swap_cores(weights_mine)
    parcels = [from_noise(parcel, k) for k in range(noise_size)]

    for _ in range(steps - 3):
        ring.append(next_chip(ring[-1]))
    last = ring.pop()
    parcel_mine = jnp.stack(parcels)
    swapped = swap_cores(parcel_mine[:, tile_rows // 2 : tile_rows])
    swapped_value = swap_cores(parcel_mine[:, tile_rows:])
    for k in range(1, noise_size.bit_length() - 1):
        output_mine = jnp.concatenate([output_mine, from_noise(output_mine, 2**k)], axis=0)
    output_other = swap_cores(output_mine)

    bias_row = query_bias.reshape(1, head_features)
    record = head_features + 2 * heads
    full_type = f32 if half % 16 else bf16
    output_type = f32 if output_weight.shape[0] % 16 else bf16
    spread = pltpu.VMEM((heads * 2 * rows, 256), bf16)
    partial, queries, key_full, value_full = pl.pallas_call(
        functools.partial(early_kernel, steps, heads),
        out_shape=[
            struct((samples, record, 2 * rows), f32),
            struct((samples, 2 * rows, head_features), bf16),
            struct((features, head_features), bf16),
            struct((head_features, features), bf16),
        ],
        scratch_shapes=[
            pltpu.VMEM((features, 2 * head_features), full_type),
            pltpu.VMEM((features, head_features), full_type),
            spread,
        ],
        compiler_params=params,
        name="early",
    )(weights_mine, weights_other, bias_row, shifted, parcel_mine, swapped, swapped_value, *ring)
    keep, got = [], []
    chunks = 2
    each = samples // chunks
    for c in range(chunks):
        kept, give = pl.pallas_call(
            functools.partial(late_kernel, steps, heads, c * each),
            out_shape=[struct((each // 2, record, 2 * rows), f32)] * 2,
            scratch_shapes=[pltpu.VMEM((each, record, 2 * rows), f32), spread],
            compiler_params=params,
            name="late",
        )(partial, queries, key_full, value_full, parcel_mine, swapped, last)
        keep.append(kept)
        got.append(swap_cores(give))
    return pl.pallas_call(
        functools.partial(finish_kernel, heads, chunks),
        out_shape=struct(activations.shape, bf16),
        scratch_shapes=[pltpu.VMEM((head_features, features), output_type)],
        compiler_params=params,
        name="finish",
    )(output_mine, output_other, activations, output_gate, *keep, *got)


def solution(mesh):
    return jax.shard_map(
        body,
        mesh=mesh,
        in_specs=(
            P("noise", "row", None),
            P("noise", "row", None),
            P("noise", "row", None),
            P("noise", "row", None),
            P("row", "noise", None),
            P(),
            P("noise", None),
            P(),
            P("noise", None),
            P("noise", None),
            P("noise", None),
            P("noise", "row"),
        ),
        out_specs=P("noise", "row", None),
        check_vma=False,
    )
```

```python
import functools
import math

import jax
import jax.numpy as jnp
from jax import lax
from jax.experimental import pallas as pl
from jax.experimental.pallas import tpu as pltpu
from jax.sharding import PartitionSpec as P

epsilon = 1e-05
masked_score = -1e30
absent = 32768.0
log2_e = math.log2(math.e)
vmem_bytes = 40 * 2**20
wide_bytes = 60 * 2**20


def layer_norm(tensor):
    average = jnp.mean(tensor, axis=-1, keepdims=True)
    centred = tensor - average
    variance = jnp.mean(centred * centred, axis=-1, keepdims=True)
    return centred * lax.rsqrt(variance + epsilon)


def shift_kernel(
    activations_hbm,
    scale_hbm,
    shift_hbm,
    mask_hbm,
    query_hbm,
    key_hbm,
    output_hbm,
    shifted_hbm,
    sent_hbm,
    packed_hbm,
    extended_hbm,
    shifted,
    sent,
    extended,
    activations,
    cond_scale,
    cond_shift,
    token_mask,
    query_weight,
    key_weight,
    output_weight,
    sems,
    sems_out,
):
    samples, rows, features = activations.shape
    copies = [pltpu.make_async_copy(mask_hbm, token_mask, sems.at[0])]
    for s in range(samples):
        for t, (source, target) in enumerate(
            ((activations_hbm, activations), (scale_hbm, cond_scale), (shift_hbm, cond_shift))
        ):
            copies.append(pltpu.make_async_copy(source.at[s], target.at[s], sems.at[1 + 3 * s + t]))
    copies.append(pltpu.make_async_copy(query_hbm, query_weight, sems.at[1 + 3 * samples]))
    copies.append(pltpu.make_async_copy(key_hbm, key_weight, sems.at[2 + 3 * samples]))
    copies.append(pltpu.make_async_copy(output_hbm, output_weight, sems.at[3 + 3 * samples]))
    for copy in copies:
        copy.start()
    diagonal = lax.broadcasted_iota(jnp.int32, (rows, rows), 0) == lax.broadcasted_iota(
        jnp.int32, (rows, rows), 1
    )
    copies[0].wait()
    written = []
    for s in range(samples):
        for copy in copies[1 + 3 * s : 4 + 3 * s]:
            copy.wait()
        normed = layer_norm(activations[s].astype(jnp.float32))
        result = cond_scale[s].astype(jnp.float32) * normed + cond_shift[s].astype(jnp.float32)
        flags = jnp.where(diagonal, token_mask[s : s + 1, :].astype(jnp.float32), 0.0)
        valid = jnp.sum(flags, axis=1, keepdims=True) > 0.0
        shifted[s] = result.astype(jnp.bfloat16)
        sent[s] = jnp.where(valid, result, absent).astype(jnp.bfloat16)
        for t, (source, target) in enumerate(((sent, sent_hbm), (shifted, shifted_hbm))):
            written.append(pltpu.make_async_copy(source.at[s], target.at[s], sems_out.at[2 * s + t]))
            written[-1].start()
    core = lax.rem(lax.axis_index("row"), 2)
    half, breadth = packed_hbm.shape[0], query_weight.shape[1]
    for w, weight in enumerate((query_weight, key_weight)):
        copies[1 + 3 * samples + w].wait()
        whole = weight[...].astype(jnp.float32)
        extended[0:half, w * breadth : (w + 1) * breadth] = jnp.where(
            core == 0, whole[:half], whole[half:]
        ).astype(jnp.bfloat16)
    written.append(
        pltpu.make_async_copy(
            extended.at[0:half, 0 : 2 * breadth], packed_hbm, sems_out.at[2 * samples]
        )
    )
    written[-1].start()
    copies[-1].wait()
    extended[:, 2 * breadth :] = jnp.where(
        core == 0, output_weight[:, :breadth], output_weight[:, breadth:]
    )
    written.append(pltpu.make_async_copy(extended, extended_hbm, sems_out.at[2 * samples + 1]))
    written[-1].start()
    for copy in written:
        copy.wait()


def bias_kernel(pair_hbm, value_hbm, weights_hbm, parcel, pair, value_weight, weights, collected, sems):
    rows, columns, channels = pair.shape
    heads = weights.shape[0]
    per, batches = 8, 2
    batch = rows // batches
    copies = [pltpu.make_async_copy(weights_hbm, weights, sems.at[batches])]
    for i in range(batches):
        here = pl.ds(i * batch, batch)
        copies.append(pltpu.make_async_copy(pair_hbm.at[here], pair.at[here], sems.at[i]))
    copies.append(pltpu.make_async_copy(value_hbm, value_weight, sems.at[batches + 1]))
    for copy in copies:
        copy.start()
    copies[0].wait()
    record = 2 * heads
    extended = jnp.concatenate(
        [weights[...], jnp.full((heads, channels), 1.0 / channels, jnp.bfloat16)], axis=0
    )
    square = (channels, channels)
    diagonal = lax.broadcasted_iota(jnp.int32, square, 0) == lax.broadcasted_iota(jnp.int32, square, 1)
    centring = (jnp.where(diagonal, 1.0, 0.0) - 1.0 / channels).astype(jnp.bfloat16)
    lane = lax.broadcasted_iota(jnp.int32, (1, rows), 1)
    squares = jnp.zeros((columns, rows), jnp.float32)
    for i in range(rows // per):
        if i * per % batch == 0:
            copies[1 + i * per // batch].wait()
        block = pair[i * per : (i + 1) * per].reshape(per * columns, channels)
        centred = jnp.dot(block, centring, preferred_element_type=jnp.float32)
        summed = jnp.sum(centred * centred, axis=1, keepdims=True)
        result = lax.dot_general(
            extended, block, (((1,), (1,)), ((), ())), preferred_element_type=jnp.float32
        )
        for r in range(per):
            row = i * per + r
            collected[row * record : (row + 1) * record, :] = result[:, r * columns : (r + 1) * columns]
            squares = jnp.where(lane == row, summed[r * columns : (r + 1) * columns], squares)
    core = lax.rem(lax.axis_index("row"), 2)
    half = columns // 2
    average = collected[pl.ds(heads, rows, stride=record), :].T
    inverse = lax.rsqrt(squares / channels + epsilon)
    for p in range(heads // 2):
        own, other = [], []
        for h in (2 * p, 2 * p + 1):
            summed = jnp.sum(weights[h : h + 1, :].astype(jnp.float32), axis=1, keepdims=True)
            turned = (collected[pl.ds(h, rows, stride=record), :].T - average * summed) * inverse
            low, up = turned[:half], turned[half:]
            own.append(jnp.where(core == 0, low, up))
            other.append(jnp.where(core == 0, up, low))
        at = p * half
        parcel[at : at + half, :] = jnp.concatenate(own, axis=1).astype(jnp.bfloat16)
        at += heads // 2 * half
        parcel[at : at + half, :] = jnp.concatenate(other[::-1], axis=1).astype(jnp.bfloat16)
    copies[-1].wait()
    depth, breadth = value_weight.shape
    whole = value_weight[...].astype(jnp.float32)
    kept = jnp.where(core == 0, whole[: depth // 2], whole[depth // 2 :]).astype(jnp.bfloat16)
    for t in range(breadth // columns):
        at = heads * half + t * (depth // 2)
        parcel[at : at + depth // 2, :] = kept[:, t * columns : (t + 1) * columns]


def spread_queries(heads, queries, spread):
    count, head_features = queries.shape
    width = head_features // heads
    reach = spread.shape[1]
    lane = lax.broadcasted_iota(jnp.int32, (1, reach), 1)
    turned = jnp.concatenate([queries[count // 2 :], queries[: count // 2]], axis=0)
    for h in range(heads):
        start, free = (0, reach - 1) if h < heads // 2 else (head_features - reach, 0)
        inside = ((lane >= h * width - start) & (lane < (h + 1) * width - start)).astype(jnp.bfloat16)
        extra = (lane == free).astype(jnp.bfloat16)
        own = (turned if h % 2 else queries)[:, start : start + reach]
        spread[h * count : (h + 1) * count, :] = own * inside + extra


def attend_keys(heads, tokens, keys, values, bias_of, spread):
    head_features = values.shape[0]
    width = head_features // heads
    count, reach = spread.shape[0] // heads, spread.shape[1]
    used = heads // 2 * width
    penalty = jnp.where(tokens[:, 0:1].astype(jnp.float32) > absent / 2, masked_score, 0.0)
    lane = lax.broadcasted_iota(jnp.int32, (1, reach), 1)
    scores = []
    for part in range(2):
        start = part * (head_features - reach)
        inside = lane < used if part == 0 else lane >= reach - used
        extended = jnp.where(inside, keys[:, start : start + reach], penalty).astype(jnp.bfloat16)
        scores.append(
            lax.dot_general(
                extended,
                spread[part * heads // 2 * count : (part + 1) * heads // 2 * count, :],
                (((1,), (1,)), ((), ())),
                preferred_element_type=jnp.float32,
            )
        )
    sums, highs, totals = [], [], []
    for h in range(heads):
        at = h % (heads // 2) * count
        score = scores[h // (heads // 2)][:, at : at + count] * (log2_e / math.sqrt(width))
        score = score + bias_of(h) * log2_e
        high = jnp.max(score, axis=0, keepdims=True)
        probs = jnp.exp2(score - high)
        totals.append(jnp.sum(probs, axis=0, keepdims=True))
        highs.append(high)
        sums.append(
            jnp.dot(
                values[h * width : (h + 1) * width],
                probs.astype(jnp.bfloat16),
                preferred_element_type=jnp.float32,
            )
        )
    return sums, highs, totals


def bias_picker(parcel, swapped, steps, first, rows):
    chip = lax.axis_index("row") // 2
    place = lax.axis_index("noise")
    left = lax.broadcasted_iota(jnp.int32, (1, 2 * rows), 1) < rows

    here = jnp.where(chip % 2 == 1, (chip + 1) // 2, lax.rem(steps - chip // 2, steps))

    def pick(b, h):
        position = lax.rem(here - (first + b) + steps, steps)
        outward = (position > 0) & (position <= steps // 2)
        origin = jnp.where(outward, 2 * position - 1, 2 * lax.rem(steps - position, steps))
        part = origin ^ place
        at = slice(h // 2 * rows, (h // 2 + 1) * rows)
        pairs = parcel[part, at].astype(jnp.float32), swapped[part, at].astype(jnp.float32)
        return jnp.where(left, pairs[h % 2], pairs[1 - h % 2])

    return pick


def early_kernel(steps, heads, weights_mine, weights_other, query_bias, shifted, shifted_other, parcel, swapped, swapped_value, *refs):
    blocks = refs[: steps - 1]
    partial, queries, key_weight, value_weight, full, full_value, spread = refs[steps - 1 :]
    samples, rows, features = shifted.shape
    noise_size, half, _ = weights_mine.shape
    breadth = key_weight.shape[1]
    width = breadth // heads
    core = lax.rem(lax.axis_index("row"), 2)
    place = lax.axis_index("noise")
    below = parcel.shape[1] - breadth // 128 * half
    for part, value, skipped, of_core in (
        (weights_mine, parcel, below, core),
        (weights_other, swapped_value, 0, 1 - core),
    ):
        for k in range(noise_size):
            start = ((place ^ k) * 2 + of_core) * half
            down = pl.ds(pl.multiple_of(start, math.gcd(half, 32)), half)
            full[down, :] = part[k].astype(full.dtype)
            for t in range(breadth // 128):
                at = skipped + t * half
                full_value[down, t * 128 : (t + 1) * 128] = value[k, at : at + half].astype(full.dtype)
    key_weight[...] = full[:, breadth : 2 * breadth].astype(jnp.bfloat16)
    value_weight[...] = full_value[...].astype(jnp.float32).T.astype(jnp.bfloat16)
    for side, tokens in enumerate((shifted, shifted_other)):
        result = jnp.dot(
            tokens[...].reshape(samples * rows, features),
            full[:, 0:breadth].astype(jnp.bfloat16),
            preferred_element_type=jnp.float32,
        ) + query_bias[...].astype(jnp.float32)
        queries[:, side * rows : (side + 1) * rows] = result.astype(jnp.bfloat16).reshape(
            samples, rows, breadth
        )
    pick = bias_picker(parcel, swapped, steps, 0, rows)
    for s in range(samples):
        tokens = jnp.concatenate([block[s] for block in blocks], axis=0)
        keys = jnp.dot(tokens, key_weight[...], preferred_element_type=jnp.float32)
        values = lax.dot_general(
            value_weight[...], tokens, (((1,), (1,)), ((), ())), preferred_element_type=jnp.float32
        ).astype(jnp.bfloat16)
        spread_queries(heads, queries[s], spread)
        sums, highs, totals = attend_keys(
            heads,
            tokens,
            keys,
            values,
            lambda h: jnp.concatenate([pick(b, h) for b in range(steps - 1)], axis=0),
            spread,
        )
        for h in range(heads):
            partial[s, h * width : (h + 1) * width] = sums[h]
            partial[s, breadth + h : breadth + h + 1] = highs[h]
            partial[s, breadth + heads + h : breadth + heads + h + 1] = totals[h]


def late_kernel(steps, heads, first, partial, queries, key_weight, value_weight, parcel, swapped, block, keep, give, merged, spread):
    samples = merged.shape[0]
    rows = block.shape[1]
    breadth = key_weight.shape[1]
    width = breadth // heads
    pick = bias_picker(parcel, swapped, steps, steps - 1, rows)
    tokens = block[first : first + samples].reshape(samples * rows, block.shape[2])
    keys = jnp.dot(tokens, key_weight[...], preferred_element_type=jnp.float32)
    values = lax.dot_general(
        value_weight[...], tokens, (((1,), (1,)), ((), ())), preferred_element_type=jnp.float32
    ).astype(jnp.bfloat16)
    for s in range(samples):
        here = slice(s * rows, (s + 1) * rows)
        spread_queries(heads, queries[first + s], spread)
        sums, highs, totals = attend_keys(
            heads, tokens[here], keys[here], values[:, here], lambda h: pick(0, h), spread
        )
        before = partial.at[first + s]
        for h in range(heads):
            at_high = slice(breadth + h, breadth + h + 1)
            at_total = slice(breadth + heads + h, breadth + heads + h + 1)
            high = jnp.maximum(before[at_high], highs[h])
            old, new = jnp.exp2(before[at_high] - high), jnp.exp2(highs[h] - high)
            across = slice(h * width, (h + 1) * width)
            merged[s, across] = before[across] * old + sums[h] * new
            merged[s, at_high] = high
            merged[s, at_total] = before[at_total] * old + totals[h] * new
    half = merged.shape[2] // 2
    left = lax.broadcasted_iota(jnp.int32, (1, 2 * half), 1) < half
    row = lax.broadcasted_iota(jnp.int32, (merged.shape[1], 1), 0)
    head = jnp.where(row < breadth, row // width, (row - breadth) % heads)
    even = head % 2 == 0
    for pair in range(samples // 2):
        a, b = merged[2 * pair], merged[2 * pair + 1]
        lefts = jnp.where(left, a, pltpu.roll(b, half, 1))
        rights = jnp.where(left, pltpu.roll(a, half, 1), b)
        keep[pair] = jnp.where(even, lefts, rights)
        give[pair] = jnp.where(even, rights, lefts)


def finish_kernel(heads, chunks, output_mine, output_other, activations, output_gate, *refs):
    keep, got = refs[:chunks], refs[chunks : 2 * chunks]
    updated, output_weight = refs[2 * chunks :]
    noise_size, part_rows, part_columns = output_mine.shape
    core = lax.rem(lax.axis_index("row"), 2)
    breadth = output_weight.shape[0]
    width = breadth // heads
    rows = updated.shape[1]
    place = lax.axis_index("noise")
    for k in range(noise_size):
        down = pl.ds(pl.multiple_of((place ^ k) * part_rows, math.gcd(part_rows, 32)), part_rows)
        for part, of_core in ((output_mine, core), (output_other, 1 - core)):
            along = pl.ds(pl.multiple_of(of_core * part_columns, 128), part_columns)
            output_weight[down, along] = part[k].astype(output_weight.dtype)
    pairs = keep[0].shape[0]
    for pair in range(chunks * pairs):
        own, other = keep[pair // pairs].at[pair % pairs], got[pair // pairs].at[pair % pairs]
        parts = []
        for h in range(heads):
            at_high = slice(breadth + h, breadth + h + 1)
            at_total = slice(breadth + heads + h, breadth + heads + h + 1)
            across = slice(h * width, (h + 1) * width)
            high = jnp.maximum(own[at_high], other[at_high])
            mine, theirs = jnp.exp2(own[at_high] - high), jnp.exp2(other[at_high] - high)
            total = own[at_total] * mine + other[at_total] * theirs
            parts.append((own[across] * mine + other[across] * theirs) / total)
        attended = jnp.concatenate(parts, axis=0).T.astype(jnp.bfloat16)
        projected = jnp.dot(
            attended, output_weight[...].astype(jnp.bfloat16), preferred_element_type=jnp.float32
        )
        for side in range(2):
            s = 2 * pair + side
            gate = jax.nn.sigmoid(output_gate[s].astype(jnp.float32))
            updated[s] = (
                activations[s].astype(jnp.float32) + gate * projected[side * rows : (side + 1) * rows]
            ).astype(jnp.bfloat16)


def swap_cores(array):
    return lax.ppermute(array, "row", [(i, i ^ 1) for i in range(lax.axis_size("row"))])


def ring_chip(position, steps):
    return 2 * position - 1 if 0 < position <= steps // 2 else 2 * ((steps - position) % steps)


def next_chip(array):
    steps = lax.axis_size("row") // 2
    order = [ring_chip(p, steps) for p in range(steps)]
    pairs = [
        (2 * order[p] + c, 2 * order[(p + 1) % steps] + c) for p in range(steps) for c in range(2)
    ]
    return lax.ppermute(array, "row", pairs)


def from_noise(array, k):
    if k == 0:
        return array
    return lax.ppermute(array, "noise", [(i, i ^ k) for i in range(lax.axis_size("noise"))])


def body(
    activations,
    cond_scale,
    cond_shift,
    output_gate,
    pair_repr,
    bias_weight,
    query_weight,
    query_bias,
    key_weight,
    value_weight,
    output_weight,
    token_mask,
):
    samples, rows, features = activations.shape
    heads = bias_weight.shape[1]
    head_features = query_weight.shape[1]
    noise_size = lax.axis_size("noise")
    steps = lax.axis_size("row") // 2
    assert noise_size == steps and pair_repr.shape[1] == 2 * rows
    bf16, f32 = jnp.bfloat16, jnp.float32
    params = pltpu.CompilerParams(vmem_limit_bytes=vmem_bytes)
    struct = jax.ShapeDtypeStruct
    after = lax.optimization_barrier
    half = query_weight.shape[0] // 2

    in_hbm = pl.BlockSpec(memory_space=pltpu.HBM)
    packed_shape, extended_shape = (half, 2 * head_features), (half, 3 * head_features)
    assert output_weight.shape == (half, 2 * head_features)
    shifted, sent, packed, extended = pl.pallas_call(
        shift_kernel,
        in_specs=[in_hbm] * 7,
        out_specs=[in_hbm] * 4,
        out_shape=[struct(activations.shape, bf16)] * 2
        + [struct(packed_shape, bf16), struct(extended_shape, bf16)],
        scratch_shapes=[pltpu.VMEM(activations.shape, bf16)] * 2
        + [pltpu.VMEM(extended_shape, bf16)]
        + [pltpu.VMEM(activations.shape, bf16)] * 3
        + [pltpu.VMEM(token_mask.shape, jnp.int32)]
        + [pltpu.VMEM(query_weight.shape, bf16)] * 2
        + [pltpu.VMEM(output_weight.shape, bf16)]
        + [pltpu.SemaphoreType.DMA((3 * samples + 4,)), pltpu.SemaphoreType.DMA((2 * samples + 2,))],
        compiler_params=pltpu.CompilerParams(vmem_limit_bytes=wide_bytes),
        name="shift",
    )(activations, cond_scale, cond_shift, token_mask, query_weight, key_weight, output_weight)

    ring = [sent, next_chip(sent)]
    weights = [extended, from_noise(extended, 1)] + [from_noise(packed, k) for k in range(2, noise_size)]
    shifted_other = swap_cores(shifted)
    head_weights, _ = after((bias_weight.T, packed))
    columns = pair_repr.shape[1]
    tile_rows = heads * rows
    parcel = pl.pallas_call(
        bias_kernel,
        in_specs=[in_hbm] * 3,
        out_shape=struct((tile_rows + 3 * half, columns), bf16),
        scratch_shapes=[
            pltpu.VMEM(pair_repr.shape, bf16),
            pltpu.VMEM(value_weight.shape, bf16),
            pltpu.VMEM(head_weights.shape, bf16),
            pltpu.VMEM((rows * 2 * heads, columns), f32),
            pltpu.SemaphoreType.DMA((4,)),
        ],
        compiler_params=pltpu.CompilerParams(vmem_limit_bytes=wide_bytes),
        name="bias",
    )(pair_repr, value_weight, head_weights)
    ring[1], weights, parcel, shifted_other = after((ring[1], weights, parcel, shifted_other))
    ring.append(next_chip(ring[1]))
    output_mine = jnp.stack([part[:, 2 * head_features :] for part in weights[:2]])
    weights_mine = jnp.stack([part[:, : 2 * head_features] for part in weights])
    weights_other = swap_cores(weights_mine)
    parcel, _ = after((parcel, weights_mine))
    parcels = [from_noise(parcel, k) for k in range(noise_size)]

    for _ in range(steps - 3):
        ring.append(next_chip(ring[-1]))
    last = ring.pop()
    parcel_mine = jnp.stack(parcels)
    swapped = swap_cores(parcel_mine[:, tile_rows // 2 : tile_rows])
    swapped_value = swap_cores(parcel_mine[:, tile_rows:])
    for k in range(1, noise_size.bit_length() - 1):
        output_mine = jnp.concatenate([output_mine, from_noise(output_mine, 2**k)], axis=0)
    output_other = swap_cores(output_mine)

    bias_row = query_bias.reshape(1, head_features)
    record = head_features + 2 * heads
    full_type = f32 if half % 16 else bf16
    output_type = f32 if output_weight.shape[0] % 16 else bf16
    spread = pltpu.VMEM((heads * 2 * rows, 256), bf16)
    partial, queries, key_full, value_full = pl.pallas_call(
        functools.partial(early_kernel, steps, heads),
        out_shape=[
            struct((samples, record, 2 * rows), f32),
            struct((samples, 2 * rows, head_features), bf16),
            struct((features, head_features), bf16),
            struct((head_features, features), bf16),
        ],
        scratch_shapes=[
            pltpu.VMEM((features, 2 * head_features), full_type),
            pltpu.VMEM((features, head_features), full_type),
            spread,
        ],
        compiler_params=params,
        name="early",
    )(weights_mine, weights_other, bias_row, shifted, shifted_other, parcel_mine, swapped, swapped_value, *ring)
    keep, got = [], []
    chunks = 2
    each = samples // chunks
    for c in range(chunks):
        kept, give = pl.pallas_call(
            functools.partial(late_kernel, steps, heads, c * each),
            out_shape=[struct((each // 2, record, 2 * rows), f32)] * 2,
            scratch_shapes=[pltpu.VMEM((each, record, 2 * rows), f32), spread],
            compiler_params=params,
            name="late",
        )(partial, queries, key_full, value_full, parcel_mine, swapped, last)
        keep.append(kept)
        got.append(swap_cores(give))
    return pl.pallas_call(
        functools.partial(finish_kernel, heads, chunks),
        out_shape=struct(activations.shape, bf16),
        scratch_shapes=[pltpu.VMEM((head_features, features), output_type)],
        compiler_params=params,
        name="finish",
    )(output_mine, output_other, activations, output_gate, *keep, *got)


def solution(mesh):
    return jax.shard_map(
        body,
        mesh=mesh,
        in_specs=(
            P("noise", "row", None),
            P("noise", "row", None),
            P("noise", "row", None),
            P("noise", "row", None),
            P("row", "noise", None),
            P(),
            P("noise", None),
            P(),
            P("noise", None),
            P("noise", None),
            P("noise", None),
            P("noise", "row"),
        ),
        out_specs=P("noise", "row", None),
        check_vma=False,
    )
```

```python
import functools
import math

import jax
import jax.numpy as jnp
from jax import lax
from jax.experimental import pallas as pl
from jax.experimental.pallas import tpu as pltpu
from jax.sharding import PartitionSpec as P

epsilon = 1e-05
masked_score = -1e30
absent = 32768.0
log2_e = math.log2(math.e)
vmem_bytes = 40 * 2**20
wide_bytes = 60 * 2**20


def layer_norm(tensor):
    average = jnp.mean(tensor, axis=-1, keepdims=True)
    centred = tensor - average
    variance = jnp.mean(centred * centred, axis=-1, keepdims=True)
    return centred * lax.rsqrt(variance + epsilon)


def shift_kernel(
    activations_hbm,
    scale_hbm,
    shift_hbm,
    mask_hbm,
    query_hbm,
    key_hbm,
    output_hbm,
    shifted_hbm,
    sent_hbm,
    packed_hbm,
    columns_hbm,
    shifted,
    sent,
    packed,
    columns,
    activations,
    cond_scale,
    cond_shift,
    token_mask,
    query_weight,
    key_weight,
    output_weight,
    sems,
    sems_out,
):
    samples, rows, features = activations.shape
    copies = [pltpu.make_async_copy(mask_hbm, token_mask, sems.at[0])]
    for s in range(samples):
        for t, (source, target) in enumerate(
            ((activations_hbm, activations), (scale_hbm, cond_scale), (shift_hbm, cond_shift))
        ):
            copies.append(pltpu.make_async_copy(source.at[s], target.at[s], sems.at[1 + 3 * s + t]))
    copies.append(pltpu.make_async_copy(query_hbm, query_weight, sems.at[1 + 3 * samples]))
    copies.append(pltpu.make_async_copy(key_hbm, key_weight, sems.at[2 + 3 * samples]))
    copies.append(pltpu.make_async_copy(output_hbm, output_weight, sems.at[3 + 3 * samples]))
    for copy in copies:
        copy.start()
    diagonal = lax.broadcasted_iota(jnp.int32, (rows, rows), 0) == lax.broadcasted_iota(
        jnp.int32, (rows, rows), 1
    )
    copies[0].wait()
    written = []
    for s in range(samples):
        for copy in copies[1 + 3 * s : 4 + 3 * s]:
            copy.wait()
        normed = layer_norm(activations[s].astype(jnp.float32))
        result = cond_scale[s].astype(jnp.float32) * normed + cond_shift[s].astype(jnp.float32)
        flags = jnp.where(diagonal, token_mask[s : s + 1, :].astype(jnp.float32), 0.0)
        valid = jnp.sum(flags, axis=1, keepdims=True) > 0.0
        shifted[s] = result.astype(jnp.bfloat16)
        sent[s] = jnp.where(valid, result, absent).astype(jnp.bfloat16)
        for t, (source, target) in enumerate(((sent, sent_hbm), (shifted, shifted_hbm))):
            written.append(pltpu.make_async_copy(source.at[s], target.at[s], sems_out.at[2 * s + t]))
            written[-1].start()
    core = lax.rem(lax.axis_index("row"), 2)
    half, breadth = packed.shape[0], query_weight.shape[1]
    for w, weight in enumerate((query_weight, key_weight)):
        copies[1 + 3 * samples + w].wait()
        whole = weight[...].astype(jnp.float32)
        packed[:, w * breadth : (w + 1) * breadth] = jnp.where(
            core == 0, whole[:half], whole[half:]
        ).astype(jnp.bfloat16)
    written.append(pltpu.make_async_copy(packed, packed_hbm, sems_out.at[2 * samples]))
    written[-1].start()
    copies[-1].wait()
    columns[...] = jnp.where(core == 0, output_weight[:, :breadth], output_weight[:, breadth:])
    written.append(pltpu.make_async_copy(columns, columns_hbm, sems_out.at[2 * samples + 1]))
    written[-1].start()
    for copy in written:
        copy.wait()


def bias_kernel(pair_hbm, value_hbm, weights_hbm, parcel, pair, value_weight, weights, collected, sems):
    rows, columns, channels = pair.shape
    heads = weights.shape[0]
    per, batches = 8, 2
    batch = rows // batches
    copies = [pltpu.make_async_copy(weights_hbm, weights, sems.at[batches])]
    for i in range(batches):
        here = pl.ds(i * batch, batch)
        copies.append(pltpu.make_async_copy(pair_hbm.at[here], pair.at[here], sems.at[i]))
    copies.append(pltpu.make_async_copy(value_hbm, value_weight, sems.at[batches + 1]))
    for copy in copies:
        copy.start()
    copies[0].wait()
    record = 2 * heads
    extended = jnp.concatenate(
        [weights[...], jnp.full((heads, channels), 1.0 / channels, jnp.bfloat16)], axis=0
    )
    square = (channels, channels)
    diagonal = lax.broadcasted_iota(jnp.int32, square, 0) == lax.broadcasted_iota(jnp.int32, square, 1)
    centring = (jnp.where(diagonal, 1.0, 0.0) - 1.0 / channels).astype(jnp.bfloat16)
    lane = lax.broadcasted_iota(jnp.int32, (1, rows), 1)
    squares = jnp.zeros((columns, rows), jnp.float32)
    for i in range(rows // per):
        if i * per % batch == 0:
            copies[1 + i * per // batch].wait()
        block = pair[i * per : (i + 1) * per].reshape(per * columns, channels)
        centred = jnp.dot(block, centring, preferred_element_type=jnp.float32)
        summed = jnp.sum(centred * centred, axis=1, keepdims=True)
        result = lax.dot_general(
            extended, block, (((1,), (1,)), ((), ())), preferred_element_type=jnp.float32
        )
        for r in range(per):
            row = i * per + r
            collected[row * record : (row + 1) * record, :] = result[:, r * columns : (r + 1) * columns]
            squares = jnp.where(lane == row, summed[r * columns : (r + 1) * columns], squares)
    core = lax.rem(lax.axis_index("row"), 2)
    half = columns // 2
    average = collected[pl.ds(heads, rows, stride=record), :].T
    inverse = lax.rsqrt(squares / channels + epsilon)
    for p in range(heads // 2):
        own, other = [], []
        for h in (2 * p, 2 * p + 1):
            summed = jnp.sum(weights[h : h + 1, :].astype(jnp.float32), axis=1, keepdims=True)
            turned = (collected[pl.ds(h, rows, stride=record), :].T - average * summed) * inverse
            low, up = turned[:half], turned[half:]
            own.append(jnp.where(core == 0, low, up))
            other.append(jnp.where(core == 0, up, low))
        at = p * half
        parcel[at : at + half, :] = jnp.concatenate(own, axis=1).astype(jnp.bfloat16)
        at += heads // 2 * half
        parcel[at : at + half, :] = jnp.concatenate(other[::-1], axis=1).astype(jnp.bfloat16)
    copies[-1].wait()
    depth, breadth = value_weight.shape
    whole = value_weight[...].astype(jnp.float32)
    kept = jnp.where(core == 0, whole[: depth // 2], whole[depth // 2 :]).astype(jnp.bfloat16)
    for t in range(breadth // columns):
        at = heads * half + t * (depth // 2)
        parcel[at : at + depth // 2, :] = kept[:, t * columns : (t + 1) * columns]


def spread_queries(heads, queries, spread):
    count, head_features = queries.shape
    width = head_features // heads
    reach = spread.shape[1]
    lane = lax.broadcasted_iota(jnp.int32, (1, reach), 1)
    turned = jnp.concatenate([queries[count // 2 :], queries[: count // 2]], axis=0)
    for h in range(heads):
        start, free = (0, reach - 1) if h < heads // 2 else (head_features - reach, 0)
        inside = ((lane >= h * width - start) & (lane < (h + 1) * width - start)).astype(jnp.bfloat16)
        extra = (lane == free).astype(jnp.bfloat16)
        own = (turned if h % 2 else queries)[:, start : start + reach]
        spread[h * count : (h + 1) * count, :] = own * inside + extra


def attend_keys(heads, tokens, keys, values, bias_of, spread):
    head_features = values.shape[0]
    width = head_features // heads
    count, reach = spread.shape[0] // heads, spread.shape[1]
    used = heads // 2 * width
    penalty = jnp.where(tokens[:, 0:1].astype(jnp.float32) > absent / 2, masked_score, 0.0)
    lane = lax.broadcasted_iota(jnp.int32, (1, reach), 1)
    scores = []
    for part in range(2):
        start = part * (head_features - reach)
        inside = lane < used if part == 0 else lane >= reach - used
        extended = jnp.where(inside, keys[:, start : start + reach], penalty).astype(jnp.bfloat16)
        scores.append(
            lax.dot_general(
                extended,
                spread[part * heads // 2 * count : (part + 1) * heads // 2 * count, :],
                (((1,), (1,)), ((), ())),
                preferred_element_type=jnp.float32,
            )
        )
    sums, highs, totals = [], [], []
    for h in range(heads):
        at = h % (heads // 2) * count
        score = scores[h // (heads // 2)][:, at : at + count] * (log2_e / math.sqrt(width))
        score = score + bias_of(h) * log2_e
        high = jnp.max(score, axis=0, keepdims=True)
        probs = jnp.exp2(score - high)
        totals.append(jnp.sum(probs, axis=0, keepdims=True))
        highs.append(high)
        sums.append(
            jnp.dot(
                values[h * width : (h + 1) * width],
                probs.astype(jnp.bfloat16),
                preferred_element_type=jnp.float32,
            )
        )
    return sums, highs, totals


def bias_picker(parcel, swapped, steps, first, rows):
    chip = lax.axis_index("row") // 2
    place = lax.axis_index("noise")
    left = lax.broadcasted_iota(jnp.int32, (1, 2 * rows), 1) < rows

    here = jnp.where(chip % 2 == 1, (chip + 1) // 2, lax.rem(steps - chip // 2, steps))

    def pick(b, h):
        position = lax.rem(here - (first + b) + steps, steps)
        outward = (position > 0) & (position <= steps // 2)
        origin = jnp.where(outward, 2 * position - 1, 2 * lax.rem(steps - position, steps))
        part = origin ^ place
        at = slice(h // 2 * rows, (h // 2 + 1) * rows)
        pairs = parcel[part, at].astype(jnp.float32), swapped[part, at].astype(jnp.float32)
        return jnp.where(left, pairs[h % 2], pairs[1 - h % 2])

    return pick


def early_kernel(steps, heads, weights_mine, weights_other, query_bias, shifted, parcel, swapped, swapped_value, *refs):
    blocks = refs[: steps - 1]
    partial, queries, key_weight, value_weight, full, full_value, spread = refs[steps - 1 :]
    samples, rows, features = shifted.shape
    noise_size = swapped_value.shape[0]
    half = weights_mine.shape[1] - samples * rows // noise_size
    breadth = key_weight.shape[1]
    width = breadth // heads
    core = lax.rem(lax.axis_index("row"), 2)
    place = lax.axis_index("noise")
    below = parcel.shape[1] - breadth // 128 * half
    for part, value, skipped, of_core in (
        (weights_mine, parcel, below, core),
        (weights_other, swapped_value, 0, 1 - core),
    ):
        for k in range(noise_size):
            start = ((place ^ k) * 2 + of_core) * half
            down = pl.ds(pl.multiple_of(start, math.gcd(half, 32)), half)
            full[down, :] = part[k, 0:half].astype(full.dtype)
            for t in range(breadth // 128):
                at = skipped + t * half
                full_value[down, t * 128 : (t + 1) * 128] = value[k, at : at + half].astype(full.dtype)
    key_weight[...] = full[:, breadth : 2 * breadth].astype(jnp.bfloat16)
    value_weight[...] = full_value[...].astype(jnp.float32).T.astype(jnp.bfloat16)
    for side, tokens in enumerate((shifted[...], weights_other[:, half:])):
        result = jnp.dot(
            tokens.reshape(samples * rows, features),
            full[:, 0:breadth].astype(jnp.bfloat16),
            preferred_element_type=jnp.float32,
        ) + query_bias[...].astype(jnp.float32)
        queries[:, side * rows : (side + 1) * rows] = result.astype(jnp.bfloat16).reshape(
            samples, rows, breadth
        )
    pick = bias_picker(parcel, swapped, steps, 0, rows)
    for s in range(samples):
        tokens = jnp.concatenate([block[s] for block in blocks], axis=0)
        keys = jnp.dot(tokens, key_weight[...], preferred_element_type=jnp.float32)
        values = lax.dot_general(
            value_weight[...], tokens, (((1,), (1,)), ((), ())), preferred_element_type=jnp.float32
        ).astype(jnp.bfloat16)
        spread_queries(heads, queries[s], spread)
        sums, highs, totals = attend_keys(
            heads,
            tokens,
            keys,
            values,
            lambda h: jnp.concatenate([pick(b, h) for b in range(steps - 1)], axis=0),
            spread,
        )
        for h in range(heads):
            partial[s, h * width : (h + 1) * width] = sums[h]
            partial[s, breadth + h : breadth + h + 1] = highs[h]
            partial[s, breadth + heads + h : breadth + heads + h + 1] = totals[h]


def late_kernel(steps, heads, first, partial, queries, key_weight, value_weight, parcel, swapped, block, keep, give, merged, spread):
    samples = merged.shape[0]
    rows = block.shape[1]
    breadth = key_weight.shape[1]
    width = breadth // heads
    pick = bias_picker(parcel, swapped, steps, steps - 1, rows)
    tokens = block[first : first + samples].reshape(samples * rows, block.shape[2])
    keys = jnp.dot(tokens, key_weight[...], preferred_element_type=jnp.float32)
    values = lax.dot_general(
        value_weight[...], tokens, (((1,), (1,)), ((), ())), preferred_element_type=jnp.float32
    ).astype(jnp.bfloat16)
    for s in range(samples):
        here = slice(s * rows, (s + 1) * rows)
        spread_queries(heads, queries[first + s], spread)
        sums, highs, totals = attend_keys(
            heads, tokens[here], keys[here], values[:, here], lambda h: pick(0, h), spread
        )
        before = partial.at[first + s]
        for h in range(heads):
            at_high = slice(breadth + h, breadth + h + 1)
            at_total = slice(breadth + heads + h, breadth + heads + h + 1)
            high = jnp.maximum(before[at_high], highs[h])
            old, new = jnp.exp2(before[at_high] - high), jnp.exp2(highs[h] - high)
            across = slice(h * width, (h + 1) * width)
            merged[s, across] = before[across] * old + sums[h] * new
            merged[s, at_high] = high
            merged[s, at_total] = before[at_total] * old + totals[h] * new
    half = merged.shape[2] // 2
    left = lax.broadcasted_iota(jnp.int32, (1, 2 * half), 1) < half
    row = lax.broadcasted_iota(jnp.int32, (merged.shape[1], 1), 0)
    head = jnp.where(row < breadth, row // width, (row - breadth) % heads)
    even = head % 2 == 0
    for pair in range(samples // 2):
        a, b = merged[2 * pair], merged[2 * pair + 1]
        lefts = jnp.where(left, a, pltpu.roll(b, half, 1))
        rights = jnp.where(left, pltpu.roll(a, half, 1), b)
        keep[pair] = jnp.where(even, lefts, rights)
        give[pair] = jnp.where(even, rights, lefts)


def finish_kernel(heads, first, output_mine, output_other, activations, output_gate, keep, got, *refs):
    updated_hbm, updated, output_weight, sems = refs[-4:]
    noise_size, part_rows, part_columns = output_mine.shape
    breadth = output_weight.shape[0]
    width = breadth // heads
    samples, rows, _ = updated.shape
    core = lax.rem(lax.axis_index("row"), 2)
    place = lax.axis_index("noise")
    for k in range(noise_size):
        down = pl.ds(pl.multiple_of((place ^ k) * part_rows, math.gcd(part_rows, 32)), part_rows)
        for part, of_core in ((output_mine, core), (output_other, 1 - core)):
            along = pl.ds(pl.multiple_of(of_core * part_columns, 128), part_columns)
            output_weight[down, along] = part[k].astype(output_weight.dtype)
    writes = []
    for pair in range(samples // 2):
        own, other = keep.at[pair], got.at[pair]
        parts = []
        for h in range(heads):
            at_high = slice(breadth + h, breadth + h + 1)
            at_total = slice(breadth + heads + h, breadth + heads + h + 1)
            across = slice(h * width, (h + 1) * width)
            high = jnp.maximum(own[at_high], other[at_high])
            mine, theirs = jnp.exp2(own[at_high] - high), jnp.exp2(other[at_high] - high)
            total = own[at_total] * mine + other[at_total] * theirs
            parts.append((own[across] * mine + other[across] * theirs) / total)
        attended = jnp.concatenate(parts, axis=0).T.astype(jnp.bfloat16)
        projected = jnp.dot(
            attended, output_weight[...].astype(jnp.bfloat16), preferred_element_type=jnp.float32
        )
        for side in range(2):
            s = 2 * pair + side
            gate = jax.nn.sigmoid(output_gate[first + s].astype(jnp.float32))
            updated[s] = (
                activations[first + s].astype(jnp.float32)
                + gate * projected[side * rows : (side + 1) * rows]
            ).astype(jnp.bfloat16)
            writes.append(pltpu.make_async_copy(updated.at[s], updated_hbm.at[first + s], sems.at[s]))
            writes[-1].start()
    for write in writes:
        write.wait()


def swap_cores(array):
    return lax.ppermute(array, "row", [(i, i ^ 1) for i in range(lax.axis_size("row"))])


def ring_chip(position, steps):
    return 2 * position - 1 if 0 < position <= steps // 2 else 2 * ((steps - position) % steps)


def next_chip(array):
    steps = lax.axis_size("row") // 2
    order = [ring_chip(p, steps) for p in range(steps)]
    pairs = [
        (2 * order[p] + c, 2 * order[(p + 1) % steps] + c) for p in range(steps) for c in range(2)
    ]
    return lax.ppermute(array, "row", pairs)


def from_noise(array, k):
    if k == 0:
        return array
    return lax.ppermute(array, "noise", [(i, i ^ k) for i in range(lax.axis_size("noise"))])


def body(
    activations,
    cond_scale,
    cond_shift,
    output_gate,
    pair_repr,
    bias_weight,
    query_weight,
    query_bias,
    key_weight,
    value_weight,
    output_weight,
    token_mask,
):
    samples, rows, features = activations.shape
    heads = bias_weight.shape[1]
    head_features = query_weight.shape[1]
    noise_size = lax.axis_size("noise")
    steps = lax.axis_size("row") // 2
    assert noise_size == steps and pair_repr.shape[1] == 2 * rows
    bf16, f32 = jnp.bfloat16, jnp.float32
    params = pltpu.CompilerParams(vmem_limit_bytes=vmem_bytes)
    struct = jax.ShapeDtypeStruct
    after = lax.optimization_barrier
    half = query_weight.shape[0] // 2

    in_hbm = pl.BlockSpec(memory_space=pltpu.HBM)
    packed_shape, columns_shape = (half, 2 * head_features), (output_weight.shape[0], features // 2)
    shifted, sent, packed, output_columns = pl.pallas_call(
        shift_kernel,
        in_specs=[in_hbm] * 7,
        out_specs=[in_hbm] * 4,
        out_shape=[struct(activations.shape, bf16)] * 2
        + [struct(packed_shape, bf16), struct(columns_shape, bf16)],
        scratch_shapes=[pltpu.VMEM(activations.shape, bf16)] * 2
        + [pltpu.VMEM(packed_shape, bf16), pltpu.VMEM(columns_shape, bf16)]
        + [pltpu.VMEM(activations.shape, bf16)] * 3
        + [pltpu.VMEM(token_mask.shape, jnp.int32)]
        + [pltpu.VMEM(query_weight.shape, bf16)] * 2
        + [pltpu.VMEM(output_weight.shape, bf16)]
        + [pltpu.SemaphoreType.DMA((3 * samples + 4,)), pltpu.SemaphoreType.DMA((2 * samples + 2,))],
        compiler_params=pltpu.CompilerParams(vmem_limit_bytes=wide_bytes),
        name="shift",
    )(activations, cond_scale, cond_shift, token_mask, query_weight, key_weight, output_weight)

    ring = [sent, next_chip(sent)]
    weights = [packed] + [from_noise(packed, k) for k in range(noise_size - 1, 0, -1)][::-1]
    output_next = from_noise(output_columns, 1)
    head_weights, _ = after((bias_weight.T, packed))
    columns = pair_repr.shape[1]
    tile_rows = heads * rows
    parcel = pl.pallas_call(
        bias_kernel,
        in_specs=[in_hbm] * 3,
        out_shape=struct((tile_rows + 3 * half, columns), bf16),
        scratch_shapes=[
            pltpu.VMEM(pair_repr.shape, bf16),
            pltpu.VMEM(value_weight.shape, bf16),
            pltpu.VMEM(head_weights.shape, bf16),
            pltpu.VMEM((rows * 2 * heads, columns), f32),
            pltpu.SemaphoreType.DMA((4,)),
        ],
        compiler_params=pltpu.CompilerParams(vmem_limit_bytes=wide_bytes),
        name="bias",
    )(pair_repr, value_weight, head_weights)
    ring[1], weights, parcel, output_next = after((ring[1], weights, parcel, output_next))
    ring.append(next_chip(ring[1]))
    output_mine = jnp.stack([output_columns, output_next])
    tokens = shifted.reshape(noise_size, samples * rows // noise_size, features)
    weights_mine = jnp.concatenate([jnp.stack(weights), tokens], axis=1)
    weights_other = swap_cores(weights_mine)
    parcels = [from_noise(parcel, k) for k in range(noise_size)]

    for _ in range(steps - 3):
        ring.append(next_chip(ring[-1]))
    last = ring.pop()
    parcel_mine = jnp.stack(parcels)
    swapped = swap_cores(parcel_mine[:, tile_rows // 2 : tile_rows])
    swapped_value = swap_cores(parcel_mine[:, tile_rows:])
    for k in range(1, noise_size.bit_length() - 1):
        output_mine = jnp.concatenate([output_mine, from_noise(output_mine, 2**k)], axis=0)
    output_other = swap_cores(output_mine)

    bias_row = query_bias.reshape(1, head_features)
    record = head_features + 2 * heads
    full_type = f32 if half % 16 else bf16
    output_type = f32 if output_weight.shape[0] % 16 else bf16
    spread = pltpu.VMEM((heads * 2 * rows, 256), bf16)
    partial, queries, key_full, value_full = pl.pallas_call(
        functools.partial(early_kernel, steps, heads),
        out_shape=[
            struct((samples, record, 2 * rows), f32),
            struct((samples, 2 * rows, head_features), bf16),
            struct((features, head_features), bf16),
            struct((head_features, features), bf16),
        ],
        scratch_shapes=[
            pltpu.VMEM((features, 2 * head_features), full_type),
            pltpu.VMEM((features, head_features), full_type),
            spread,
        ],
        compiler_params=params,
        name="early",
    )(weights_mine, weights_other, bias_row, shifted, parcel_mine, swapped, swapped_value, *ring)
    keep, got = [], []
    chunks = 2
    each = samples // chunks
    for c in range(chunks):
        kept, give = pl.pallas_call(
            functools.partial(late_kernel, steps, heads, c * each),
            out_shape=[struct((each // 2, record, 2 * rows), f32)] * 2,
            scratch_shapes=[pltpu.VMEM((each, record, 2 * rows), f32), spread],
            compiler_params=params,
            name="late",
        )(partial, queries, key_full, value_full, parcel_mine, swapped, last)
        keep.append(kept)
        got.append(swap_cores(give))
    updated = []
    for c in range(chunks):
        operands = [output_mine, output_other, activations, output_gate, keep[c], got[c], *updated]
        updated = [
            pl.pallas_call(
                functools.partial(finish_kernel, heads, c * each),
                in_specs=[pl.BlockSpec(memory_space=pltpu.VMEM)] * 6 + [in_hbm] * len(updated),
                out_specs=in_hbm,
                out_shape=struct(activations.shape, bf16),
                input_output_aliases={6: 0} if updated else {},
                scratch_shapes=[
                    pltpu.VMEM((each, rows, features), bf16),
                    pltpu.VMEM((head_features, features), output_type),
                    pltpu.SemaphoreType.DMA((each,)),
                ],
                compiler_params=params,
                name="finish",
            )(*operands)
        ]
    return updated[0]


def solution(mesh):
    return jax.shard_map(
        body,
        mesh=mesh,
        in_specs=(
            P("noise", "row", None),
            P("noise", "row", None),
            P("noise", "row", None),
            P("noise", "row", None),
            P("row", "noise", None),
            P(),
            P("noise", None),
            P(),
            P("noise", None),
            P("noise", None),
            P("noise", None),
            P("noise", "row"),
        ),
        out_specs=P("noise", "row", None),
        check_vma=False,
    )
```

```python
import functools
import math

import jax
import jax.numpy as jnp
from jax import lax
from jax.experimental import pallas as pl
from jax.experimental.pallas import tpu as pltpu
from jax.sharding import PartitionSpec as P

epsilon = 1e-05
masked_score = -1e30
absent = 32768.0
log2_e = math.log2(math.e)
vmem_bytes = 40 * 2**20
wide_bytes = 60 * 2**20


def layer_norm(tensor):
    average = jnp.mean(tensor, axis=-1, keepdims=True)
    centred = tensor - average
    variance = jnp.mean(centred * centred, axis=-1, keepdims=True)
    return centred * lax.rsqrt(variance + epsilon)


def shift_kernel(
    activations_hbm,
    scale_hbm,
    shift_hbm,
    mask_hbm,
    query_hbm,
    key_hbm,
    output_hbm,
    shifted_hbm,
    sent_hbm,
    packed_hbm,
    columns_hbm,
    shifted,
    sent,
    packed,
    columns,
    activations,
    cond_scale,
    cond_shift,
    token_mask,
    query_weight,
    key_weight,
    output_weight,
    sems,
    sems_out,
):
    samples, rows, features = activations.shape
    copies = [pltpu.make_async_copy(mask_hbm, token_mask, sems.at[0])]
    for s in range(samples):
        for t, (source, target) in enumerate(
            ((activations_hbm, activations), (scale_hbm, cond_scale), (shift_hbm, cond_shift))
        ):
            copies.append(pltpu.make_async_copy(source.at[s], target.at[s], sems.at[1 + 3 * s + t]))
    copies.append(pltpu.make_async_copy(query_hbm, query_weight, sems.at[1 + 3 * samples]))
    copies.append(pltpu.make_async_copy(key_hbm, key_weight, sems.at[2 + 3 * samples]))
    copies.append(pltpu.make_async_copy(output_hbm, output_weight, sems.at[3 + 3 * samples]))
    for copy in copies:
        copy.start()
    diagonal = lax.broadcasted_iota(jnp.int32, (rows, rows), 0) == lax.broadcasted_iota(
        jnp.int32, (rows, rows), 1
    )
    copies[0].wait()
    written = []
    for s in range(samples):
        for copy in copies[1 + 3 * s : 4 + 3 * s]:
            copy.wait()
        normed = layer_norm(activations[s].astype(jnp.float32))
        result = cond_scale[s].astype(jnp.float32) * normed + cond_shift[s].astype(jnp.float32)
        flags = jnp.where(diagonal, token_mask[s : s + 1, :].astype(jnp.float32), 0.0)
        valid = jnp.sum(flags, axis=1, keepdims=True) > 0.0
        shifted[s] = result.astype(jnp.bfloat16)
        sent[s] = jnp.where(valid, result, absent).astype(jnp.bfloat16)
        for t, (source, target) in enumerate(((sent, sent_hbm), (shifted, shifted_hbm))):
            written.append(pltpu.make_async_copy(source.at[s], target.at[s], sems_out.at[2 * s + t]))
            written[-1].start()
    core = lax.rem(lax.axis_index("row"), 2)
    half, breadth = packed.shape[0], query_weight.shape[1]
    for w, weight in enumerate((query_weight, key_weight)):
        copies[1 + 3 * samples + w].wait()
        whole = weight[...].astype(jnp.float32)
        packed[:, w * breadth : (w + 1) * breadth] = jnp.where(
            core == 0, whole[:half], whole[half:]
        ).astype(jnp.bfloat16)
    written.append(pltpu.make_async_copy(packed, packed_hbm, sems_out.at[2 * samples]))
    written[-1].start()
    copies[-1].wait()
    columns[...] = jnp.where(core == 0, output_weight[:, :breadth], output_weight[:, breadth:])
    written.append(pltpu.make_async_copy(columns, columns_hbm, sems_out.at[2 * samples + 1]))
    written[-1].start()
    for copy in written:
        copy.wait()


def bias_kernel(pair_hbm, value_hbm, weights_hbm, parcel, pair, value_weight, weights, collected, sems):
    rows, columns, channels = pair.shape
    heads = weights.shape[0]
    per, batches = 8, 2
    batch = rows // batches
    copies = [pltpu.make_async_copy(weights_hbm, weights, sems.at[batches])]
    for i in range(batches):
        here = pl.ds(i * batch, batch)
        copies.append(pltpu.make_async_copy(pair_hbm.at[here], pair.at[here], sems.at[i]))
    copies.append(pltpu.make_async_copy(value_hbm, value_weight, sems.at[batches + 1]))
    for copy in copies:
        copy.start()
    copies[0].wait()
    record = 2 * heads
    extended = jnp.concatenate(
        [weights[...], jnp.full((heads, channels), 1.0 / channels, jnp.bfloat16)], axis=0
    )
    square = (channels, channels)
    diagonal = lax.broadcasted_iota(jnp.int32, square, 0) == lax.broadcasted_iota(jnp.int32, square, 1)
    centring = (jnp.where(diagonal, 1.0, 0.0) - 1.0 / channels).astype(jnp.bfloat16)
    lane = lax.broadcasted_iota(jnp.int32, (1, rows), 1)
    squares = jnp.zeros((columns, rows), jnp.float32)
    for i in range(rows // per):
        if i * per % batch == 0:
            copies[1 + i * per // batch].wait()
        block = pair[i * per : (i + 1) * per].reshape(per * columns, channels)
        centred = jnp.dot(block, centring, preferred_element_type=jnp.float32)
        summed = jnp.sum(centred * centred, axis=1, keepdims=True)
        result = lax.dot_general(
            extended, block, (((1,), (1,)), ((), ())), preferred_element_type=jnp.float32
        )
        for r in range(per):
            row = i * per + r
            collected[row * record : (row + 1) * record, :] = result[:, r * columns : (r + 1) * columns]
            squares = jnp.where(lane == row, summed[r * columns : (r + 1) * columns], squares)
    core = lax.rem(lax.axis_index("row"), 2)
    half = columns // 2
    average = collected[pl.ds(heads, rows, stride=record), :].T
    inverse = lax.rsqrt(squares / channels + epsilon)
    for p in range(heads // 2):
        own, other = [], []
        for h in (2 * p, 2 * p + 1):
            summed = jnp.sum(weights[h : h + 1, :].astype(jnp.float32), axis=1, keepdims=True)
            turned = (collected[pl.ds(h, rows, stride=record), :].T - average * summed) * inverse
            low, up = turned[:half], turned[half:]
            own.append(jnp.where(core == 0, low, up))
            other.append(jnp.where(core == 0, up, low))
        at = p * half
        parcel[at : at + half, :] = jnp.concatenate(own, axis=1).astype(jnp.bfloat16)
        at += heads // 2 * half
        parcel[at : at + half, :] = jnp.concatenate(other[::-1], axis=1).astype(jnp.bfloat16)
    copies[-1].wait()
    depth, breadth = value_weight.shape
    whole = value_weight[...].astype(jnp.float32)
    kept = jnp.where(core == 0, whole[: depth // 2], whole[depth // 2 :]).astype(jnp.bfloat16)
    for t in range(breadth // columns):
        at = heads * half + t * (depth // 2)
        parcel[at : at + depth // 2, :] = kept[:, t * columns : (t + 1) * columns]


def spread_queries(heads, queries, spread):
    count, head_features = queries.shape
    width = head_features // heads
    reach = spread.shape[1]
    lane = lax.broadcasted_iota(jnp.int32, (1, reach), 1)
    turned = jnp.concatenate([queries[count // 2 :], queries[: count // 2]], axis=0)
    for h in range(heads):
        start, free = (0, reach - 1) if h < heads // 2 else (head_features - reach, 0)
        inside = ((lane >= h * width - start) & (lane < (h + 1) * width - start)).astype(jnp.bfloat16)
        extra = (lane == free).astype(jnp.bfloat16)
        own = (turned if h % 2 else queries)[:, start : start + reach]
        spread[h * count : (h + 1) * count, :] = own * inside + extra


def attend_keys(heads, tokens, keys, values, bias_of, spread):
    head_features = values.shape[0]
    width = head_features // heads
    count, reach = spread.shape[0] // heads, spread.shape[1]
    used = heads // 2 * width
    penalty = jnp.where(tokens[:, 0:1].astype(jnp.float32) > absent / 2, masked_score, 0.0)
    lane = lax.broadcasted_iota(jnp.int32, (1, reach), 1)
    scores = []
    for part in range(2):
        start = part * (head_features - reach)
        inside = lane < used if part == 0 else lane >= reach - used
        extended = jnp.where(inside, keys[:, start : start + reach], penalty).astype(jnp.bfloat16)
        scores.append(
            lax.dot_general(
                extended,
                spread[part * heads // 2 * count : (part + 1) * heads // 2 * count, :],
                (((1,), (1,)), ((), ())),
                preferred_element_type=jnp.float32,
            )
        )
    sums, highs, totals = [], [], []
    for h in range(heads):
        at = h % (heads // 2) * count
        score = scores[h // (heads // 2)][:, at : at + count] * (log2_e / math.sqrt(width))
        score = score + bias_of(h) * log2_e
        high = jnp.max(score, axis=0, keepdims=True)
        probs = jnp.exp2(score - high)
        totals.append(jnp.sum(probs, axis=0, keepdims=True))
        highs.append(high)
        sums.append(
            jnp.dot(
                values[h * width : (h + 1) * width],
                probs.astype(jnp.bfloat16),
                preferred_element_type=jnp.float32,
            )
        )
    return sums, highs, totals


def bias_picker(parcel, swapped, steps, first, rows):
    chip = lax.axis_index("row") // 2
    place = lax.axis_index("noise")
    left = lax.broadcasted_iota(jnp.int32, (1, 2 * rows), 1) < rows

    here = jnp.where(chip % 2 == 1, (chip + 1) // 2, lax.rem(steps - chip // 2, steps))

    def pick(b, h):
        position = lax.rem(here - (first + b) + steps, steps)
        outward = (position > 0) & (position <= steps // 2)
        origin = jnp.where(outward, 2 * position - 1, 2 * lax.rem(steps - position, steps))
        part = origin ^ place
        at = slice(h // 2 * rows, (h // 2 + 1) * rows)
        pairs = parcel[part, at].astype(jnp.float32), swapped[part, at].astype(jnp.float32)
        return jnp.where(left, pairs[h % 2], pairs[1 - h % 2])

    return pick


def early_kernel(steps, heads, weights_mine, weights_other, query_bias, shifted, shifted_other, parcel, swapped, swapped_value, *refs):
    blocks = refs[: steps - 1]
    partial, queries, key_weight, value_weight, full, full_value, spread = refs[steps - 1 :]
    samples, rows, features = shifted.shape
    noise_size, half, _ = weights_mine.shape
    breadth = key_weight.shape[1]
    width = breadth // heads
    core = lax.rem(lax.axis_index("row"), 2)
    place = lax.axis_index("noise")
    below = parcel.shape[1] - breadth // 128 * half
    for part, value, skipped, of_core in (
        (weights_mine, parcel, below, core),
        (weights_other, swapped_value, 0, 1 - core),
    ):
        for k in range(noise_size):
            start = ((place ^ k) * 2 + of_core) * half
            down = pl.ds(pl.multiple_of(start, math.gcd(half, 32)), half)
            full[down, :] = part[k, 0:half].astype(full.dtype)
            for t in range(breadth // 128):
                at = skipped + t * half
                full_value[down, t * 128 : (t + 1) * 128] = value[k, at : at + half].astype(full.dtype)
    key_weight[...] = full[:, breadth : 2 * breadth].astype(jnp.bfloat16)
    value_weight[...] = full_value[...].astype(jnp.float32).T.astype(jnp.bfloat16)
    for side, tokens in enumerate((shifted, shifted_other)):
        result = jnp.dot(
            tokens[...].reshape(samples * rows, features),
            full[:, 0:breadth].astype(jnp.bfloat16),
            preferred_element_type=jnp.float32,
        ) + query_bias[...].astype(jnp.float32)
        queries[:, side * rows : (side + 1) * rows] = result.astype(jnp.bfloat16).reshape(
            samples, rows, breadth
        )
    pick = bias_picker(parcel, swapped, steps, 0, rows)
    for s in range(samples):
        tokens = jnp.concatenate([block[s] for block in blocks], axis=0)
        keys = jnp.dot(tokens, key_weight[...], preferred_element_type=jnp.float32)
        values = lax.dot_general(
            value_weight[...], tokens, (((1,), (1,)), ((), ())), preferred_element_type=jnp.float32
        ).astype(jnp.bfloat16)
        spread_queries(heads, queries[s], spread)
        sums, highs, totals = attend_keys(
            heads,
            tokens,
            keys,
            values,
            lambda h: jnp.concatenate([pick(b, h) for b in range(steps - 1)], axis=0),
            spread,
        )
        for h in range(heads):
            partial[s, h * width : (h + 1) * width] = sums[h]
            partial[s, breadth + h : breadth + h + 1] = highs[h]
            partial[s, breadth + heads + h : breadth + heads + h + 1] = totals[h]


def late_kernel(steps, heads, first, partial, queries, key_weight, value_weight, parcel, swapped, block, keep, give, merged, spread):
    samples = merged.shape[0]
    rows = block.shape[1]
    breadth = key_weight.shape[1]
    width = breadth // heads
    pick = bias_picker(parcel, swapped, steps, steps - 1, rows)
    tokens = block[first : first + samples].reshape(samples * rows, block.shape[2])
    keys = jnp.dot(tokens, key_weight[...], preferred_element_type=jnp.float32)
    values = lax.dot_general(
        value_weight[...], tokens, (((1,), (1,)), ((), ())), preferred_element_type=jnp.float32
    ).astype(jnp.bfloat16)
    for s in range(samples):
        here = slice(s * rows, (s + 1) * rows)
        spread_queries(heads, queries[first + s], spread)
        sums, highs, totals = attend_keys(
            heads, tokens[here], keys[here], values[:, here], lambda h: pick(0, h), spread
        )
        before = partial.at[first + s]
        for h in range(heads):
            at_high = slice(breadth + h, breadth + h + 1)
            at_total = slice(breadth + heads + h, breadth + heads + h + 1)
            high = jnp.maximum(before[at_high], highs[h])
            old, new = jnp.exp2(before[at_high] - high), jnp.exp2(highs[h] - high)
            across = slice(h * width, (h + 1) * width)
            merged[s, across] = before[across] * old + sums[h] * new
            merged[s, at_high] = high
            merged[s, at_total] = before[at_total] * old + totals[h] * new
    half = merged.shape[2] // 2
    left = lax.broadcasted_iota(jnp.int32, (1, 2 * half), 1) < half
    row = lax.broadcasted_iota(jnp.int32, (merged.shape[1], 1), 0)
    head = jnp.where(row < breadth, row // width, (row - breadth) % heads)
    even = head % 2 == 0
    for pair in range(samples // 2):
        a, b = merged[2 * pair], merged[2 * pair + 1]
        lefts = jnp.where(left, a, pltpu.roll(b, half, 1))
        rights = jnp.where(left, pltpu.roll(a, half, 1), b)
        keep[pair] = jnp.where(even, lefts, rights)
        give[pair] = jnp.where(even, rights, lefts)


def finish_kernel(heads, first, output_mine, output_other, activations, output_gate, keep, got, *refs):
    updated_hbm, updated, output_weight, sems = refs[-4:]
    noise_size, part_rows, part_columns = output_mine.shape
    breadth = output_weight.shape[0]
    width = breadth // heads
    samples, rows, _ = updated.shape
    core = lax.rem(lax.axis_index("row"), 2)
    place = lax.axis_index("noise")
    for k in range(noise_size):
        down = pl.ds(pl.multiple_of((place ^ k) * part_rows, math.gcd(part_rows, 32)), part_rows)
        for part, of_core in ((output_mine, core), (output_other, 1 - core)):
            along = pl.ds(pl.multiple_of(of_core * part_columns, 128), part_columns)
            output_weight[down, along] = part[k].astype(output_weight.dtype)
    writes = []
    for pair in range(samples // 2):
        own, other = keep.at[pair], got.at[pair]
        parts = []
        for h in range(heads):
            at_high = slice(breadth + h, breadth + h + 1)
            at_total = slice(breadth + heads + h, breadth + heads + h + 1)
            across = slice(h * width, (h + 1) * width)
            high = jnp.maximum(own[at_high], other[at_high])
            mine, theirs = jnp.exp2(own[at_high] - high), jnp.exp2(other[at_high] - high)
            total = own[at_total] * mine + other[at_total] * theirs
            parts.append((own[across] * mine + other[across] * theirs) / total)
        attended = jnp.concatenate(parts, axis=0).T.astype(jnp.bfloat16)
        projected = jnp.dot(
            attended, output_weight[...].astype(jnp.bfloat16), preferred_element_type=jnp.float32
        )
        for side in range(2):
            s = 2 * pair + side
            gate = jax.nn.sigmoid(output_gate[first + s].astype(jnp.float32))
            updated[s] = (
                activations[first + s].astype(jnp.float32)
                + gate * projected[side * rows : (side + 1) * rows]
            ).astype(jnp.bfloat16)
            writes.append(pltpu.make_async_copy(updated.at[s], updated_hbm.at[first + s], sems.at[s]))
            writes[-1].start()
    for write in writes:
        write.wait()


def swap_cores(array):
    return lax.ppermute(array, "row", [(i, i ^ 1) for i in range(lax.axis_size("row"))])


def ring_chip(position, steps):
    return 2 * position - 1 if 0 < position <= steps // 2 else 2 * ((steps - position) % steps)


def next_chip(array):
    steps = lax.axis_size("row") // 2
    order = [ring_chip(p, steps) for p in range(steps)]
    pairs = [
        (2 * order[p] + c, 2 * order[(p + 1) % steps] + c) for p in range(steps) for c in range(2)
    ]
    return lax.ppermute(array, "row", pairs)


def from_noise(array, k):
    if k == 0:
        return array
    return lax.ppermute(array, "noise", [(i, i ^ k) for i in range(lax.axis_size("noise"))])


def body(
    activations,
    cond_scale,
    cond_shift,
    output_gate,
    pair_repr,
    bias_weight,
    query_weight,
    query_bias,
    key_weight,
    value_weight,
    output_weight,
    token_mask,
):
    samples, rows, features = activations.shape
    heads = bias_weight.shape[1]
    head_features = query_weight.shape[1]
    noise_size = lax.axis_size("noise")
    steps = lax.axis_size("row") // 2
    assert noise_size == steps and pair_repr.shape[1] == 2 * rows
    bf16, f32 = jnp.bfloat16, jnp.float32
    params = pltpu.CompilerParams(vmem_limit_bytes=vmem_bytes)
    struct = jax.ShapeDtypeStruct
    after = lax.optimization_barrier
    half = query_weight.shape[0] // 2

    in_hbm = pl.BlockSpec(memory_space=pltpu.HBM)
    packed_shape, columns_shape = (half, 2 * head_features), (output_weight.shape[0], features // 2)
    shifted, sent, packed, output_columns = pl.pallas_call(
        shift_kernel,
        in_specs=[in_hbm] * 7,
        out_specs=[in_hbm] * 4,
        out_shape=[struct(activations.shape, bf16)] * 2
        + [struct(packed_shape, bf16), struct(columns_shape, bf16)],
        scratch_shapes=[pltpu.VMEM(activations.shape, bf16)] * 2
        + [pltpu.VMEM(packed_shape, bf16), pltpu.VMEM(columns_shape, bf16)]
        + [pltpu.VMEM(activations.shape, bf16)] * 3
        + [pltpu.VMEM(token_mask.shape, jnp.int32)]
        + [pltpu.VMEM(query_weight.shape, bf16)] * 2
        + [pltpu.VMEM(output_weight.shape, bf16)]
        + [pltpu.SemaphoreType.DMA((3 * samples + 4,)), pltpu.SemaphoreType.DMA((2 * samples + 2,))],
        compiler_params=pltpu.CompilerParams(vmem_limit_bytes=wide_bytes),
        name="shift",
    )(activations, cond_scale, cond_shift, token_mask, query_weight, key_weight, output_weight)

    ring = [sent, next_chip(sent)]
    weights = [packed] + [from_noise(packed, k) for k in range(noise_size - 1, 0, -1)][::-1]
    head_weights, _ = after((bias_weight.T, packed))
    columns = pair_repr.shape[1]
    tile_rows = heads * rows
    parcel = pl.pallas_call(
        bias_kernel,
        in_specs=[in_hbm] * 3,
        out_shape=struct((tile_rows + 3 * half, columns), bf16),
        scratch_shapes=[
            pltpu.VMEM(pair_repr.shape, bf16),
            pltpu.VMEM(value_weight.shape, bf16),
            pltpu.VMEM(head_weights.shape, bf16),
            pltpu.VMEM((rows * 2 * heads, columns), f32),
            pltpu.SemaphoreType.DMA((4,)),
        ],
        compiler_params=pltpu.CompilerParams(vmem_limit_bytes=wide_bytes),
        name="bias",
    )(pair_repr, value_weight, head_weights)
    shifted_other = swap_cores(shifted)
    ring[1], weights, parcel, shifted_other = after((ring[1], weights, parcel, shifted_other))
    output_next = from_noise(output_columns, 1)
    ring.append(next_chip(ring[1]))
    output_mine = jnp.stack([output_columns, output_next])
    weights_mine = jnp.stack(weights)
    weights_other = swap_cores(weights_mine)
    parcel, _ = after((parcel, weights_mine))
    parcels = [from_noise(parcel, k) for k in range(noise_size)]

    for _ in range(steps - 3):
        ring.append(next_chip(ring[-1]))
    last = ring.pop()
    parcel_mine = jnp.stack(parcels)
    swapped = swap_cores(parcel_mine[:, tile_rows // 2 : tile_rows])
    swapped_value = swap_cores(parcel_mine[:, tile_rows:])
    for k in range(1, noise_size.bit_length() - 1):
        output_mine = jnp.concatenate([output_mine, from_noise(output_mine, 2**k)], axis=0)
    output_other = swap_cores(output_mine)

    bias_row = query_bias.reshape(1, head_features)
    record = head_features + 2 * heads
    full_type = f32 if half % 16 else bf16
    output_type = f32 if output_weight.shape[0] % 16 else bf16
    spread = pltpu.VMEM((heads * 2 * rows, 256), bf16)
    partial, queries, key_full, value_full = pl.pallas_call(
        functools.partial(early_kernel, steps, heads),
        out_shape=[
            struct((samples, record, 2 * rows), f32),
            struct((samples, 2 * rows, head_features), bf16),
            struct((features, head_features), bf16),
            struct((head_features, features), bf16),
        ],
        scratch_shapes=[
            pltpu.VMEM((features, 2 * head_features), full_type),
            pltpu.VMEM((features, head_features), full_type),
            spread,
        ],
        compiler_params=params,
        name="early",
    )(weights_mine, weights_other, bias_row, shifted, shifted_other, parcel_mine, swapped, swapped_value, *ring)
    keep, got = [], []
    chunks = 2
    each = samples // chunks
    for c in range(chunks):
        kept, give = pl.pallas_call(
            functools.partial(late_kernel, steps, heads, c * each),
            out_shape=[struct((each // 2, record, 2 * rows), f32)] * 2,
            scratch_shapes=[pltpu.VMEM((each, record, 2 * rows), f32), spread],
            compiler_params=params,
            name="late",
        )(partial, queries, key_full, value_full, parcel_mine, swapped, last)
        keep.append(kept)
        got.append(swap_cores(give))
    updated = []
    for c in range(chunks):
        operands = [output_mine, output_other, activations, output_gate, keep[c], got[c], *updated]
        updated = [
            pl.pallas_call(
                functools.partial(finish_kernel, heads, c * each),
                in_specs=[pl.BlockSpec(memory_space=pltpu.VMEM)] * 6 + [in_hbm] * len(updated),
                out_specs=in_hbm,
                out_shape=struct(activations.shape, bf16),
                input_output_aliases={6: 0} if updated else {},
                scratch_shapes=[
                    pltpu.VMEM((each, rows, features), bf16),
                    pltpu.VMEM((head_features, features), output_type),
                    pltpu.SemaphoreType.DMA((each,)),
                ],
                compiler_params=params,
                name="finish",
            )(*operands)
        ]
    return updated[0]


def solution(mesh):
    return jax.shard_map(
        body,
        mesh=mesh,
        in_specs=(
            P("noise", "row", None),
            P("noise", "row", None),
            P("noise", "row", None),
            P("noise", "row", None),
            P("row", "noise", None),
            P(),
            P("noise", None),
            P(),
            P("noise", None),
            P("noise", None),
            P("noise", None),
            P("noise", "row"),
        ),
        out_specs=P("noise", "row", None),
        check_vma=False,
    )
```

```python
import functools
import math

import jax
import jax.numpy as jnp
from jax import lax
from jax.experimental import pallas as pl
from jax.experimental.pallas import tpu as pltpu
from jax.sharding import PartitionSpec as P

epsilon = 1e-05
masked_score = -1e30
absent = 32768.0
log2_e = math.log2(math.e)
vmem_bytes = 40 * 2**20
wide_bytes = 60 * 2**20


def layer_norm(tensor):
    average = jnp.mean(tensor, axis=-1, keepdims=True)
    centred = tensor - average
    variance = jnp.mean(centred * centred, axis=-1, keepdims=True)
    return centred * lax.rsqrt(variance + epsilon)


def shift_kernel(
    activations_hbm,
    scale_hbm,
    shift_hbm,
    mask_hbm,
    query_hbm,
    key_hbm,
    shifted_hbm,
    sent_hbm,
    packed_hbm,
    shifted,
    sent,
    packed,
    activations,
    cond_scale,
    cond_shift,
    token_mask,
    query_weight,
    key_weight,
    sems,
    sems_out,
):
    samples, rows, features = activations.shape
    copies = [pltpu.make_async_copy(mask_hbm, token_mask, sems.at[0])]
    for s in range(samples):
        for t, (source, target) in enumerate(
            ((activations_hbm, activations), (scale_hbm, cond_scale), (shift_hbm, cond_shift))
        ):
            copies.append(pltpu.make_async_copy(source.at[s], target.at[s], sems.at[1 + 3 * s + t]))
    copies.append(pltpu.make_async_copy(query_hbm, query_weight, sems.at[1 + 3 * samples]))
    copies.append(pltpu.make_async_copy(key_hbm, key_weight, sems.at[2 + 3 * samples]))
    for copy in copies:
        copy.start()
    diagonal = lax.broadcasted_iota(jnp.int32, (rows, rows), 0) == lax.broadcasted_iota(
        jnp.int32, (rows, rows), 1
    )
    copies[0].wait()
    written = []
    for s in range(samples):
        for copy in copies[1 + 3 * s : 4 + 3 * s]:
            copy.wait()
        normed = layer_norm(activations[s].astype(jnp.float32))
        result = cond_scale[s].astype(jnp.float32) * normed + cond_shift[s].astype(jnp.float32)
        flags = jnp.where(diagonal, token_mask[s : s + 1, :].astype(jnp.float32), 0.0)
        valid = jnp.sum(flags, axis=1, keepdims=True) > 0.0
        shifted[s] = result.astype(jnp.bfloat16)
        sent[s] = jnp.where(valid, result, absent).astype(jnp.bfloat16)
        for t, (source, target) in enumerate(((sent, sent_hbm), (shifted, shifted_hbm))):
            written.append(pltpu.make_async_copy(source.at[s], target.at[s], sems_out.at[2 * s + t]))
            written[-1].start()
    core = lax.rem(lax.axis_index("row"), 2)
    half, breadth = packed.shape[0], query_weight.shape[1]
    for w, weight in enumerate((query_weight, key_weight)):
        copies[1 + 3 * samples + w].wait()
        whole = weight[...].astype(jnp.float32)
        packed[:, w * breadth : (w + 1) * breadth] = jnp.where(
            core == 0, whole[:half], whole[half:]
        ).astype(jnp.bfloat16)
    written.append(pltpu.make_async_copy(packed, packed_hbm, sems_out.at[2 * samples]))
    written[-1].start()
    for copy in written:
        copy.wait()


def bias_kernel(
    pair_hbm, value_hbm, output_hbm, weights_hbm, parcel, pair, value_weight, output_weight, weights, collected, sems
):
    rows, columns, channels = pair.shape
    heads = weights.shape[0]
    per, batches = 8, 2
    batch = rows // batches
    copies = [pltpu.make_async_copy(weights_hbm, weights, sems.at[batches])]
    for i in range(batches):
        here = pl.ds(i * batch, batch)
        copies.append(pltpu.make_async_copy(pair_hbm.at[here], pair.at[here], sems.at[i]))
    copies.append(pltpu.make_async_copy(value_hbm, value_weight, sems.at[batches + 1]))
    copies.append(pltpu.make_async_copy(output_hbm, output_weight, sems.at[batches + 2]))
    for copy in copies:
        copy.start()
    copies[0].wait()
    record = 2 * heads
    extended = jnp.concatenate(
        [weights[...], jnp.full((heads, channels), 1.0 / channels, jnp.bfloat16)], axis=0
    )
    square = (channels, channels)
    diagonal = lax.broadcasted_iota(jnp.int32, square, 0) == lax.broadcasted_iota(jnp.int32, square, 1)
    centring = (jnp.where(diagonal, 1.0, 0.0) - 1.0 / channels).astype(jnp.bfloat16)
    lane = lax.broadcasted_iota(jnp.int32, (1, rows), 1)
    squares = jnp.zeros((columns, rows), jnp.float32)
    for i in range(rows // per):
        if i * per % batch == 0:
            copies[1 + i * per // batch].wait()
        block = pair[i * per : (i + 1) * per].reshape(per * columns, channels)
        centred = jnp.dot(block, centring, preferred_element_type=jnp.float32)
        summed = jnp.sum(centred * centred, axis=1, keepdims=True)
        result = lax.dot_general(
            extended, block, (((1,), (1,)), ((), ())), preferred_element_type=jnp.float32
        )
        for r in range(per):
            row = i * per + r
            collected[row * record : (row + 1) * record, :] = result[:, r * columns : (r + 1) * columns]
            squares = jnp.where(lane == row, summed[r * columns : (r + 1) * columns], squares)
    core = lax.rem(lax.axis_index("row"), 2)
    half = columns // 2
    average = collected[pl.ds(heads, rows, stride=record), :].T
    inverse = lax.rsqrt(squares / channels + epsilon)
    for p in range(heads // 2):
        own, other = [], []
        for h in (2 * p, 2 * p + 1):
            summed = jnp.sum(weights[h : h + 1, :].astype(jnp.float32), axis=1, keepdims=True)
            turned = (collected[pl.ds(h, rows, stride=record), :].T - average * summed) * inverse
            low, up = turned[:half], turned[half:]
            own.append(jnp.where(core == 0, low, up))
            other.append(jnp.where(core == 0, up, low))
        at = p * half
        parcel[at : at + half, :] = jnp.concatenate(own, axis=1).astype(jnp.bfloat16)
        at += heads // 2 * half
        parcel[at : at + half, :] = jnp.concatenate(other[::-1], axis=1).astype(jnp.bfloat16)
    copies[-2].wait()
    copies[-1].wait()
    depth, breadth = value_weight.shape
    whole = value_weight[...].astype(jnp.float32)
    kept = jnp.where(core == 0, whole[: depth // 2], whole[depth // 2 :]).astype(jnp.bfloat16)
    beside = jnp.where(core == 0, output_weight[:, :breadth], output_weight[:, breadth:])
    at = heads * half
    for part in (kept, beside):
        for t in range(breadth // columns):
            parcel[at : at + depth // 2, :] = part[:, t * columns : (t + 1) * columns]
            at += depth // 2


def sort_kernel(*refs):
    stacks = refs[-4:]
    for k, parcel in enumerate(refs[:-4]):
        at = 0
        for stack in stacks:
            stack[k] = parcel[at : at + stack.shape[1]]
            at += stack.shape[1]


def spread_queries(heads, queries, spread):
    count, head_features = queries.shape
    width = head_features // heads
    reach = spread.shape[1]
    lane = lax.broadcasted_iota(jnp.int32, (1, reach), 1)
    turned = jnp.concatenate([queries[count // 2 :], queries[: count // 2]], axis=0)
    for h in range(heads):
        start, free = (0, reach - 1) if h < heads // 2 else (head_features - reach, 0)
        inside = ((lane >= h * width - start) & (lane < (h + 1) * width - start)).astype(jnp.bfloat16)
        extra = (lane == free).astype(jnp.bfloat16)
        own = (turned if h % 2 else queries)[:, start : start + reach]
        spread[h * count : (h + 1) * count, :] = own * inside + extra


def attend_keys(heads, tokens, keys, values, bias_of, spread):
    head_features = values.shape[0]
    width = head_features // heads
    count, reach = spread.shape[0] // heads, spread.shape[1]
    used = heads // 2 * width
    penalty = jnp.where(tokens[:, 0:1].astype(jnp.float32) > absent / 2, masked_score, 0.0)
    lane = lax.broadcasted_iota(jnp.int32, (1, reach), 1)
    scores = []
    for part in range(2):
        start = part * (head_features - reach)
        inside = lane < used if part == 0 else lane >= reach - used
        extended = jnp.where(inside, keys[:, start : start + reach], penalty).astype(jnp.bfloat16)
        scores.append(
            lax.dot_general(
                extended,
                spread[part * heads // 2 * count : (part + 1) * heads // 2 * count, :],
                (((1,), (1,)), ((), ())),
                preferred_element_type=jnp.float32,
            )
        )
    sums, highs, totals = [], [], []
    for h in range(heads):
        at = h % (heads // 2) * count
        score = scores[h // (heads // 2)][:, at : at + count] * (log2_e / math.sqrt(width))
        score = score + bias_of(h) * log2_e
        high = jnp.max(score, axis=0, keepdims=True)
        probs = jnp.exp2(score - high)
        totals.append(jnp.sum(probs, axis=0, keepdims=True))
        highs.append(high)
        sums.append(
            jnp.dot(
                values[h * width : (h + 1) * width],
                probs.astype(jnp.bfloat16),
                preferred_element_type=jnp.float32,
            )
        )
    return sums, highs, totals


def bias_picker(parcel, swapped, steps, first, rows):
    chip = lax.axis_index("row") // 2
    place = lax.axis_index("noise")
    left = lax.broadcasted_iota(jnp.int32, (1, 2 * rows), 1) < rows

    here = jnp.where(chip % 2 == 1, (chip + 1) // 2, lax.rem(steps - chip // 2, steps))

    def pick(b, h):
        position = lax.rem(here - (first + b) + steps, steps)
        outward = (position > 0) & (position <= steps // 2)
        origin = jnp.where(outward, 2 * position - 1, 2 * lax.rem(steps - position, steps))
        part = origin ^ place
        at = slice(h // 2 * rows, (h // 2 + 1) * rows)
        pairs = parcel[part, at].astype(jnp.float32), swapped[part, at].astype(jnp.float32)
        return jnp.where(left, pairs[h % 2], pairs[1 - h % 2])

    return pick


def early_kernel(steps, heads, weights_mine, weights_other, query_bias, shifted, shifted_other, own_bias, swapped, own_value, swapped_value, *refs):
    blocks = refs[: steps - 1]
    partial, queries, key_weight, value_weight, full, full_value, spread = refs[steps - 1 :]
    samples, rows, features = shifted.shape
    noise_size, half, _ = weights_mine.shape
    breadth = key_weight.shape[1]
    width = breadth // heads
    core = lax.rem(lax.axis_index("row"), 2)
    place = lax.axis_index("noise")
    for part, value, of_core in ((weights_mine, own_value, core), (weights_other, swapped_value, 1 - core)):
        for k in range(noise_size):
            start = ((place ^ k) * 2 + of_core) * half
            down = pl.ds(pl.multiple_of(start, math.gcd(half, 32)), half)
            full[down, :] = part[k].astype(full.dtype)
            for t in range(breadth // 128):
                at = t * half
                full_value[down, t * 128 : (t + 1) * 128] = value[k, at : at + half].astype(full.dtype)
    key_weight[...] = full[:, breadth : 2 * breadth].astype(jnp.bfloat16)
    value_weight[...] = full_value[...].astype(jnp.float32).T.astype(jnp.bfloat16)
    for side, tokens in enumerate((shifted, shifted_other)):
        result = jnp.dot(
            tokens[...].reshape(samples * rows, features),
            full[:, 0:breadth].astype(jnp.bfloat16),
            preferred_element_type=jnp.float32,
        ) + query_bias[...].astype(jnp.float32)
        queries[:, side * rows : (side + 1) * rows] = result.astype(jnp.bfloat16).reshape(
            samples, rows, breadth
        )
    pick = bias_picker(own_bias, swapped, steps, 0, rows)
    for s in range(samples):
        tokens = jnp.concatenate([block[s] for block in blocks], axis=0)
        keys = jnp.dot(tokens, key_weight[...], preferred_element_type=jnp.float32)
        values = lax.dot_general(
            value_weight[...], tokens, (((1,), (1,)), ((), ())), preferred_element_type=jnp.float32
        ).astype(jnp.bfloat16)
        spread_queries(heads, queries[s], spread)
        sums, highs, totals = attend_keys(
            heads,
            tokens,
            keys,
            values,
            lambda h: jnp.concatenate([pick(b, h) for b in range(steps - 1)], axis=0),
            spread,
        )
        for h in range(heads):
            partial[s, h * width : (h + 1) * width] = sums[h]
            partial[s, breadth + h : breadth + h + 1] = highs[h]
            partial[s, breadth + heads + h : breadth + heads + h + 1] = totals[h]


def late_kernel(steps, heads, first, partial, queries, key_weight, value_weight, own_bias, swapped, block, keep, give, merged, spread):
    samples = merged.shape[0]
    rows = block.shape[1]
    breadth = key_weight.shape[1]
    width = breadth // heads
    pick = bias_picker(own_bias, swapped, steps, steps - 1, rows)
    tokens = block[first : first + samples].reshape(samples * rows, block.shape[2])
    keys = jnp.dot(tokens, key_weight[...], preferred_element_type=jnp.float32)
    values = lax.dot_general(
        value_weight[...], tokens, (((1,), (1,)), ((), ())), preferred_element_type=jnp.float32
    ).astype(jnp.bfloat16)
    for s in range(samples):
        here = slice(s * rows, (s + 1) * rows)
        spread_queries(heads, queries[first + s], spread)
        sums, highs, totals = attend_keys(
            heads, tokens[here], keys[here], values[:, here], lambda h: pick(0, h), spread
        )
        before = partial.at[first + s]
        for h in range(heads):
            at_high = slice(breadth + h, breadth + h + 1)
            at_total = slice(breadth + heads + h, breadth + heads + h + 1)
            high = jnp.maximum(before[at_high], highs[h])
            old, new = jnp.exp2(before[at_high] - high), jnp.exp2(highs[h] - high)
            across = slice(h * width, (h + 1) * width)
            merged[s, across] = before[across] * old + sums[h] * new
            merged[s, at_high] = high
            merged[s, at_total] = before[at_total] * old + totals[h] * new
    half = merged.shape[2] // 2
    left = lax.broadcasted_iota(jnp.int32, (1, 2 * half), 1) < half
    row = lax.broadcasted_iota(jnp.int32, (merged.shape[1], 1), 0)
    head = jnp.where(row < breadth, row // width, (row - breadth) % heads)
    even = head % 2 == 0
    for pair in range(samples // 2):
        a, b = merged[2 * pair], merged[2 * pair + 1]
        lefts = jnp.where(left, a, pltpu.roll(b, half, 1))
        rights = jnp.where(left, pltpu.roll(a, half, 1), b)
        keep[pair] = jnp.where(even, lefts, rights)
        give[pair] = jnp.where(even, rights, lefts)


def finish_kernel(heads, first, own_output, swapped_output, activations, output_gate, keep, got, *refs):
    updated_hbm, updated, output_weight, sems = refs[-4:]
    noise_size, piece_rows, tile = swapped_output.shape
    breadth = output_weight.shape[0]
    tiles = breadth // tile
    part_rows = piece_rows // tiles
    width = breadth // heads
    samples, rows, _ = updated.shape
    core = lax.rem(lax.axis_index("row"), 2)
    place = lax.axis_index("noise")
    for k in range(noise_size):
        down = pl.ds(pl.multiple_of((place ^ k) * part_rows, math.gcd(part_rows, 32)), part_rows)
        for part, of_core in ((own_output, core), (swapped_output, 1 - core)):
            for t in range(tiles):
                along = pl.ds(pl.multiple_of((of_core * tiles + t) * tile, tile), tile)
                at = t * part_rows
                output_weight[down, along] = part[k, at : at + part_rows].astype(output_weight.dtype)
    writes = []
    for pair in range(samples // 2):
        own, other = keep.at[pair], got.at[pair]
        parts = []
        for h in range(heads):
            at_high = slice(breadth + h, breadth + h + 1)
            at_total = slice(breadth + heads + h, breadth + heads + h + 1)
            across = slice(h * width, (h + 1) * width)
            high = jnp.maximum(own[at_high], other[at_high])
            mine, theirs = jnp.exp2(own[at_high] - high), jnp.exp2(other[at_high] - high)
            total = own[at_total] * mine + other[at_total] * theirs
            parts.append((own[across] * mine + other[across] * theirs) / total)
        attended = jnp.concatenate(parts, axis=0).T.astype(jnp.bfloat16)
        projected = jnp.dot(
            attended, output_weight[...].astype(jnp.bfloat16), preferred_element_type=jnp.float32
        )
        for side in range(2):
            s = 2 * pair + side
            gate = jax.nn.sigmoid(output_gate[first + s].astype(jnp.float32))
            updated[s] = (
                activations[first + s].astype(jnp.float32)
                + gate * projected[side * rows : (side + 1) * rows]
            ).astype(jnp.bfloat16)
            writes.append(pltpu.make_async_copy(updated.at[s], updated_hbm.at[first + s], sems.at[s]))
            writes[-1].start()
    for write in writes:
        write.wait()


def swap_cores(array):
    return lax.ppermute(array, "row", [(i, i ^ 1) for i in range(lax.axis_size("row"))])


def ring_chip(position, steps):
    return 2 * position - 1 if 0 < position <= steps // 2 else 2 * ((steps - position) % steps)


def next_chip(array):
    steps = lax.axis_size("row") // 2
    order = [ring_chip(p, steps) for p in range(steps)]
    pairs = [
        (2 * order[p] + c, 2 * order[(p + 1) % steps] + c) for p in range(steps) for c in range(2)
    ]
    return lax.ppermute(array, "row", pairs)


def from_noise(array, k):
    if k == 0:
        return array
    return lax.ppermute(array, "noise", [(i, i ^ k) for i in range(lax.axis_size("noise"))])


def body(
    activations,
    cond_scale,
    cond_shift,
    output_gate,
    pair_repr,
    bias_weight,
    query_weight,
    query_bias,
    key_weight,
    value_weight,
    output_weight,
    token_mask,
):
    samples, rows, features = activations.shape
    heads = bias_weight.shape[1]
    head_features = query_weight.shape[1]
    noise_size = lax.axis_size("noise")
    steps = lax.axis_size("row") // 2
    assert noise_size == steps and pair_repr.shape[1] == 2 * rows
    bf16, f32 = jnp.bfloat16, jnp.float32
    params = pltpu.CompilerParams(vmem_limit_bytes=vmem_bytes)
    struct = jax.ShapeDtypeStruct
    after = lax.optimization_barrier
    half = query_weight.shape[0] // 2

    in_hbm = pl.BlockSpec(memory_space=pltpu.HBM)
    packed_shape = (half, 2 * head_features)
    shifted, sent, packed = pl.pallas_call(
        shift_kernel,
        in_specs=[in_hbm] * 6,
        out_specs=[in_hbm] * 3,
        out_shape=[struct(activations.shape, bf16)] * 2 + [struct(packed_shape, bf16)],
        scratch_shapes=[pltpu.VMEM(activations.shape, bf16)] * 2
        + [pltpu.VMEM(packed_shape, bf16)]
        + [pltpu.VMEM(activations.shape, bf16)] * 3
        + [pltpu.VMEM(token_mask.shape, jnp.int32)]
        + [pltpu.VMEM(query_weight.shape, bf16)] * 2
        + [pltpu.SemaphoreType.DMA((3 * samples + 3,)), pltpu.SemaphoreType.DMA((2 * samples + 1,))],
        compiler_params=pltpu.CompilerParams(vmem_limit_bytes=wide_bytes),
        name="shift",
    )(activations, cond_scale, cond_shift, token_mask, query_weight, key_weight)

    ring = [sent, next_chip(sent)]
    weights = [packed] + [from_noise(packed, k) for k in range(noise_size - 1, 0, -1)][::-1]
    head_weights, _ = after((bias_weight.T, packed))
    columns = pair_repr.shape[1]
    tile_rows, piece_rows = heads * rows, head_features // columns * half
    assert output_weight.shape == (half, 2 * head_features)
    parcel = pl.pallas_call(
        bias_kernel,
        in_specs=[in_hbm] * 4,
        out_shape=struct((tile_rows + 2 * piece_rows, columns), bf16),
        scratch_shapes=[
            pltpu.VMEM(pair_repr.shape, bf16),
            pltpu.VMEM(value_weight.shape, bf16),
            pltpu.VMEM(output_weight.shape, bf16),
            pltpu.VMEM(head_weights.shape, bf16),
            pltpu.VMEM((rows * 2 * heads, columns), f32),
            pltpu.SemaphoreType.DMA((5,)),
        ],
        compiler_params=pltpu.CompilerParams(vmem_limit_bytes=wide_bytes),
        name="bias",
    )(pair_repr, value_weight, output_weight, head_weights)
    shifted_other = swap_cores(shifted)
    ring[1], weights, parcel, shifted_other = after((ring[1], weights, parcel, shifted_other))
    ring.append(next_chip(ring[1]))
    weights_mine = jnp.stack(weights)
    weights_other = swap_cores(weights_mine)
    parcels = [from_noise(parcel, k) for k in range(noise_size)]

    for _ in range(steps - 3):
        ring.append(next_chip(ring[-1]))
    last = ring.pop()
    tile_shape, piece_shape = (noise_size, tile_rows // 2, columns), (noise_size, piece_rows, columns)
    own_bias, other_bias, own_value, own_output = pl.pallas_call(
        sort_kernel,
        out_shape=[struct(shape, bf16) for shape in (tile_shape, tile_shape, piece_shape, piece_shape)],
        compiler_params=params,
        name="sort",
    )(*parcels)
    swapped = swap_cores(other_bias)
    swapped_value = swap_cores(own_value)

    bias_row = query_bias.reshape(1, head_features)
    record = head_features + 2 * heads
    full_type = f32 if half % 16 else bf16
    output_type = f32 if output_weight.shape[0] % 16 else bf16
    spread = pltpu.VMEM((heads * 2 * rows, 256), bf16)
    partial, queries, key_full, value_full = pl.pallas_call(
        functools.partial(early_kernel, steps, heads),
        out_shape=[
            struct((samples, record, 2 * rows), f32),
            struct((samples, 2 * rows, head_features), bf16),
            struct((features, head_features), bf16),
            struct((head_features, features), bf16),
        ],
        scratch_shapes=[
            pltpu.VMEM((features, 2 * head_features), full_type),
            pltpu.VMEM((features, head_features), full_type),
            spread,
        ],
        compiler_params=params,
        name="early",
    )(weights_mine, weights_other, bias_row, shifted, shifted_other, own_bias, swapped, own_value, swapped_value, *ring)
    then_output, _ = after((own_output, partial))
    swapped_output = swap_cores(then_output)
    keep, got = [], []
    chunks = 2
    each = samples // chunks
    for c in range(chunks):
        kept, give = pl.pallas_call(
            functools.partial(late_kernel, steps, heads, c * each),
            out_shape=[struct((each // 2, record, 2 * rows), f32)] * 2,
            scratch_shapes=[pltpu.VMEM((each, record, 2 * rows), f32), spread],
            compiler_params=params,
            name="late",
        )(partial, queries, key_full, value_full, own_bias, swapped, last)
        keep.append(kept)
        got.append(swap_cores(give))
    updated = []
    for c in range(chunks):
        operands = [own_output, swapped_output, activations, output_gate, keep[c], got[c], *updated]
        updated = [
            pl.pallas_call(
                functools.partial(finish_kernel, heads, c * each),
                in_specs=[pl.BlockSpec(memory_space=pltpu.VMEM)] * 6 + [in_hbm] * len(updated),
                out_specs=in_hbm,
                out_shape=struct(activations.shape, bf16),
                input_output_aliases={6: 0} if updated else {},
                scratch_shapes=[
                    pltpu.VMEM((each, rows, features), bf16),
                    pltpu.VMEM((head_features, features), output_type),
                    pltpu.SemaphoreType.DMA((each,)),
                ],
                compiler_params=params,
                name="finish",
            )(*operands)
        ]
    return updated[0]


def solution(mesh):
    return jax.shard_map(
        body,
        mesh=mesh,
        in_specs=(
            P("noise", "row", None),
            P("noise", "row", None),
            P("noise", "row", None),
            P("noise", "row", None),
            P("row", "noise", None),
            P(),
            P("noise", None),
            P(),
            P("noise", None),
            P("noise", None),
            P("noise", None),
            P("noise", "row"),
        ),
        out_specs=P("noise", "row", None),
        check_vma=False,
    )
```

```python
import functools
import math

import jax
import jax.numpy as jnp
from jax import lax
from jax.experimental import pallas as pl
from jax.experimental.pallas import tpu as pltpu
from jax.sharding import PartitionSpec as P

epsilon = 1e-05
masked_score = -1e30
absent = 32768.0
log2_e = math.log2(math.e)
vmem_bytes = 40 * 2**20
wide_bytes = 60 * 2**20


def layer_norm(tensor):
    average = jnp.mean(tensor, axis=-1, keepdims=True)
    centred = tensor - average
    variance = jnp.mean(centred * centred, axis=-1, keepdims=True)
    return centred * lax.rsqrt(variance + epsilon)


def shift_kernel(
    activations_hbm,
    scale_hbm,
    shift_hbm,
    mask_hbm,
    key_hbm,
    value_hbm,
    output_hbm,
    shifted_hbm,
    sent_hbm,
    packed_hbm,
    columns_hbm,
    shifted,
    sent,
    packed,
    columns,
    activations,
    cond_scale,
    cond_shift,
    token_mask,
    key_weight,
    value_weight,
    output_weight,
    sems,
    sems_out,
):
    samples, rows, features = activations.shape
    copies = [pltpu.make_async_copy(mask_hbm, token_mask, sems.at[0])]
    for s in range(samples):
        for t, (source, target) in enumerate(
            ((activations_hbm, activations), (scale_hbm, cond_scale), (shift_hbm, cond_shift))
        ):
            copies.append(pltpu.make_async_copy(source.at[s], target.at[s], sems.at[1 + 3 * s + t]))
    copies.append(pltpu.make_async_copy(key_hbm, key_weight, sems.at[1 + 3 * samples]))
    copies.append(pltpu.make_async_copy(value_hbm, value_weight, sems.at[2 + 3 * samples]))
    copies.append(pltpu.make_async_copy(output_hbm, output_weight, sems.at[3 + 3 * samples]))
    for copy in copies:
        copy.start()
    diagonal = lax.broadcasted_iota(jnp.int32, (rows, rows), 0) == lax.broadcasted_iota(
        jnp.int32, (rows, rows), 1
    )
    copies[0].wait()
    written = []
    for s in range(samples):
        for copy in copies[1 + 3 * s : 4 + 3 * s]:
            copy.wait()
        normed = layer_norm(activations[s].astype(jnp.float32))
        result = cond_scale[s].astype(jnp.float32) * normed + cond_shift[s].astype(jnp.float32)
        flags = jnp.where(diagonal, token_mask[s : s + 1, :].astype(jnp.float32), 0.0)
        valid = jnp.sum(flags, axis=1, keepdims=True) > 0.0
        shifted[s] = result.astype(jnp.bfloat16)
        sent[s] = jnp.where(valid, result, absent).astype(jnp.bfloat16)
        for t, (source, target) in enumerate(((sent, sent_hbm), (shifted, shifted_hbm))):
            written.append(pltpu.make_async_copy(source.at[s], target.at[s], sems_out.at[2 * s + t]))
            written[-1].start()
    core = lax.rem(lax.axis_index("row"), 2)
    half, breadth = packed.shape[0], key_weight.shape[1]
    for w, weight in enumerate((key_weight, value_weight)):
        copies[1 + 3 * samples + w].wait()
        whole = weight[...].astype(jnp.float32)
        packed[:, w * breadth : (w + 1) * breadth] = jnp.where(
            core == 0, whole[:half], whole[half:]
        ).astype(jnp.bfloat16)
    written.append(pltpu.make_async_copy(packed, packed_hbm, sems_out.at[2 * samples]))
    written[-1].start()
    copies[-1].wait()
    columns[...] = jnp.where(core == 0, output_weight[:, :breadth], output_weight[:, breadth:])
    written.append(pltpu.make_async_copy(columns, columns_hbm, sems_out.at[2 * samples + 1]))
    written[-1].start()
    for copy in written:
        copy.wait()


def bias_kernel(pair_hbm, query_hbm, weights_hbm, parcel, pair, query_weight, weights, collected, sems):
    rows, columns, channels = pair.shape
    heads = weights.shape[0]
    per, batches = 8, 2
    batch = rows // batches
    copies = [pltpu.make_async_copy(weights_hbm, weights, sems.at[batches])]
    for i in range(batches):
        here = pl.ds(i * batch, batch)
        copies.append(pltpu.make_async_copy(pair_hbm.at[here], pair.at[here], sems.at[i]))
    copies.append(pltpu.make_async_copy(query_hbm, query_weight, sems.at[batches + 1]))
    for copy in copies:
        copy.start()
    copies[0].wait()
    record = 2 * heads
    extended = jnp.concatenate(
        [weights[...], jnp.full((heads, channels), 1.0 / channels, jnp.bfloat16)], axis=0
    )
    square = (channels, channels)
    diagonal = lax.broadcasted_iota(jnp.int32, square, 0) == lax.broadcasted_iota(jnp.int32, square, 1)
    centring = (jnp.where(diagonal, 1.0, 0.0) - 1.0 / channels).astype(jnp.bfloat16)
    lane = lax.broadcasted_iota(jnp.int32, (1, rows), 1)
    squares = jnp.zeros((columns, rows), jnp.float32)
    for i in range(rows // per):
        if i * per % batch == 0:
            copies[1 + i * per // batch].wait()
        block = pair[i * per : (i + 1) * per].reshape(per * columns, channels)
        centred = jnp.dot(block, centring, preferred_element_type=jnp.float32)
        summed = jnp.sum(centred * centred, axis=1, keepdims=True)
        result = lax.dot_general(
            extended, block, (((1,), (1,)), ((), ())), preferred_element_type=jnp.float32
        )
        for r in range(per):
            row = i * per + r
            collected[row * record : (row + 1) * record, :] = result[:, r * columns : (r + 1) * columns]
            squares = jnp.where(lane == row, summed[r * columns : (r + 1) * columns], squares)
    core = lax.rem(lax.axis_index("row"), 2)
    half = columns // 2
    average = collected[pl.ds(heads, rows, stride=record), :].T
    inverse = lax.rsqrt(squares / channels + epsilon)
    for p in range(heads // 2):
        own, other = [], []
        for h in (2 * p, 2 * p + 1):
            summed = jnp.sum(weights[h : h + 1, :].astype(jnp.float32), axis=1, keepdims=True)
            turned = (collected[pl.ds(h, rows, stride=record), :].T - average * summed) * inverse
            low, up = turned[:half], turned[half:]
            own.append(jnp.where(core == 0, low, up))
            other.append(jnp.where(core == 0, up, low))
        at = p * half
        parcel[at : at + half, :] = jnp.concatenate(own, axis=1).astype(jnp.bfloat16)
        at += heads // 2 * half
        parcel[at : at + half, :] = jnp.concatenate(other[::-1], axis=1).astype(jnp.bfloat16)
    copies[-1].wait()
    depth, breadth = query_weight.shape
    whole = query_weight[...].astype(jnp.float32)
    kept = jnp.where(core == 0, whole[: depth // 2], whole[depth // 2 :]).astype(jnp.bfloat16)
    for t in range(breadth // columns):
        at = heads * half + t * (depth // 2)
        parcel[at : at + depth // 2, :] = kept[:, t * columns : (t + 1) * columns]


def spread_queries(heads, queries, spread):
    count, head_features = queries.shape
    width = head_features // heads
    reach = spread.shape[1]
    lane = lax.broadcasted_iota(jnp.int32, (1, reach), 1)
    turned = jnp.concatenate([queries[count // 2 :], queries[: count // 2]], axis=0)
    for h in range(heads):
        start, free = (0, reach - 1) if h < heads // 2 else (head_features - reach, 0)
        inside = ((lane >= h * width - start) & (lane < (h + 1) * width - start)).astype(jnp.bfloat16)
        extra = (lane == free).astype(jnp.bfloat16)
        own = (turned if h % 2 else queries)[:, start : start + reach]
        spread[h * count : (h + 1) * count, :] = own * inside + extra


def extend_keys(heads, tokens, keys, reach):
    head_features = keys.shape[1]
    used = head_features // 2
    penalty = jnp.where(tokens[:, 0:1].astype(jnp.float32) > absent / 2, masked_score, 0.0)
    lane = lax.broadcasted_iota(jnp.int32, (1, reach), 1)
    first = jnp.where(lane < used, keys[:, :reach], penalty)
    second = jnp.where(lane >= reach - used, keys[:, head_features - reach :], penalty)
    return first.astype(jnp.bfloat16), second.astype(jnp.bfloat16)


def project_tokens(heads, tokens, key_weight, value_weight, reach):
    keys = jnp.dot(tokens, key_weight[...], preferred_element_type=jnp.float32)
    values = lax.dot_general(
        value_weight[...], tokens, (((1,), (1,)), ((), ())), preferred_element_type=jnp.float32
    ).astype(jnp.bfloat16)
    return extend_keys(heads, tokens, keys, reach), values


def attend_keys(heads, extended, values, bias_of, spread):
    width = values.shape[0] // heads
    count, group = spread.shape[0] // heads, heads // 2
    scores = [
        lax.dot_general(
            extended[part],
            spread[part * group * count : (part + 1) * group * count, :],
            (((1,), (1,)), ((), ())),
            preferred_element_type=jnp.float32,
        )
        for part in range(2)
    ]
    sums, highs, totals = [], [], []
    for h in range(heads):
        at = h % group * count
        score = scores[h // group][:, at : at + count] * (log2_e / math.sqrt(width))
        score = score + bias_of(h) * log2_e
        high = jnp.max(score, axis=0, keepdims=True)
        probs = jnp.exp2(score - high)
        totals.append(jnp.sum(probs, axis=0, keepdims=True))
        highs.append(high)
        sums.append(
            jnp.dot(
                values[h * width : (h + 1) * width],
                probs.astype(jnp.bfloat16),
                preferred_element_type=jnp.float32,
            )
        )
    return sums, highs, totals


def sort_kernel(*refs):
    stacks = refs[-3:]
    for k, parcel in enumerate(refs[:-3]):
        at = 0
        for stack in stacks:
            stack[k] = parcel[at : at + stack.shape[1]]
            at += stack.shape[1]


def bias_picker(parcel, swapped, steps, first, rows):
    chip = lax.axis_index("row") // 2
    place = lax.axis_index("noise")
    left = lax.broadcasted_iota(jnp.int32, (1, 2 * rows), 1) < rows

    here = jnp.where(chip % 2 == 1, (chip + 1) // 2, lax.rem(steps - chip // 2, steps))

    def pick(b, h):
        position = lax.rem(here - (first + b) + steps, steps)
        outward = (position > 0) & (position <= steps // 2)
        origin = jnp.where(outward, 2 * position - 1, 2 * lax.rem(steps - position, steps))
        part = origin ^ place
        at = slice(h // 2 * rows, (h // 2 + 1) * rows)
        pairs = parcel[part, at].astype(jnp.float32), swapped[part, at].astype(jnp.float32)
        return jnp.where(left, pairs[h % 2], pairs[1 - h % 2])

    return pick


def project_kernel(heads, noise_size, weights_mine, weights_other, *refs):
    blocks, (key_weight, value_weight, extended, values, full) = refs[:-5], refs[-5:]
    half, breadth = weights_mine.shape[1], key_weight.shape[1]
    samples = extended.shape[1]
    core = lax.rem(lax.axis_index("row"), 2)
    place = lax.axis_index("noise")
    for part, of_core in ((weights_mine, core), (weights_other, 1 - core)):
        for k in range(noise_size):
            start = ((place ^ k) * 2 + of_core) * half
            down = pl.ds(pl.multiple_of(start, math.gcd(half, 32)), half)
            full[down, :] = part[k].astype(full.dtype)
    key_weight[...] = full[:, :breadth].astype(jnp.bfloat16)
    value_weight[...] = full[:, breadth:].astype(jnp.float32).T.astype(jnp.bfloat16)
    for s in range(samples):
        tokens = jnp.concatenate([block[s] for block in blocks], axis=0)
        both, values[s] = project_tokens(heads, tokens, key_weight, value_weight, extended.shape[3])
        for part in range(2):
            extended[part, s] = both[part]


def early_kernel(
    steps,
    heads,
    query_bias,
    shifted,
    shifted_other,
    own_bias,
    swapped,
    own_query,
    swapped_query,
    key_weight,
    value_weight,
    extended,
    values,
    *refs,
):
    blocks, (partial, queries, full, spread) = refs[:-4], refs[-4:]
    samples, rows, features = shifted.shape
    noise_size = own_query.shape[0]
    breadth = key_weight.shape[1]
    half = own_query.shape[1] // (breadth // 128)
    width = breadth // heads
    core = lax.rem(lax.axis_index("row"), 2)
    place = lax.axis_index("noise")
    for part, of_core in ((own_query, core), (swapped_query, 1 - core)):
        for k in range(noise_size):
            start = ((place ^ k) * 2 + of_core) * half
            down = pl.ds(pl.multiple_of(start, math.gcd(half, 32)), half)
            for t in range(breadth // 128):
                full[down, t * 128 : (t + 1) * 128] = part[k, t * half : (t + 1) * half].astype(full.dtype)
    for side, tokens in enumerate((shifted, shifted_other)):
        result = jnp.dot(
            tokens[...].reshape(samples * rows, features),
            full[...].astype(jnp.bfloat16),
            preferred_element_type=jnp.float32,
        ) + query_bias[...].astype(jnp.float32)
        queries[:, side * rows : (side + 1) * rows] = result.astype(jnp.bfloat16).reshape(
            samples, rows, breadth
        )
    pick = bias_picker(own_bias, swapped, steps, 0, rows)
    for s in range(samples):
        tokens = jnp.concatenate([block[s] for block in blocks], axis=0)
        both, more = project_tokens(heads, tokens, key_weight, value_weight, spread.shape[1])
        spread_queries(heads, queries[s], spread)
        sums, highs, totals = attend_keys(
            heads,
            [jnp.concatenate([extended[part, s], both[part]], axis=0) for part in range(2)],
            jnp.concatenate([values[s], more], axis=1),
            lambda h: jnp.concatenate([pick(b, h) for b in range(steps - 1)], axis=0),
            spread,
        )
        for h in range(heads):
            partial[s, h * width : (h + 1) * width] = sums[h]
            partial[s, breadth + h : breadth + h + 1] = highs[h]
            partial[s, breadth + heads + h : breadth + heads + h + 1] = totals[h]


def late_kernel(steps, heads, first, partial, queries, key_weight, value_weight, own_bias, swapped, block, keep, give, merged, spread):
    samples = merged.shape[0]
    rows = block.shape[1]
    breadth = key_weight.shape[1]
    width = breadth // heads
    pick = bias_picker(own_bias, swapped, steps, steps - 1, rows)
    tokens = block[first : first + samples].reshape(samples * rows, block.shape[2])
    both, values = project_tokens(heads, tokens, key_weight, value_weight, spread.shape[1])
    for s in range(samples):
        here = slice(s * rows, (s + 1) * rows)
        spread_queries(heads, queries[first + s], spread)
        sums, highs, totals = attend_keys(
            heads, [part[here] for part in both], values[:, here], lambda h: pick(0, h), spread
        )
        before = partial.at[first + s]
        for h in range(heads):
            at_high = slice(breadth + h, breadth + h + 1)
            at_total = slice(breadth + heads + h, breadth + heads + h + 1)
            high = jnp.maximum(before[at_high], highs[h])
            old, new = jnp.exp2(before[at_high] - high), jnp.exp2(highs[h] - high)
            across = slice(h * width, (h + 1) * width)
            merged[s, across] = before[across] * old + sums[h] * new
            merged[s, at_high] = high
            merged[s, at_total] = before[at_total] * old + totals[h] * new
    half = merged.shape[2] // 2
    left = lax.broadcasted_iota(jnp.int32, (1, 2 * half), 1) < half
    row = lax.broadcasted_iota(jnp.int32, (merged.shape[1], 1), 0)
    head = jnp.where(row < breadth, row // width, (row - breadth) % heads)
    even = head % 2 == 0
    for pair in range(samples // 2):
        a, b = merged[2 * pair], merged[2 * pair + 1]
        lefts = jnp.where(left, a, pltpu.roll(b, half, 1))
        rights = jnp.where(left, pltpu.roll(a, half, 1), b)
        keep[pair] = jnp.where(even, lefts, rights)
        give[pair] = jnp.where(even, rights, lefts)


def finish_kernel(heads, first, output_mine, output_other, activations, output_gate, keep, got, *refs):
    updated_hbm, updated, output_weight, sems = refs[-4:]
    noise_size, part_rows, part_columns = output_mine.shape
    breadth = output_weight.shape[0]
    width = breadth // heads
    samples, rows, _ = updated.shape
    core = lax.rem(lax.axis_index("row"), 2)
    place = lax.axis_index("noise")
    for k in range(noise_size):
        down = pl.ds(pl.multiple_of((place ^ k) * part_rows, math.gcd(part_rows, 32)), part_rows)
        for part, of_core in ((output_mine, core), (output_other, 1 - core)):
            along = pl.ds(pl.multiple_of(of_core * part_columns, 128), part_columns)
            output_weight[down, along] = part[k].astype(output_weight.dtype)
    writes = []
    for pair in range(samples // 2):
        own, other = keep.at[pair], got.at[pair]
        parts = []
        for h in range(heads):
            at_high = slice(breadth + h, breadth + h + 1)
            at_total = slice(breadth + heads + h, breadth + heads + h + 1)
            across = slice(h * width, (h + 1) * width)
            high = jnp.maximum(own[at_high], other[at_high])
            mine, theirs = jnp.exp2(own[at_high] - high), jnp.exp2(other[at_high] - high)
            total = own[at_total] * mine + other[at_total] * theirs
            parts.append((own[across] * mine + other[across] * theirs) / total)
        attended = jnp.concatenate(parts, axis=0).T.astype(jnp.bfloat16)
        projected = jnp.dot(
            attended, output_weight[...].astype(jnp.bfloat16), preferred_element_type=jnp.float32
        )
        for side in range(2):
            s = 2 * pair + side
            gate = jax.nn.sigmoid(output_gate[first + s].astype(jnp.float32))
            updated[s] = (
                activations[first + s].astype(jnp.float32)
                + gate * projected[side * rows : (side + 1) * rows]
            ).astype(jnp.bfloat16)
            writes.append(pltpu.make_async_copy(updated.at[s], updated_hbm.at[first + s], sems.at[s]))
            writes[-1].start()
    for write in writes:
        write.wait()


def swap_cores(array):
    return lax.ppermute(array, "row", [(i, i ^ 1) for i in range(lax.axis_size("row"))])


def ring_chip(position, steps):
    return 2 * position - 1 if 0 < position <= steps // 2 else 2 * ((steps - position) % steps)


def next_chip(array):
    steps = lax.axis_size("row") // 2
    order = [ring_chip(p, steps) for p in range(steps)]
    pairs = [
        (2 * order[p] + c, 2 * order[(p + 1) % steps] + c) for p in range(steps) for c in range(2)
    ]
    return lax.ppermute(array, "row", pairs)


def from_noise(array, k):
    if k == 0:
        return array
    return lax.ppermute(array, "noise", [(i, i ^ k) for i in range(lax.axis_size("noise"))])


def body(
    activations,
    cond_scale,
    cond_shift,
    output_gate,
    pair_repr,
    bias_weight,
    query_weight,
    query_bias,
    key_weight,
    value_weight,
    output_weight,
    token_mask,
):
    samples, rows, features = activations.shape
    heads = bias_weight.shape[1]
    head_features = query_weight.shape[1]
    noise_size = lax.axis_size("noise")
    steps = lax.axis_size("row") // 2
    assert noise_size == steps and pair_repr.shape[1] == 2 * rows
    bf16, f32 = jnp.bfloat16, jnp.float32
    params = pltpu.CompilerParams(vmem_limit_bytes=vmem_bytes)
    struct = jax.ShapeDtypeStruct
    after = lax.optimization_barrier
    half = query_weight.shape[0] // 2

    in_hbm = pl.BlockSpec(memory_space=pltpu.HBM)
    packed_shape, columns_shape = (half, 2 * head_features), (output_weight.shape[0], features // 2)
    shifted, sent, packed, output_columns = pl.pallas_call(
        shift_kernel,
        in_specs=[in_hbm] * 7,
        out_specs=[in_hbm] * 4,
        out_shape=[struct(activations.shape, bf16)] * 2
        + [struct(packed_shape, bf16), struct(columns_shape, bf16)],
        scratch_shapes=[pltpu.VMEM(activations.shape, bf16)] * 2
        + [pltpu.VMEM(packed_shape, bf16), pltpu.VMEM(columns_shape, bf16)]
        + [pltpu.VMEM(activations.shape, bf16)] * 3
        + [pltpu.VMEM(token_mask.shape, jnp.int32)]
        + [pltpu.VMEM(query_weight.shape, bf16)] * 2
        + [pltpu.VMEM(output_weight.shape, bf16)]
        + [pltpu.SemaphoreType.DMA((3 * samples + 4,)), pltpu.SemaphoreType.DMA((2 * samples + 2,))],
        compiler_params=pltpu.CompilerParams(vmem_limit_bytes=wide_bytes),
        name="shift",
    )(activations, cond_scale, cond_shift, token_mask, key_weight, value_weight, output_weight)

    ring = [sent, next_chip(sent)]
    weights = [packed] + [from_noise(packed, k) for k in range(noise_size - 1, 0, -1)][::-1]
    head_weights, _ = after((bias_weight.T, packed))
    columns = pair_repr.shape[1]
    tile_rows = heads * rows
    parcel = pl.pallas_call(
        bias_kernel,
        in_specs=[in_hbm] * 3,
        out_shape=struct((tile_rows + 3 * half, columns), bf16),
        scratch_shapes=[
            pltpu.VMEM(pair_repr.shape, bf16),
            pltpu.VMEM(query_weight.shape, bf16),
            pltpu.VMEM(head_weights.shape, bf16),
            pltpu.VMEM((rows * 2 * heads, columns), f32),
            pltpu.SemaphoreType.DMA((4,)),
        ],
        compiler_params=pltpu.CompilerParams(vmem_limit_bytes=wide_bytes),
        name="bias",
    )(pair_repr, query_weight, head_weights)
    shifted_other = swap_cores(shifted)
    ring[1], weights, parcel, shifted_other = after((ring[1], weights, parcel, shifted_other))
    output_next = from_noise(output_columns, 1)
    ring.append(next_chip(ring[1]))
    output_mine = jnp.stack([output_columns, output_next])
    weights_mine = jnp.stack(weights)
    weights_other = swap_cores(weights_mine)
    parcels = [from_noise(parcel, k) for k in range(noise_size)]

    bias_row = query_bias.reshape(1, head_features)
    record = head_features + 2 * heads
    reach = 256
    spread = pltpu.VMEM((heads * 2 * rows, reach), bf16)
    full_type = f32 if half % 16 else bf16
    output_type = f32 if output_weight.shape[0] % 16 else bf16
    key_full, value_full, extended, values = pl.pallas_call(
        functools.partial(project_kernel, heads, noise_size),
        out_shape=[
            struct((features, head_features), bf16),
            struct((head_features, features), bf16),
            struct((2, samples, 2 * rows, reach), bf16),
            struct((samples, head_features, 2 * rows), bf16),
        ],
        scratch_shapes=[pltpu.VMEM((features, 2 * head_features), full_type)],
        compiler_params=params,
        name="project",
    )(weights_mine, weights_other, *ring[:2])

    ring[2], _ = after((ring[2], extended))
    for _ in range(steps - 3):
        ring.append(next_chip(ring[-1]))
    last = ring.pop()
    tile_shape = (noise_size, tile_rows // 2, columns)
    query_shape = (noise_size, parcel.shape[0] - tile_rows, columns)
    own_bias, other_bias, own_query = pl.pallas_call(
        sort_kernel,
        out_shape=[struct(shape, bf16) for shape in (tile_shape, tile_shape, query_shape)],
        compiler_params=params,
        name="sort",
    )(*parcels)
    swapped = swap_cores(other_bias)
    swapped_query = swap_cores(own_query)
    output_mine, _ = after((output_mine, extended))
    for k in range(1, noise_size.bit_length() - 1):
        output_mine = jnp.concatenate([output_mine, from_noise(output_mine, 2**k)], axis=0)
    output_other = swap_cores(output_mine)
    partial, queries = pl.pallas_call(
        functools.partial(early_kernel, steps, heads),
        out_shape=[
            struct((samples, record, 2 * rows), f32),
            struct((samples, 2 * rows, head_features), bf16),
        ],
        scratch_shapes=[pltpu.VMEM((features, head_features), full_type), spread],
        compiler_params=params,
        name="early",
    )(
        bias_row,
        shifted,
        shifted_other,
        own_bias,
        swapped,
        own_query,
        swapped_query,
        key_full,
        value_full,
        extended,
        values,
        *ring[2:],
    )
    keep, got = [], []
    chunks = 2
    each = samples // chunks
    for c in range(chunks):
        kept, give = pl.pallas_call(
            functools.partial(late_kernel, steps, heads, c * each),
            out_shape=[struct((each // 2, record, 2 * rows), f32)] * 2,
            scratch_shapes=[pltpu.VMEM((each, record, 2 * rows), f32), spread],
            compiler_params=params,
            name="late",
        )(partial, queries, key_full, value_full, own_bias, swapped, last)
        keep.append(kept)
        got.append(swap_cores(give))
    updated = []
    for c in range(chunks):
        operands = [output_mine, output_other, activations, output_gate, keep[c], got[c], *updated]
        updated = [
            pl.pallas_call(
                functools.partial(finish_kernel, heads, c * each),
                in_specs=[pl.BlockSpec(memory_space=pltpu.VMEM)] * 6 + [in_hbm] * len(updated),
                out_specs=in_hbm,
                out_shape=struct(activations.shape, bf16),
                input_output_aliases={6: 0} if updated else {},
                scratch_shapes=[
                    pltpu.VMEM((each, rows, features), bf16),
                    pltpu.VMEM((head_features, features), output_type),
                    pltpu.SemaphoreType.DMA((each,)),
                ],
                compiler_params=params,
                name="finish",
            )(*operands)
        ]
    return updated[0]


def solution(mesh):
    return jax.shard_map(
        body,
        mesh=mesh,
        in_specs=(
            P("noise", "row", None),
            P("noise", "row", None),
            P("noise", "row", None),
            P("noise", "row", None),
            P("row", "noise", None),
            P(),
            P("noise", None),
            P(),
            P("noise", None),
            P("noise", None),
            P("noise", None),
            P("noise", "row"),
        ),
        out_specs=P("noise", "row", None),
        check_vma=False,
    )
```

```python
import functools
import math

import jax
import jax.numpy as jnp
from jax import lax
from jax.experimental import pallas as pl
from jax.experimental.pallas import tpu as pltpu
from jax.sharding import PartitionSpec as P

epsilon = 1e-05
masked_score = -1e30
absent = 32768.0
log2_e = math.log2(math.e)
vmem_bytes = 40 * 2**20
wide_bytes = 60 * 2**20


def layer_norm(tensor):
    average = jnp.mean(tensor, axis=-1, keepdims=True)
    centred = tensor - average
    variance = jnp.mean(centred * centred, axis=-1, keepdims=True)
    return centred * lax.rsqrt(variance + epsilon)


def shift_kernel(
    activations_hbm,
    scale_hbm,
    shift_hbm,
    mask_hbm,
    query_hbm,
    key_hbm,
    output_hbm,
    shifted_hbm,
    sent_hbm,
    packed_hbm,
    extended_hbm,
    shifted,
    sent,
    extended,
    activations,
    cond_scale,
    cond_shift,
    token_mask,
    query_weight,
    key_weight,
    output_weight,
    sems,
    sems_out,
):
    samples, rows, features = activations.shape
    copies = [pltpu.make_async_copy(mask_hbm, token_mask, sems.at[0])]
    for s in range(samples):
        for t, (source, target) in enumerate(
            ((activations_hbm, activations), (scale_hbm, cond_scale), (shift_hbm, cond_shift))
        ):
            copies.append(pltpu.make_async_copy(source.at[s], target.at[s], sems.at[1 + 3 * s + t]))
    copies.append(pltpu.make_async_copy(query_hbm, query_weight, sems.at[1 + 3 * samples]))
    copies.append(pltpu.make_async_copy(key_hbm, key_weight, sems.at[2 + 3 * samples]))
    copies.append(pltpu.make_async_copy(output_hbm, output_weight, sems.at[3 + 3 * samples]))
    for copy in copies:
        copy.start()
    diagonal = lax.broadcasted_iota(jnp.int32, (rows, rows), 0) == lax.broadcasted_iota(
        jnp.int32, (rows, rows), 1
    )
    copies[0].wait()
    written = []
    for s in range(samples):
        for copy in copies[1 + 3 * s : 4 + 3 * s]:
            copy.wait()
        normed = layer_norm(activations[s].astype(jnp.float32))
        result = cond_scale[s].astype(jnp.float32) * normed + cond_shift[s].astype(jnp.float32)
        flags = jnp.where(diagonal, token_mask[s : s + 1, :].astype(jnp.float32), 0.0)
        valid = jnp.sum(flags, axis=1, keepdims=True) > 0.0
        shifted[s] = result.astype(jnp.bfloat16)
        sent[s] = jnp.where(valid, result, absent).astype(jnp.bfloat16)
        for t, (source, target) in enumerate(((sent, sent_hbm), (shifted, shifted_hbm))):
            written.append(pltpu.make_async_copy(source.at[s], target.at[s], sems_out.at[2 * s + t]))
            written[-1].start()
    core = lax.rem(lax.axis_index("row"), 2)
    half, breadth = packed_hbm.shape[0], query_weight.shape[1]
    for w, weight in enumerate((query_weight, key_weight)):
        copies[1 + 3 * samples + w].wait()
        whole = weight[...].astype(jnp.float32)
        extended[0:half, w * breadth : (w + 1) * breadth] = jnp.where(
            core == 0, whole[:half], whole[half:]
        ).astype(jnp.bfloat16)
    written.append(
        pltpu.make_async_copy(
            extended.at[0:half, 0 : 2 * breadth], packed_hbm, sems_out.at[2 * samples]
        )
    )
    written[-1].start()
    copies[-1].wait()
    extended[:, 2 * breadth :] = jnp.where(
        core == 0, output_weight[:, :breadth], output_weight[:, breadth:]
    )
    written.append(pltpu.make_async_copy(extended, extended_hbm, sems_out.at[2 * samples + 1]))
    written[-1].start()
    for copy in written:
        copy.wait()


def bias_kernel(
    pair_hbm, value_hbm, weights_hbm, parcel, pair, value_weight, weights, collected, sems
):
    rows, columns, channels = pair.shape
    heads = weights.shape[0]
    per, batches = 8, 2
    batch = rows // batches
    copies = [pltpu.make_async_copy(weights_hbm, weights, sems.at[batches])]
    for i in range(batches):
        here = pl.ds(i * batch, batch)
        copies.append(pltpu.make_async_copy(pair_hbm.at[here], pair.at[here], sems.at[i]))
    copies.append(pltpu.make_async_copy(value_hbm, value_weight, sems.at[batches + 1]))
    for copy in copies:
        copy.start()
    copies[0].wait()
    record = 2 * heads
    extended = jnp.concatenate(
        [weights[...], jnp.full((heads, channels), 1.0 / channels, jnp.bfloat16)], axis=0
    )
    square = (channels, channels)
    diagonal = lax.broadcasted_iota(jnp.int32, square, 0) == lax.broadcasted_iota(jnp.int32, square, 1)
    centring = (jnp.where(diagonal, 1.0, 0.0) - 1.0 / channels).astype(jnp.bfloat16)
    lane = lax.broadcasted_iota(jnp.int32, (1, rows), 1)
    squares = jnp.zeros((columns, rows), jnp.float32)
    for i in range(rows // per):
        if i * per % batch == 0:
            copies[1 + i * per // batch].wait()
        block = pair[i * per : (i + 1) * per].reshape(per * columns, channels)
        centred = jnp.dot(block, centring, preferred_element_type=jnp.float32)
        summed = jnp.sum(centred * centred, axis=1, keepdims=True)
        result = lax.dot_general(
            extended, block, (((1,), (1,)), ((), ())), preferred_element_type=jnp.float32
        )
        for r in range(per):
            row = i * per + r
            collected[row * record : (row + 1) * record, :] = result[:, r * columns : (r + 1) * columns]
            squares = jnp.where(lane == row, summed[r * columns : (r + 1) * columns], squares)
    core = lax.rem(lax.axis_index("row"), 2)
    half = columns // 2
    average = collected[pl.ds(heads, rows, stride=record), :].T
    inverse = lax.rsqrt(squares / channels + epsilon)
    for p in range(heads // 2):
        own, other = [], []
        for h in (2 * p, 2 * p + 1):
            summed = jnp.sum(weights[h : h + 1, :].astype(jnp.float32), axis=1, keepdims=True)
            turned = (collected[pl.ds(h, rows, stride=record), :].T - average * summed) * inverse
            low, up = turned[:half], turned[half:]
            own.append(jnp.where(core == 0, low, up))
            other.append(jnp.where(core == 0, up, low))
        at = p * half
        parcel[at : at + half, :] = jnp.concatenate(own, axis=1).astype(jnp.bfloat16)
        at += heads // 2 * half
        parcel[at : at + half, :] = jnp.concatenate(other[::-1], axis=1).astype(jnp.bfloat16)
    copies[-1].wait()
    depth, breadth = value_weight.shape
    whole = value_weight[...].astype(jnp.float32)
    kept = jnp.where(core == 0, whole[: depth // 2], whole[depth // 2 :]).astype(jnp.bfloat16)
    at = heads * half
    for t in range(breadth // columns):
        parcel[at : at + depth // 2, :] = kept[:, t * columns : (t + 1) * columns]
        at += depth // 2


def sort_kernel(*refs):
    stacks = refs[-3:]
    for k, parcel in enumerate(refs[:-3]):
        at = 0
        for stack in stacks:
            stack[k] = parcel[at : at + stack.shape[1]]
            at += stack.shape[1]


def stack_kernel(first, *refs):
    stacks = [ref for ref in refs if len(ref.shape) == 3]
    for k, part in enumerate(refs[: -len(stacks)]):
        for t, stack in enumerate(stacks):
            breadth = stack.shape[2]
            stack[k] = part[:, (first + t) * breadth : (first + t + 1) * breadth]


def spread_queries(heads, queries, spread):
    count, head_features = queries.shape
    width = head_features // heads
    reach = spread.shape[1]
    lane = lax.broadcasted_iota(jnp.int32, (1, reach), 1)
    turned = jnp.concatenate([queries[count // 2 :], queries[: count // 2]], axis=0)
    for h in range(heads):
        start, free = (0, reach - 1) if h < heads // 2 else (head_features - reach, 0)
        inside = ((lane >= h * width - start) & (lane < (h + 1) * width - start)).astype(jnp.bfloat16)
        extra = (lane == free).astype(jnp.bfloat16)
        own = (turned if h % 2 else queries)[:, start : start + reach]
        spread[h * count : (h + 1) * count, :] = own * inside + extra


def attend_keys(heads, tokens, keys, values, bias_of, spread):
    head_features = values.shape[0]
    width = head_features // heads
    count, reach = spread.shape[0] // heads, spread.shape[1]
    used = heads // 2 * width
    penalty = jnp.where(tokens[:, 0:1].astype(jnp.float32) > absent / 2, masked_score, 0.0)
    lane = lax.broadcasted_iota(jnp.int32, (1, reach), 1)
    scores = []
    for part in range(2):
        start = part * (head_features - reach)
        inside = lane < used if part == 0 else lane >= reach - used
        extended = jnp.where(inside, keys[:, start : start + reach], penalty).astype(jnp.bfloat16)
        scores.append(
            lax.dot_general(
                extended,
                spread[part * heads // 2 * count : (part + 1) * heads // 2 * count, :],
                (((1,), (1,)), ((), ())),
                preferred_element_type=jnp.float32,
            )
        )
    sums, highs, totals = [], [], []
    for h in range(heads):
        at = h % (heads // 2) * count
        score = scores[h // (heads // 2)][:, at : at + count] * (log2_e / math.sqrt(width))
        score = score + bias_of(h) * log2_e
        high = jnp.max(score, axis=0, keepdims=True)
        probs = jnp.exp2(score - high)
        totals.append(jnp.sum(probs, axis=0, keepdims=True))
        highs.append(high)
        sums.append(
            jnp.dot(
                values[h * width : (h + 1) * width],
                probs.astype(jnp.bfloat16),
                preferred_element_type=jnp.float32,
            )
        )
    return sums, highs, totals


def bias_picker(parcel, swapped, steps, first, rows):
    chip = lax.axis_index("row") // 2
    place = lax.axis_index("noise")
    left = lax.broadcasted_iota(jnp.int32, (1, 2 * rows), 1) < rows

    here = jnp.where(chip % 2 == 1, (chip + 1) // 2, lax.rem(steps - chip // 2, steps))

    def pick(b, h):
        position = lax.rem(here - (first + b) + steps, steps)
        outward = (position > 0) & (position <= steps // 2)
        origin = jnp.where(outward, 2 * position - 1, 2 * lax.rem(steps - position, steps))
        part = origin ^ place
        at = slice(h // 2 * rows, (h // 2 + 1) * rows)
        pairs = parcel[part, at].astype(jnp.float32), swapped[part, at].astype(jnp.float32)
        return jnp.where(left, pairs[h % 2], pairs[1 - h % 2])

    return pick


def early_kernel(steps, heads, query_mine, key_mine, query_other, key_other, query_bias, shifted, shifted_other, own_bias, swapped, own_value, swapped_value, *refs):
    blocks = refs[: steps - 1]
    partial, queries, key_weight, value_weight, full, full_value, spread = refs[steps - 1 :]
    samples, rows, features = shifted.shape
    noise_size, half, _ = query_mine.shape
    breadth = key_weight.shape[1]
    width = breadth // heads
    core = lax.rem(lax.axis_index("row"), 2)
    place = lax.axis_index("noise")
    for query, key, value, of_core in (
        (query_mine, key_mine, own_value, core),
        (query_other, key_other, swapped_value, 1 - core),
    ):
        for k in range(noise_size):
            start = ((place ^ k) * 2 + of_core) * half
            down = pl.ds(pl.multiple_of(start, math.gcd(half, 32)), half)
            full[down, 0:breadth] = query[k].astype(full.dtype)
            full[down, breadth:] = key[k].astype(full.dtype)
            for t in range(breadth // 128):
                at = t * half
                full_value[down, t * 128 : (t + 1) * 128] = value[k, at : at + half].astype(full.dtype)
    key_weight[...] = full[:, breadth : 2 * breadth].astype(jnp.bfloat16)
    value_weight[...] = full_value[...].astype(jnp.float32).T.astype(jnp.bfloat16)
    for side, tokens in enumerate((shifted, shifted_other)):
        result = jnp.dot(
            tokens[...].reshape(samples * rows, features),
            full[:, 0:breadth].astype(jnp.bfloat16),
            preferred_element_type=jnp.float32,
        ) + query_bias[...].astype(jnp.float32)
        queries[:, side * rows : (side + 1) * rows] = result.astype(jnp.bfloat16).reshape(
            samples, rows, breadth
        )
    pick = bias_picker(own_bias, swapped, steps, 0, rows)
    for s in range(samples):
        tokens = jnp.concatenate([block[s] for block in blocks], axis=0)
        keys = jnp.dot(tokens, key_weight[...], preferred_element_type=jnp.float32)
        values = lax.dot_general(
            value_weight[...], tokens, (((1,), (1,)), ((), ())), preferred_element_type=jnp.float32
        ).astype(jnp.bfloat16)
        spread_queries(heads, queries[s], spread)
        sums, highs, totals = attend_keys(
            heads,
            tokens,
            keys,
            values,
            lambda h: jnp.concatenate([pick(b, h) for b in range(steps - 1)], axis=0),
            spread,
        )
        for h in range(heads):
            partial[s, h * width : (h + 1) * width] = sums[h]
            partial[s, breadth + h : breadth + h + 1] = highs[h]
            partial[s, breadth + heads + h : breadth + heads + h + 1] = totals[h]


def late_kernel(steps, heads, first, partial, queries, key_weight, value_weight, own_bias, swapped, block, keep, give, merged, spread):
    samples = merged.shape[0]
    rows = block.shape[1]
    breadth = key_weight.shape[1]
    width = breadth // heads
    pick = bias_picker(own_bias, swapped, steps, steps - 1, rows)
    tokens = block[first : first + samples].reshape(samples * rows, block.shape[2])
    keys = jnp.dot(tokens, key_weight[...], preferred_element_type=jnp.float32)
    values = lax.dot_general(
        value_weight[...], tokens, (((1,), (1,)), ((), ())), preferred_element_type=jnp.float32
    ).astype(jnp.bfloat16)
    for s in range(samples):
        here = slice(s * rows, (s + 1) * rows)
        spread_queries(heads, queries[first + s], spread)
        sums, highs, totals = attend_keys(
            heads, tokens[here], keys[here], values[:, here], lambda h: pick(0, h), spread
        )
        before = partial.at[first + s]
        for h in range(heads):
            at_high = slice(breadth + h, breadth + h + 1)
            at_total = slice(breadth + heads + h, breadth + heads + h + 1)
            high = jnp.maximum(before[at_high], highs[h])
            old, new = jnp.exp2(before[at_high] - high), jnp.exp2(highs[h] - high)
            across = slice(h * width, (h + 1) * width)
            merged[s, across] = before[across] * old + sums[h] * new
            merged[s, at_high] = high
            merged[s, at_total] = before[at_total] * old + totals[h] * new
    half = merged.shape[2] // 2
    left = lax.broadcasted_iota(jnp.int32, (1, 2 * half), 1) < half
    row = lax.broadcasted_iota(jnp.int32, (merged.shape[1], 1), 0)
    head = jnp.where(row < breadth, row // width, (row - breadth) % heads)
    even = head % 2 == 0
    for pair in range(samples // 2):
        a, b = merged[2 * pair], merged[2 * pair + 1]
        lefts = jnp.where(left, a, pltpu.roll(b, half, 1))
        rights = jnp.where(left, pltpu.roll(a, half, 1), b)
        keep[pair] = jnp.where(even, lefts, rights)
        give[pair] = jnp.where(even, rights, lefts)


def finish_kernel(heads, first, groups, *refs):
    own_output, swapped_output = refs[:groups], refs[groups : 2 * groups]
    activations, output_gate, keep, got = refs[2 * groups : 2 * groups + 4]
    updated_hbm, updated, output_weight, sems = refs[-4:]
    _, part_rows, part_columns = own_output[0].shape
    breadth = output_weight.shape[0]
    width = breadth // heads
    samples, rows, _ = updated.shape
    core = lax.rem(lax.axis_index("row"), 2)
    place = lax.axis_index("noise")
    for parts, of_core in ((own_output, core), (swapped_output, 1 - core)):
        along = pl.ds(pl.multiple_of(of_core * part_columns, 128), part_columns)
        ordered = [part.at[k] for part in parts for k in range(part.shape[0])]
        for k, part in enumerate(ordered):
            down = pl.ds(pl.multiple_of((place ^ k) * part_rows, math.gcd(part_rows, 32)), part_rows)
            output_weight[down, along] = part[...].astype(output_weight.dtype)
    writes = []
    for pair in range(samples // 2):
        own, other = keep.at[pair], got.at[pair]
        parts = []
        for h in range(heads):
            at_high = slice(breadth + h, breadth + h + 1)
            at_total = slice(breadth + heads + h, breadth + heads + h + 1)
            across = slice(h * width, (h + 1) * width)
            high = jnp.maximum(own[at_high], other[at_high])
            mine, theirs = jnp.exp2(own[at_high] - high), jnp.exp2(other[at_high] - high)
            total = own[at_total] * mine + other[at_total] * theirs
            parts.append((own[across] * mine + other[across] * theirs) / total)
        attended = jnp.concatenate(parts, axis=0).T.astype(jnp.bfloat16)
        projected = jnp.dot(
            attended, output_weight[...].astype(jnp.bfloat16), preferred_element_type=jnp.float32
        )
        for side in range(2):
            s = 2 * pair + side
            gate = jax.nn.sigmoid(output_gate[first + s].astype(jnp.float32))
            updated[s] = (
                activations[first + s].astype(jnp.float32)
                + gate * projected[side * rows : (side + 1) * rows]
            ).astype(jnp.bfloat16)
            writes.append(pltpu.make_async_copy(updated.at[s], updated_hbm.at[first + s], sems.at[s]))
            writes[-1].start()
    for write in writes:
        write.wait()


def swap_cores(array):
    return lax.ppermute(array, "row", [(i, i ^ 1) for i in range(lax.axis_size("row"))])


def ring_chip(position, steps):
    return 2 * position - 1 if 0 < position <= steps // 2 else 2 * ((steps - position) % steps)


def next_chip(array):
    steps = lax.axis_size("row") // 2
    order = [ring_chip(p, steps) for p in range(steps)]
    pairs = [
        (2 * order[p] + c, 2 * order[(p + 1) % steps] + c) for p in range(steps) for c in range(2)
    ]
    return lax.ppermute(array, "row", pairs)


def from_noise(array, k):
    if k == 0:
        return array
    return lax.ppermute(array, "noise", [(i, i ^ k) for i in range(lax.axis_size("noise"))])


def from_all_noise(own, direct, breadth):
    parts = [own] + [None] * (2 ** len(direct) - 1)
    for k in range(1, len(parts)):
        low = k & -k
        if low == k:
            parts[k] = direct[low.bit_length() - 1]
        else:
            parts[k] = from_noise(parts[k ^ low][:, :breadth], low)
    return parts


def body(
    activations,
    cond_scale,
    cond_shift,
    output_gate,
    pair_repr,
    bias_weight,
    query_weight,
    query_bias,
    key_weight,
    value_weight,
    output_weight,
    token_mask,
):
    samples, rows, features = activations.shape
    heads = bias_weight.shape[1]
    head_features = query_weight.shape[1]
    noise_size = lax.axis_size("noise")
    steps = lax.axis_size("row") // 2
    assert noise_size == steps and pair_repr.shape[1] == 2 * rows
    bf16, f32 = jnp.bfloat16, jnp.float32
    params = pltpu.CompilerParams(vmem_limit_bytes=vmem_bytes)
    struct = jax.ShapeDtypeStruct
    after = lax.optimization_barrier
    half = query_weight.shape[0] // 2

    in_hbm = pl.BlockSpec(memory_space=pltpu.HBM)
    packed_shape, extended_shape = (half, 2 * head_features), (half, 3 * head_features)
    assert output_weight.shape == (half, 2 * head_features)
    shifted, sent, packed, extended = pl.pallas_call(
        shift_kernel,
        in_specs=[in_hbm] * 7,
        out_specs=[in_hbm] * 4,
        out_shape=[struct(activations.shape, bf16)] * 2
        + [struct(packed_shape, bf16), struct(extended_shape, bf16)],
        scratch_shapes=[pltpu.VMEM(activations.shape, bf16)] * 2
        + [pltpu.VMEM(extended_shape, bf16)]
        + [pltpu.VMEM(activations.shape, bf16)] * 3
        + [pltpu.VMEM(token_mask.shape, jnp.int32)]
        + [pltpu.VMEM(query_weight.shape, bf16)] * 2
        + [pltpu.VMEM(output_weight.shape, bf16)]
        + [pltpu.SemaphoreType.DMA((3 * samples + 4,)), pltpu.SemaphoreType.DMA((2 * samples + 2,))],
        compiler_params=pltpu.CompilerParams(vmem_limit_bytes=wide_bytes),
        name="shift",
    )(activations, cond_scale, cond_shift, token_mask, query_weight, key_weight, output_weight)

    ring = [sent, next_chip(sent)]
    direct = [from_noise(extended, 1)] + [from_noise(packed, 2**k) for k in range(1, noise_size.bit_length() - 1)]
    head_weights, _ = after((bias_weight.T, packed))
    columns = pair_repr.shape[1]
    tile_rows, piece_rows = heads * rows, head_features // columns * half
    assert output_weight.shape == (half, 2 * head_features)
    parcel = pl.pallas_call(
        bias_kernel,
        in_specs=[in_hbm] * 3,
        out_shape=struct((tile_rows + piece_rows, columns), bf16),
        scratch_shapes=[
            pltpu.VMEM(pair_repr.shape, bf16),
            pltpu.VMEM(value_weight.shape, bf16),
            pltpu.VMEM(head_weights.shape, bf16),
            pltpu.VMEM((rows * 2 * heads, columns), f32),
            pltpu.SemaphoreType.DMA((4,)),
        ],
        compiler_params=pltpu.CompilerParams(vmem_limit_bytes=wide_bytes),
        name="bias",
    )(pair_repr, value_weight, head_weights)
    shifted_other = swap_cores(shifted)
    ring[1], direct, parcel, shifted_other = after((ring[1], direct, parcel, shifted_other))
    ring.append(next_chip(ring[1]))
    parcels = [from_noise(parcel, k) for k in range(noise_size)]
    weights = from_all_noise(extended, direct, 2 * head_features)
    part_shape = (noise_size, half, head_features)
    query_mine, key_mine = pl.pallas_call(
        functools.partial(stack_kernel, 0),
        out_shape=[struct(part_shape, bf16)] * 2,
        compiler_params=params,
        name="stack",
    )(*weights)
    query_other, key_other = swap_cores(query_mine), swap_cores(key_mine)
    output_mine = pl.pallas_call(
        functools.partial(stack_kernel, 2),
        out_shape=struct((2, half, head_features), bf16),
        compiler_params=params,
        name="stack_output",
    )(extended, direct[0])
    output_mine, _ = after((output_mine, ring[2]))

    for _ in range(steps - 3):
        ring.append(next_chip(ring[-1]))
    last = ring.pop()
    tile_shape, piece_shape = (noise_size, tile_rows // 2, columns), (noise_size, piece_rows, columns)
    own_bias, other_bias, own_value = pl.pallas_call(
        sort_kernel,
        out_shape=[struct(shape, bf16) for shape in (tile_shape, tile_shape, piece_shape)],
        compiler_params=params,
        name="sort",
    )(*parcels)
    swapped = swap_cores(other_bias)
    swapped_value = swap_cores(own_value)

    bias_row = query_bias.reshape(1, head_features)
    record = head_features + 2 * heads
    full_type = f32 if half % 16 else bf16
    output_type = f32 if output_weight.shape[0] % 16 else bf16
    spread = pltpu.VMEM((heads * 2 * rows, 256), bf16)
    partial, queries, key_full, value_full = pl.pallas_call(
        functools.partial(early_kernel, steps, heads),
        out_shape=[
            struct((samples, record, 2 * rows), f32),
            struct((samples, 2 * rows, head_features), bf16),
            struct((features, head_features), bf16),
            struct((head_features, features), bf16),
        ],
        scratch_shapes=[
            pltpu.VMEM((features, 2 * head_features), full_type),
            pltpu.VMEM((features, head_features), full_type),
            spread,
        ],
        compiler_params=params,
        name="early",
    )(query_mine, key_mine, query_other, key_other, bias_row, shifted, shifted_other, own_bias, swapped, own_value, swapped_value, *ring)
    own_output = [output_mine]
    for k in range(1, noise_size.bit_length() - 1):
        arrived = from_noise(own_output[0] if k == 1 else jnp.concatenate(own_output, axis=0), 2**k)
        own_output.append(arrived)
    own_output, _ = after((own_output, partial))
    swapped_output = [swap_cores(part) for part in own_output]
    keep, got = [], []
    chunks = 2
    each = samples // chunks
    for c in range(chunks):
        kept, give = pl.pallas_call(
            functools.partial(late_kernel, steps, heads, c * each),
            out_shape=[struct((each // 2, record, 2 * rows), f32)] * 2,
            scratch_shapes=[pltpu.VMEM((each, record, 2 * rows), f32), spread],
            compiler_params=params,
            name="late",
        )(partial, queries, key_full, value_full, own_bias, swapped, last)
        keep.append(kept)
        got.append(swap_cores(give))
    updated = []
    for c in range(chunks):
        operands = [*own_output, *swapped_output, activations, output_gate, keep[c], got[c], *updated]
        updated = [
            pl.pallas_call(
                functools.partial(finish_kernel, heads, c * each, len(own_output)),
                in_specs=[pl.BlockSpec(memory_space=pltpu.VMEM)] * (2 * len(own_output) + 4) + [in_hbm] * len(updated),
                out_specs=in_hbm,
                out_shape=struct(activations.shape, bf16),
                input_output_aliases={2 * len(own_output) + 4: 0} if updated else {},
                scratch_shapes=[
                    pltpu.VMEM((each, rows, features), bf16),
                    pltpu.VMEM((head_features, features), output_type),
                    pltpu.SemaphoreType.DMA((each,)),
                ],
                compiler_params=params,
                name="finish",
            )(*operands)
        ]
    return updated[0]


def solution(mesh):
    return jax.shard_map(
        body,
        mesh=mesh,
        in_specs=(
            P("noise", "row", None),
            P("noise", "row", None),
            P("noise", "row", None),
            P("noise", "row", None),
            P("row", "noise", None),
            P(),
            P("noise", None),
            P(),
            P("noise", None),
            P("noise", None),
            P("noise", None),
            P("noise", "row"),
        ),
        out_specs=P("noise", "row", None),
        check_vma=False,
    )
```

```python
import functools
import math

import jax
import jax.numpy as jnp
from jax import lax
from jax.experimental import pallas as pl
from jax.experimental.pallas import tpu as pltpu
from jax.sharding import PartitionSpec as P

epsilon = 1e-05
masked_score = -1e30
absent = 32768.0
log2_e = math.log2(math.e)
vmem_bytes = 40 * 2**20
wide_bytes = 60 * 2**20


def layer_norm(tensor):
    average = jnp.mean(tensor, axis=-1, keepdims=True)
    centred = tensor - average
    variance = jnp.mean(centred * centred, axis=-1, keepdims=True)
    return centred * lax.rsqrt(variance + epsilon)


def shift_kernel(
    activations_hbm,
    scale_hbm,
    shift_hbm,
    mask_hbm,
    query_hbm,
    key_hbm,
    output_hbm,
    shifted_hbm,
    sent_hbm,
    packed_hbm,
    extended_hbm,
    shifted,
    sent,
    extended,
    activations,
    cond_scale,
    cond_shift,
    token_mask,
    query_weight,
    key_weight,
    output_weight,
    sems,
    sems_out,
):
    samples, rows, features = activations.shape
    copies = [pltpu.make_async_copy(mask_hbm, token_mask, sems.at[0])]
    for s in range(samples):
        for t, (source, target) in enumerate(
            ((activations_hbm, activations), (scale_hbm, cond_scale), (shift_hbm, cond_shift))
        ):
            copies.append(pltpu.make_async_copy(source.at[s], target.at[s], sems.at[1 + 3 * s + t]))
    copies.append(pltpu.make_async_copy(query_hbm, query_weight, sems.at[1 + 3 * samples]))
    copies.append(pltpu.make_async_copy(key_hbm, key_weight, sems.at[2 + 3 * samples]))
    copies.append(pltpu.make_async_copy(output_hbm, output_weight, sems.at[3 + 3 * samples]))
    for copy in copies:
        copy.start()
    diagonal = lax.broadcasted_iota(jnp.int32, (rows, rows), 0) == lax.broadcasted_iota(
        jnp.int32, (rows, rows), 1
    )
    copies[0].wait()
    written = []
    for s in range(samples):
        for copy in copies[1 + 3 * s : 4 + 3 * s]:
            copy.wait()
        normed = layer_norm(activations[s].astype(jnp.float32))
        result = cond_scale[s].astype(jnp.float32) * normed + cond_shift[s].astype(jnp.float32)
        flags = jnp.where(diagonal, token_mask[s : s + 1, :].astype(jnp.float32), 0.0)
        valid = jnp.sum(flags, axis=1, keepdims=True) > 0.0
        shifted[s] = result.astype(jnp.bfloat16)
        sent[s] = jnp.where(valid, result, absent).astype(jnp.bfloat16)
        for t, (source, target) in enumerate(((sent, sent_hbm), (shifted, shifted_hbm))):
            written.append(pltpu.make_async_copy(source.at[s], target.at[s], sems_out.at[2 * s + t]))
            written[-1].start()
    core = lax.rem(lax.axis_index("row"), 2)
    half, breadth = packed_hbm.shape[0], query_weight.shape[1]
    for w, weight in enumerate((query_weight, key_weight)):
        copies[1 + 3 * samples + w].wait()
        whole = weight[...].astype(jnp.float32)
        extended[0:half, w * breadth : (w + 1) * breadth] = jnp.where(
            core == 0, whole[:half], whole[half:]
        ).astype(jnp.bfloat16)
    written.append(
        pltpu.make_async_copy(
            extended.at[0:half, 0 : 2 * breadth], packed_hbm, sems_out.at[2 * samples]
        )
    )
    written[-1].start()
    copies[-1].wait()
    extended[:, 2 * breadth :] = output_weight[...]
    written.append(pltpu.make_async_copy(extended, extended_hbm, sems_out.at[2 * samples + 1]))
    written[-1].start()
    for copy in written:
        copy.wait()


def bias_kernel(pair, value_weight, weights, parcel, collected):
    rows, columns, channels = pair.shape
    heads = weights.shape[0]
    per = 8
    record = 2 * heads
    extended = jnp.concatenate(
        [weights[...], jnp.full((heads, channels), 1.0 / channels, jnp.bfloat16)], axis=0
    )
    square = (channels, channels)
    diagonal = lax.broadcasted_iota(jnp.int32, square, 0) == lax.broadcasted_iota(jnp.int32, square, 1)
    centring = (jnp.where(diagonal, 1.0, 0.0) - 1.0 / channels).astype(jnp.bfloat16)
    lane = lax.broadcasted_iota(jnp.int32, (1, rows), 1)
    squares = jnp.zeros((columns, rows), jnp.float32)
    for i in range(rows // per):
        block = pair[i * per : (i + 1) * per].reshape(per * columns, channels)
        centred = jnp.dot(block, centring, preferred_element_type=jnp.float32)
        summed = jnp.sum(centred * centred, axis=1, keepdims=True)
        result = lax.dot_general(
            extended, block, (((1,), (1,)), ((), ())), preferred_element_type=jnp.float32
        )
        for r in range(per):
            row = i * per + r
            collected[row * record : (row + 1) * record, :] = result[:, r * columns : (r + 1) * columns]
            squares = jnp.where(lane == row, summed[r * columns : (r + 1) * columns], squares)
    core = lax.rem(lax.axis_index("row"), 2)
    half = columns // 2
    average = collected[pl.ds(heads, rows, stride=record), :].T
    inverse = lax.rsqrt(squares / channels + epsilon)
    for p in range(heads // 2):
        own, other = [], []
        for h in (2 * p, 2 * p + 1):
            summed = jnp.sum(weights[h : h + 1, :].astype(jnp.float32), axis=1, keepdims=True)
            turned = (collected[pl.ds(h, rows, stride=record), :].T - average * summed) * inverse
            low, up = turned[:half], turned[half:]
            own.append(jnp.where(core == 0, low, up))
            other.append(jnp.where(core == 0, up, low))
        at = p * half
        parcel[at : at + half, :] = jnp.concatenate(own, axis=1).astype(jnp.bfloat16)
        at += heads // 2 * half
        parcel[at : at + half, :] = jnp.concatenate(other[::-1], axis=1).astype(jnp.bfloat16)
    depth, breadth = value_weight.shape
    whole = value_weight[...].astype(jnp.float32)
    kept = jnp.where(core == 0, whole[: depth // 2], whole[depth // 2 :]).astype(jnp.bfloat16)
    at = heads * half
    for t in range(breadth // columns):
        parcel[at : at + depth // 2, :] = kept[:, t * columns : (t + 1) * columns]
        at += depth // 2


def sort_kernel(*refs):
    stacks = refs[-3:]
    for k, parcel in enumerate(refs[:-3]):
        at = 0
        for stack in stacks:
            stack[k] = parcel[at : at + stack.shape[1]]
            at += stack.shape[1]


def stack_kernel(first, *refs):
    stacks = [ref for ref in refs if len(ref.shape) == 3]
    for k, part in enumerate(refs[: -len(stacks)]):
        for t, stack in enumerate(stacks):
            breadth = stack.shape[2]
            stack[k] = part[:, (first + t) * breadth : (first + t + 1) * breadth]


def spread_queries(heads, queries, spread):
    count, head_features = queries.shape
    width = head_features // heads
    reach = spread.shape[1]
    lane = lax.broadcasted_iota(jnp.int32, (1, reach), 1)
    turned = jnp.concatenate([queries[count // 2 :], queries[: count // 2]], axis=0)
    for h in range(heads):
        start, free = (0, reach - 1) if h < heads // 2 else (head_features - reach, 0)
        inside = ((lane >= h * width - start) & (lane < (h + 1) * width - start)).astype(jnp.bfloat16)
        extra = (lane == free).astype(jnp.bfloat16)
        own = (turned if h % 2 else queries)[:, start : start + reach]
        spread[h * count : (h + 1) * count, :] = own * inside + extra


def attend_keys(heads, tokens, keys, values, bias_of, spread):
    head_features = values.shape[0]
    width = head_features // heads
    count, reach = spread.shape[0] // heads, spread.shape[1]
    used = heads // 2 * width
    penalty = jnp.where(tokens[:, 0:1].astype(jnp.float32) > absent / 2, masked_score, 0.0)
    lane = lax.broadcasted_iota(jnp.int32, (1, reach), 1)
    scores = []
    for part in range(2):
        start = part * (head_features - reach)
        inside = lane < used if part == 0 else lane >= reach - used
        extended = jnp.where(inside, keys[:, start : start + reach], penalty).astype(jnp.bfloat16)
        scores.append(
            lax.dot_general(
                extended,
                spread[part * heads // 2 * count : (part + 1) * heads // 2 * count, :],
                (((1,), (1,)), ((), ())),
                preferred_element_type=jnp.float32,
            )
        )
    sums, highs, totals = [], [], []
    for h in range(heads):
        at = h % (heads // 2) * count
        score = scores[h // (heads // 2)][:, at : at + count] * (log2_e / math.sqrt(width))
        score = score + bias_of(h) * log2_e
        high = jnp.max(score, axis=0, keepdims=True)
        probs = jnp.exp2(score - high)
        totals.append(jnp.sum(probs, axis=0, keepdims=True))
        highs.append(high)
        sums.append(
            jnp.dot(
                values[h * width : (h + 1) * width],
                probs.astype(jnp.bfloat16),
                preferred_element_type=jnp.float32,
            )
        )
    return sums, highs, totals


def bias_picker(parcel, swapped, steps, first, rows):
    chip = lax.axis_index("row") // 2
    place = lax.axis_index("noise")
    left = lax.broadcasted_iota(jnp.int32, (1, 2 * rows), 1) < rows

    here = jnp.where(chip % 2 == 1, (chip + 1) // 2, lax.rem(steps - chip // 2, steps))

    def pick(b, h):
        position = lax.rem(here - (first + b) + steps, steps)
        outward = (position > 0) & (position <= steps // 2)
        origin = jnp.where(outward, 2 * position - 1, 2 * lax.rem(steps - position, steps))
        part = origin ^ place
        at = slice(h // 2 * rows, (h // 2 + 1) * rows)
        pairs = parcel[part, at].astype(jnp.float32), swapped[part, at].astype(jnp.float32)
        return jnp.where(left, pairs[h % 2], pairs[1 - h % 2])

    return pick


def early_kernel(steps, heads, query_mine, key_mine, query_other, key_other, query_bias, shifted, shifted_other, own_bias, swapped, own_value, swapped_value, *refs):
    blocks = refs[: steps - 1]
    partial, queries, key_weight, value_weight, full, full_value, spread = refs[steps - 1 :]
    samples, rows, features = shifted.shape
    noise_size, half, _ = query_mine.shape
    breadth = key_weight.shape[1]
    width = breadth // heads
    core = lax.rem(lax.axis_index("row"), 2)
    place = lax.axis_index("noise")
    for query, key, value, of_core in (
        (query_mine, key_mine, own_value, core),
        (query_other, key_other, swapped_value, 1 - core),
    ):
        for k in range(noise_size):
            start = ((place ^ k) * 2 + of_core) * half
            down = pl.ds(pl.multiple_of(start, math.gcd(half, 32)), half)
            full[down, 0:breadth] = query[k].astype(full.dtype)
            full[down, breadth:] = key[k].astype(full.dtype)
            for t in range(breadth // 128):
                at = t * half
                full_value[down, t * 128 : (t + 1) * 128] = value[k, at : at + half].astype(full.dtype)
    key_weight[...] = full[:, breadth : 2 * breadth].astype(jnp.bfloat16)
    value_weight[...] = full_value[...].astype(jnp.float32).T.astype(jnp.bfloat16)
    for side, tokens in enumerate((shifted, shifted_other)):
        result = jnp.dot(
            tokens[...].reshape(samples * rows, features),
            full[:, 0:breadth].astype(jnp.bfloat16),
            preferred_element_type=jnp.float32,
        ) + query_bias[...].astype(jnp.float32)
        queries[:, side * rows : (side + 1) * rows] = result.astype(jnp.bfloat16).reshape(
            samples, rows, breadth
        )
    pick = bias_picker(own_bias, swapped, steps, 0, rows)
    for s in range(samples):
        tokens = jnp.concatenate([block[s] for block in blocks], axis=0)
        keys = jnp.dot(tokens, key_weight[...], preferred_element_type=jnp.float32)
        values = lax.dot_general(
            value_weight[...], tokens, (((1,), (1,)), ((), ())), preferred_element_type=jnp.float32
        ).astype(jnp.bfloat16)
        spread_queries(heads, queries[s], spread)
        sums, highs, totals = attend_keys(
            heads,
            tokens,
            keys,
            values,
            lambda h: jnp.concatenate([pick(b, h) for b in range(steps - 1)], axis=0),
            spread,
        )
        for h in range(heads):
            partial[s, h * width : (h + 1) * width] = sums[h]
            partial[s, breadth + h : breadth + h + 1] = highs[h]
            partial[s, breadth + heads + h : breadth + heads + h + 1] = totals[h]


def late_kernel(steps, heads, first, partial, queries, key_weight, value_weight, own_bias, swapped, block, keep, give, merged, spread):
    samples = merged.shape[0]
    rows = block.shape[1]
    breadth = key_weight.shape[1]
    width = breadth // heads
    pick = bias_picker(own_bias, swapped, steps, steps - 1, rows)
    tokens = block[first : first + samples].reshape(samples * rows, block.shape[2])
    keys = jnp.dot(tokens, key_weight[...], preferred_element_type=jnp.float32)
    values = lax.dot_general(
        value_weight[...], tokens, (((1,), (1,)), ((), ())), preferred_element_type=jnp.float32
    ).astype(jnp.bfloat16)
    for s in range(samples):
        here = slice(s * rows, (s + 1) * rows)
        spread_queries(heads, queries[first + s], spread)
        sums, highs, totals = attend_keys(
            heads, tokens[here], keys[here], values[:, here], lambda h: pick(0, h), spread
        )
        before = partial.at[first + s]
        for h in range(heads):
            at_high = slice(breadth + h, breadth + h + 1)
            at_total = slice(breadth + heads + h, breadth + heads + h + 1)
            high = jnp.maximum(before[at_high], highs[h])
            old, new = jnp.exp2(before[at_high] - high), jnp.exp2(highs[h] - high)
            across = slice(h * width, (h + 1) * width)
            merged[s, across] = before[across] * old + sums[h] * new
            merged[s, at_high] = high
            merged[s, at_total] = before[at_total] * old + totals[h] * new
    half = merged.shape[2] // 2
    left = lax.broadcasted_iota(jnp.int32, (1, 2 * half), 1) < half
    row = lax.broadcasted_iota(jnp.int32, (merged.shape[1], 1), 0)
    head = jnp.where(row < breadth, row // width, (row - breadth) % heads)
    even = head % 2 == 0
    for pair in range(samples // 2):
        a, b = merged[2 * pair], merged[2 * pair + 1]
        lefts = jnp.where(left, a, pltpu.roll(b, half, 1))
        rights = jnp.where(left, pltpu.roll(a, half, 1), b)
        keep[pair] = jnp.where(even, lefts, rights)
        give[pair] = jnp.where(even, rights, lefts)


def finish_kernel(heads, first, groups, activations, output_gate, keep, got, *refs):
    output_parts = [group.at[k] for group in refs[:groups] for k in range(group.shape[0])]
    updated_hbm, updated, output_weight, sems = refs[-4:]
    part_rows = output_parts[0].shape[0]
    breadth = output_weight.shape[0]
    width = breadth // heads
    samples, rows, _ = updated.shape
    place = lax.axis_index("noise")
    for k, part in enumerate(output_parts):
        down = pl.ds(pl.multiple_of((place ^ k) * part_rows, math.gcd(part_rows, 32)), part_rows)
        output_weight[down, :] = part[...].astype(output_weight.dtype)
    writes = []
    for pair in range(samples // 2):
        own, other = keep.at[pair], got.at[pair]
        parts = []
        for h in range(heads):
            at_high = slice(breadth + h, breadth + h + 1)
            at_total = slice(breadth + heads + h, breadth + heads + h + 1)
            across = slice(h * width, (h + 1) * width)
            high = jnp.maximum(own[at_high], other[at_high])
            mine, theirs = jnp.exp2(own[at_high] - high), jnp.exp2(other[at_high] - high)
            total = own[at_total] * mine + other[at_total] * theirs
            parts.append((own[across] * mine + other[across] * theirs) / total)
        attended = jnp.concatenate(parts, axis=0).T.astype(jnp.bfloat16)
        projected = jnp.dot(
            attended, output_weight[...].astype(jnp.bfloat16), preferred_element_type=jnp.float32
        )
        for side in range(2):
            s = 2 * pair + side
            gate = jax.nn.sigmoid(output_gate[first + s].astype(jnp.float32))
            updated[s] = (
                activations[first + s].astype(jnp.float32)
                + gate * projected[side * rows : (side + 1) * rows]
            ).astype(jnp.bfloat16)
            writes.append(pltpu.make_async_copy(updated.at[s], updated_hbm.at[first + s], sems.at[s]))
            writes[-1].start()
    for write in writes:
        write.wait()


def swap_cores(array):
    return lax.ppermute(array, "row", [(i, i ^ 1) for i in range(lax.axis_size("row"))])


def ring_chip(position, steps):
    return 2 * position - 1 if 0 < position <= steps // 2 else 2 * ((steps - position) % steps)


def next_chip(array):
    steps = lax.axis_size("row") // 2
    order = [ring_chip(p, steps) for p in range(steps)]
    pairs = [
        (2 * order[p] + c, 2 * order[(p + 1) % steps] + c) for p in range(steps) for c in range(2)
    ]
    return lax.ppermute(array, "row", pairs)


def from_noise(array, k):
    if k == 0:
        return array
    return lax.ppermute(array, "noise", [(i, i ^ k) for i in range(lax.axis_size("noise"))])


def from_all_noise(own, direct, breadth):
    parts = [own] + [None] * (2 ** len(direct) - 1)
    for k in range(1, len(parts)):
        low = k & -k
        if low == k:
            parts[k] = direct[low.bit_length() - 1]
        else:
            parts[k] = from_noise(parts[k ^ low][:, :breadth], low)
    return parts


def body(
    activations,
    cond_scale,
    cond_shift,
    output_gate,
    pair_repr,
    bias_weight,
    query_weight,
    query_bias,
    key_weight,
    value_weight,
    output_weight,
    token_mask,
):
    samples, rows, features = activations.shape
    heads = bias_weight.shape[1]
    head_features = query_weight.shape[1]
    noise_size = lax.axis_size("noise")
    steps = lax.axis_size("row") // 2
    assert noise_size == steps and pair_repr.shape[1] == 2 * rows
    bf16, f32 = jnp.bfloat16, jnp.float32
    params = pltpu.CompilerParams(vmem_limit_bytes=vmem_bytes)
    struct = jax.ShapeDtypeStruct
    after = lax.optimization_barrier
    half = query_weight.shape[0] // 2

    in_hbm = pl.BlockSpec(memory_space=pltpu.HBM)
    packed_shape, extended_shape = (half, 2 * head_features), (half, 2 * head_features + features)
    assert output_weight.shape == (half, 2 * head_features)
    shifted, sent, packed, extended = pl.pallas_call(
        shift_kernel,
        in_specs=[in_hbm] * 7,
        out_specs=[in_hbm] * 4,
        out_shape=[struct(activations.shape, bf16)] * 2
        + [struct(packed_shape, bf16), struct(extended_shape, bf16)],
        scratch_shapes=[pltpu.VMEM(activations.shape, bf16)] * 2
        + [pltpu.VMEM(extended_shape, bf16)]
        + [pltpu.VMEM(activations.shape, bf16)] * 3
        + [pltpu.VMEM(token_mask.shape, jnp.int32)]
        + [pltpu.VMEM(query_weight.shape, bf16)] * 2
        + [pltpu.VMEM(output_weight.shape, bf16)]
        + [pltpu.SemaphoreType.DMA((3 * samples + 4,)), pltpu.SemaphoreType.DMA((2 * samples + 2,))],
        compiler_params=pltpu.CompilerParams(vmem_limit_bytes=wide_bytes),
        name="shift",
    )(activations, cond_scale, cond_shift, token_mask, query_weight, key_weight, output_weight)

    ring = [sent, next_chip(sent)]
    direct = [from_noise(extended, 1)] + [from_noise(packed, 2**k) for k in range(1, noise_size.bit_length() - 1)]
    head_weights, _ = after((bias_weight.T, packed))
    columns = pair_repr.shape[1]
    tile_rows, piece_rows = heads * rows, head_features // columns * half
    assert output_weight.shape == (half, 2 * head_features)
    parcel = pl.pallas_call(
        bias_kernel,
        out_shape=struct((tile_rows + piece_rows, columns), bf16),
        scratch_shapes=[pltpu.VMEM((rows * 2 * heads, columns), f32)],
        compiler_params=params,
        name="bias",
    )(pair_repr, value_weight, head_weights)
    shifted_other = swap_cores(shifted)
    ring[1], direct, parcel, shifted_other = after((ring[1], direct, parcel, shifted_other))
    ring.append(next_chip(ring[1]))
    parcels = [from_noise(parcel, k) for k in range(noise_size)]
    weights = from_all_noise(extended, direct, 2 * head_features)
    part_shape = (noise_size, half, head_features)
    query_mine, key_mine = pl.pallas_call(
        functools.partial(stack_kernel, 0),
        out_shape=[struct(part_shape, bf16)] * 2,
        compiler_params=params,
        name="stack",
    )(*weights)
    query_other, key_other = swap_cores(query_mine), swap_cores(key_mine)
    output_mine = pl.pallas_call(
        functools.partial(stack_kernel, 1),
        out_shape=struct((2, half, features), bf16),
        compiler_params=params,
        name="stack_output",
    )(extended, direct[0])
    output_mine, _ = after((output_mine, ring[2]))

    for _ in range(steps - 3):
        ring.append(next_chip(ring[-1]))
    last = ring.pop()
    tile_shape, piece_shape = (noise_size, tile_rows // 2, columns), (noise_size, piece_rows, columns)
    own_bias, other_bias, own_value = pl.pallas_call(
        sort_kernel,
        out_shape=[struct(shape, bf16) for shape in (tile_shape, tile_shape, piece_shape)],
        compiler_params=params,
        name="sort",
    )(*parcels)
    swapped = swap_cores(other_bias)
    swapped_value = swap_cores(own_value)

    bias_row = query_bias.reshape(1, head_features)
    record = head_features + 2 * heads
    full_type = f32 if half % 16 else bf16
    output_type = f32 if output_weight.shape[0] % 16 else bf16
    spread = pltpu.VMEM((heads * 2 * rows, 256), bf16)
    partial, queries, key_full, value_full = pl.pallas_call(
        functools.partial(early_kernel, steps, heads),
        out_shape=[
            struct((samples, record, 2 * rows), f32),
            struct((samples, 2 * rows, head_features), bf16),
            struct((features, head_features), bf16),
            struct((head_features, features), bf16),
        ],
        scratch_shapes=[
            pltpu.VMEM((features, 2 * head_features), full_type),
            pltpu.VMEM((features, head_features), full_type),
            spread,
        ],
        compiler_params=params,
        name="early",
    )(query_mine, key_mine, query_other, key_other, bias_row, shifted, shifted_other, own_bias, swapped, own_value, swapped_value, *ring)
    output_parts = [output_mine]
    for k in range(1, noise_size.bit_length() - 1):
        held = jnp.concatenate(output_parts, axis=0) if k > 1 else output_mine
        output_parts.append(from_noise(held, 2**k))
    keep, got = [], []
    chunks = 2
    each = samples // chunks
    for c in range(chunks):
        kept, give = pl.pallas_call(
            functools.partial(late_kernel, steps, heads, c * each),
            out_shape=[struct((each // 2, record, 2 * rows), f32)] * 2,
            scratch_shapes=[pltpu.VMEM((each, record, 2 * rows), f32), spread],
            compiler_params=params,
            name="late",
        )(partial, queries, key_full, value_full, own_bias, swapped, last)
        keep.append(kept)
        got.append(swap_cores(give))
    updated = []
    for c in range(chunks):
        operands = [activations, output_gate, keep[c], got[c], *output_parts, *updated]
        updated = [
            pl.pallas_call(
                functools.partial(finish_kernel, heads, c * each, len(output_parts)),
                in_specs=[pl.BlockSpec(memory_space=pltpu.VMEM)] * (4 + len(output_parts)) + [in_hbm] * len(updated),
                out_specs=in_hbm,
                out_shape=struct(activations.shape, bf16),
                input_output_aliases={4 + len(output_parts): 0} if updated else {},
                scratch_shapes=[
                    pltpu.VMEM((each, rows, features), bf16),
                    pltpu.VMEM((head_features, features), output_type),
                    pltpu.SemaphoreType.DMA((each,)),
                ],
                compiler_params=params,
                name="finish",
            )(*operands)
        ]
    return updated[0]


def solution(mesh):
    return jax.shard_map(
        body,
        mesh=mesh,
        in_specs=(
            P("noise", "row", None),
            P("noise", "row", None),
            P("noise", "row", None),
            P("noise", "row", None),
            P("row", "noise", None),
            P(),
            P("noise", None),
            P(),
            P("noise", None),
            P("noise", None),
            P("noise", None),
            P("noise", "row"),
        ),
        out_specs=P("noise", "row", None),
        check_vma=False,
    )
```

```python
import functools
import math

import jax
import jax.numpy as jnp
from jax import lax
from jax.experimental import pallas as pl
from jax.experimental.pallas import tpu as pltpu
from jax.sharding import PartitionSpec as P

epsilon = 1e-05
masked_score = -1e30
absent = 32768.0
log2_e = math.log2(math.e)
vmem_bytes = 40 * 2**20
wide_bytes = 60 * 2**20


def layer_norm(tensor):
    average = jnp.mean(tensor, axis=-1, keepdims=True)
    centred = tensor - average
    variance = jnp.mean(centred * centred, axis=-1, keepdims=True)
    return centred * lax.rsqrt(variance + epsilon)


def shift_kernel(
    activations_hbm,
    scale_hbm,
    shift_hbm,
    mask_hbm,
    query_hbm,
    key_hbm,
    output_hbm,
    shifted_hbm,
    sent_hbm,
    packed_hbm,
    extended_hbm,
    shifted,
    sent,
    extended,
    activations,
    cond_scale,
    cond_shift,
    token_mask,
    query_weight,
    key_weight,
    output_weight,
    sems,
    sems_out,
):
    samples, rows, features = activations.shape
    copies = [pltpu.make_async_copy(mask_hbm, token_mask, sems.at[0])]
    for s in range(samples):
        for t, (source, target) in enumerate(
            ((activations_hbm, activations), (scale_hbm, cond_scale), (shift_hbm, cond_shift))
        ):
            copies.append(pltpu.make_async_copy(source.at[s], target.at[s], sems.at[1 + 3 * s + t]))
    copies.append(pltpu.make_async_copy(query_hbm, query_weight, sems.at[1 + 3 * samples]))
    copies.append(pltpu.make_async_copy(key_hbm, key_weight, sems.at[2 + 3 * samples]))
    copies.append(pltpu.make_async_copy(output_hbm, output_weight, sems.at[3 + 3 * samples]))
    for copy in copies:
        copy.start()
    diagonal = lax.broadcasted_iota(jnp.int32, (rows, rows), 0) == lax.broadcasted_iota(
        jnp.int32, (rows, rows), 1
    )
    copies[0].wait()
    written = []
    for s in range(samples):
        for copy in copies[1 + 3 * s : 4 + 3 * s]:
            copy.wait()
        normed = layer_norm(activations[s].astype(jnp.float32))
        result = cond_scale[s].astype(jnp.float32) * normed + cond_shift[s].astype(jnp.float32)
        flags = jnp.where(diagonal, token_mask[s : s + 1, :].astype(jnp.float32), 0.0)
        valid = jnp.sum(flags, axis=1, keepdims=True) > 0.0
        shifted[s] = result.astype(jnp.bfloat16)
        sent[s] = jnp.where(valid, result, absent).astype(jnp.bfloat16)
        for t, (source, target) in enumerate(((sent, sent_hbm), (shifted, shifted_hbm))):
            written.append(pltpu.make_async_copy(source.at[s], target.at[s], sems_out.at[2 * s + t]))
            written[-1].start()
    core = lax.rem(lax.axis_index("row"), 2)
    half, breadth = packed_hbm.shape[0], query_weight.shape[1]
    for w, weight in enumerate((query_weight, key_weight)):
        copies[1 + 3 * samples + w].wait()
        whole = weight[...].astype(jnp.float32)
        extended[0:half, w * breadth : (w + 1) * breadth] = jnp.where(
            core == 0, whole[:half], whole[half:]
        ).astype(jnp.bfloat16)
    written.append(
        pltpu.make_async_copy(
            extended.at[0:half, 0 : 2 * breadth], packed_hbm, sems_out.at[2 * samples]
        )
    )
    written[-1].start()
    copies[-1].wait()
    extended[:, 2 * breadth :] = output_weight[...]
    written.append(pltpu.make_async_copy(extended, extended_hbm, sems_out.at[2 * samples + 1]))
    written[-1].start()
    for copy in written:
        copy.wait()


def bias_kernel(pair, value_weight, weights, parcel, collected):
    rows, columns, channels = pair.shape
    heads = weights.shape[0]
    per = 8
    record = 2 * heads
    extended = jnp.concatenate(
        [weights[...], jnp.full((heads, channels), 1.0 / channels, jnp.bfloat16)], axis=0
    )
    square = (channels, channels)
    diagonal = lax.broadcasted_iota(jnp.int32, square, 0) == lax.broadcasted_iota(jnp.int32, square, 1)
    centring = (jnp.where(diagonal, 1.0, 0.0) - 1.0 / channels).astype(jnp.bfloat16)
    lane = lax.broadcasted_iota(jnp.int32, (1, rows), 1)
    squares = jnp.zeros((columns, rows), jnp.float32)
    for i in range(rows // per):
        block = pair[i * per : (i + 1) * per].reshape(per * columns, channels)
        centred = jnp.dot(block, centring, preferred_element_type=jnp.float32)
        summed = jnp.sum(centred * centred, axis=1, keepdims=True)
        result = lax.dot_general(
            extended, block, (((1,), (1,)), ((), ())), preferred_element_type=jnp.float32
        )
        for r in range(per):
            row = i * per + r
            collected[row * record : (row + 1) * record, :] = result[:, r * columns : (r + 1) * columns]
            squares = jnp.where(lane == row, summed[r * columns : (r + 1) * columns], squares)
    core = lax.rem(lax.axis_index("row"), 2)
    half = columns // 2
    average = collected[pl.ds(heads, rows, stride=record), :].T
    inverse = lax.rsqrt(squares / channels + epsilon)
    for p in range(heads // 2):
        own, other = [], []
        for h in (2 * p, 2 * p + 1):
            summed = jnp.sum(weights[h : h + 1, :].astype(jnp.float32), axis=1, keepdims=True)
            turned = (collected[pl.ds(h, rows, stride=record), :].T - average * summed) * inverse
            low, up = turned[:half], turned[half:]
            own.append(jnp.where(core == 0, low, up))
            other.append(jnp.where(core == 0, up, low))
        at = p * half
        parcel[at : at + half, :] = jnp.concatenate(own, axis=1).astype(jnp.bfloat16)
        at += heads // 2 * half
        parcel[at : at + half, :] = jnp.concatenate(other[::-1], axis=1).astype(jnp.bfloat16)
    depth, breadth = value_weight.shape
    whole = value_weight[...].astype(jnp.float32)
    kept = jnp.where(core == 0, whole[: depth // 2], whole[depth // 2 :]).astype(jnp.bfloat16)
    at = heads * half
    for t in range(breadth // columns):
        parcel[at : at + depth // 2, :] = kept[:, t * columns : (t + 1) * columns]
        at += depth // 2


def sort_kernel(*refs):
    stacks = refs[-3:]
    for k, parcel in enumerate(refs[:-3]):
        at = 0
        for stack in stacks:
            stack[k] = parcel[at : at + stack.shape[1]]
            at += stack.shape[1]


def stack_kernel(first, *refs):
    stacks = [ref for ref in refs if len(ref.shape) == 3]
    for k, part in enumerate(refs[: -len(stacks)]):
        rows, breadth = stacks[0].shape[1:]
        tile = part.shape[1]
        for t, stack in enumerate(stacks):
            if tile >= breadth:
                stack[k] = part[:, (first + t) * breadth : (first + t + 1) * breadth]
                continue
            tiles = breadth // tile
            for i in range(tiles):
                at = part.shape[0] - ((len(stacks) - t) * tiles - i) * rows
                stack[k, :, i * tile : (i + 1) * tile] = part[at : at + rows]


def join_kernel(parcel, part, joined):
    rows, breadth = part.shape
    below, tile = parcel.shape
    joined[0:below] = parcel[...]
    for t in range(breadth // tile):
        at = below + t * rows
        joined[at : at + rows] = part[:, t * tile : (t + 1) * tile]


def spread_queries(heads, queries, spread):
    count, head_features = queries.shape
    width = head_features // heads
    reach = spread.shape[1]
    lane = lax.broadcasted_iota(jnp.int32, (1, reach), 1)
    turned = jnp.concatenate([queries[count // 2 :], queries[: count // 2]], axis=0)
    for h in range(heads):
        start, free = (0, reach - 1) if h < heads // 2 else (head_features - reach, 0)
        inside = ((lane >= h * width - start) & (lane < (h + 1) * width - start)).astype(jnp.bfloat16)
        extra = (lane == free).astype(jnp.bfloat16)
        own = (turned if h % 2 else queries)[:, start : start + reach]
        spread[h * count : (h + 1) * count, :] = own * inside + extra


def attend_keys(heads, tokens, keys, values, bias_of, spread):
    head_features = values.shape[0]
    width = head_features // heads
    count, reach = spread.shape[0] // heads, spread.shape[1]
    used = heads // 2 * width
    penalty = jnp.where(tokens[:, 0:1].astype(jnp.float32) > absent / 2, masked_score, 0.0)
    lane = lax.broadcasted_iota(jnp.int32, (1, reach), 1)
    scores = []
    for part in range(2):
        start = part * (head_features - reach)
        inside = lane < used if part == 0 else lane >= reach - used
        extended = jnp.where(inside, keys[:, start : start + reach], penalty).astype(jnp.bfloat16)
        scores.append(
            lax.dot_general(
                extended,
                spread[part * heads // 2 * count : (part + 1) * heads // 2 * count, :],
                (((1,), (1,)), ((), ())),
                preferred_element_type=jnp.float32,
            )
        )
    sums, highs, totals = [], [], []
    for h in range(heads):
        at = h % (heads // 2) * count
        score = scores[h // (heads // 2)][:, at : at + count] * (log2_e / math.sqrt(width))
        score = score + bias_of(h) * log2_e
        high = jnp.max(score, axis=0, keepdims=True)
        probs = jnp.exp2(score - high)
        totals.append(jnp.sum(probs, axis=0, keepdims=True))
        highs.append(high)
        sums.append(
            jnp.dot(
                values[h * width : (h + 1) * width],
                probs.astype(jnp.bfloat16),
                preferred_element_type=jnp.float32,
            )
        )
    return sums, highs, totals


def bias_picker(parcel, swapped, steps, first, rows):
    chip = lax.axis_index("row") // 2
    place = lax.axis_index("noise")
    left = lax.broadcasted_iota(jnp.int32, (1, 2 * rows), 1) < rows

    here = jnp.where(chip % 2 == 1, (chip + 1) // 2, lax.rem(steps - chip // 2, steps))

    def pick(b, h):
        position = lax.rem(here - (first + b) + steps, steps)
        outward = (position > 0) & (position <= steps // 2)
        origin = jnp.where(outward, 2 * position - 1, 2 * lax.rem(steps - position, steps))
        part = origin ^ place
        at = slice(h // 2 * rows, (h // 2 + 1) * rows)
        pairs = parcel[part, at].astype(jnp.float32), swapped[part, at].astype(jnp.float32)
        return jnp.where(left, pairs[h % 2], pairs[1 - h % 2])

    return pick


def early_kernel(steps, heads, query_mine, key_mine, query_other, key_other, query_bias, shifted, shifted_other, own_bias, swapped, own_value, swapped_value, *refs):
    blocks = refs[: steps - 1]
    partial, queries, key_weight, value_weight, full, full_value, spread = refs[steps - 1 :]
    samples, rows, features = shifted.shape
    noise_size, half, _ = query_mine.shape
    breadth = key_weight.shape[1]
    width = breadth // heads
    core = lax.rem(lax.axis_index("row"), 2)
    place = lax.axis_index("noise")
    for query, key, value, of_core in (
        (query_mine, key_mine, own_value, core),
        (query_other, key_other, swapped_value, 1 - core),
    ):
        for k in range(noise_size):
            start = ((place ^ k) * 2 + of_core) * half
            down = pl.ds(pl.multiple_of(start, math.gcd(half, 32)), half)
            full[down, 0:breadth] = query[k].astype(full.dtype)
            full[down, breadth:] = key[k].astype(full.dtype)
            for t in range(breadth // 128):
                at = t * half
                full_value[down, t * 128 : (t + 1) * 128] = value[k, at : at + half].astype(full.dtype)
    key_weight[...] = full[:, breadth : 2 * breadth].astype(jnp.bfloat16)
    value_weight[...] = full_value[...].astype(jnp.float32).T.astype(jnp.bfloat16)
    for side, tokens in enumerate((shifted, shifted_other)):
        result = jnp.dot(
            tokens[...].reshape(samples * rows, features),
            full[:, 0:breadth].astype(jnp.bfloat16),
            preferred_element_type=jnp.float32,
        ) + query_bias[...].astype(jnp.float32)
        queries[:, side * rows : (side + 1) * rows] = result.astype(jnp.bfloat16).reshape(
            samples, rows, breadth
        )
    pick = bias_picker(own_bias, swapped, steps, 0, rows)
    for s in range(samples):
        tokens = jnp.concatenate([block[s] for block in blocks], axis=0)
        keys = jnp.dot(tokens, key_weight[...], preferred_element_type=jnp.float32)
        values = lax.dot_general(
            value_weight[...], tokens, (((1,), (1,)), ((), ())), preferred_element_type=jnp.float32
        ).astype(jnp.bfloat16)
        spread_queries(heads, queries[s], spread)
        sums, highs, totals = attend_keys(
            heads,
            tokens,
            keys,
            values,
            lambda h: jnp.concatenate([pick(b, h) for b in range(steps - 1)], axis=0),
            spread,
        )
        for h in range(heads):
            partial[s, h * width : (h + 1) * width] = sums[h]
            partial[s, breadth + h : breadth + h + 1] = highs[h]
            partial[s, breadth + heads + h : breadth + heads + h + 1] = totals[h]


def late_kernel(steps, heads, first, partial, queries, key_weight, value_weight, own_bias, swapped, block, keep, give, merged, spread):
    samples = merged.shape[0]
    rows = block.shape[1]
    breadth = key_weight.shape[1]
    width = breadth // heads
    pick = bias_picker(own_bias, swapped, steps, steps - 1, rows)
    tokens = block[first : first + samples].reshape(samples * rows, block.shape[2])
    keys = jnp.dot(tokens, key_weight[...], preferred_element_type=jnp.float32)
    values = lax.dot_general(
        value_weight[...], tokens, (((1,), (1,)), ((), ())), preferred_element_type=jnp.float32
    ).astype(jnp.bfloat16)
    for s in range(samples):
        here = slice(s * rows, (s + 1) * rows)
        spread_queries(heads, queries[first + s], spread)
        sums, highs, totals = attend_keys(
            heads, tokens[here], keys[here], values[:, here], lambda h: pick(0, h), spread
        )
        before = partial.at[first + s]
        for h in range(heads):
            at_high = slice(breadth + h, breadth + h + 1)
            at_total = slice(breadth + heads + h, breadth + heads + h + 1)
            high = jnp.maximum(before[at_high], highs[h])
            old, new = jnp.exp2(before[at_high] - high), jnp.exp2(highs[h] - high)
            across = slice(h * width, (h + 1) * width)
            merged[s, across] = before[across] * old + sums[h] * new
            merged[s, at_high] = high
            merged[s, at_total] = before[at_total] * old + totals[h] * new
    half = merged.shape[2] // 2
    left = lax.broadcasted_iota(jnp.int32, (1, 2 * half), 1) < half
    row = lax.broadcasted_iota(jnp.int32, (merged.shape[1], 1), 0)
    head = jnp.where(row < breadth, row // width, (row - breadth) % heads)
    even = head % 2 == 0
    for pair in range(samples // 2):
        a, b = merged[2 * pair], merged[2 * pair + 1]
        lefts = jnp.where(left, a, pltpu.roll(b, half, 1))
        rights = jnp.where(left, pltpu.roll(a, half, 1), b)
        keep[pair] = jnp.where(even, lefts, rights)
        give[pair] = jnp.where(even, rights, lefts)


def finish_kernel(heads, first, groups, activations, output_gate, keep, got, *refs):
    output_parts = [group.at[k] for group in refs[:groups] for k in range(group.shape[0])]
    updated_hbm, updated, output_weight, sems = refs[-4:]
    part_rows = output_parts[0].shape[0]
    breadth = output_weight.shape[0]
    width = breadth // heads
    samples, rows, _ = updated.shape
    place = lax.axis_index("noise")
    for k, part in enumerate(output_parts):
        down = pl.ds(pl.multiple_of((place ^ k) * part_rows, math.gcd(part_rows, 32)), part_rows)
        output_weight[down, :] = part[...].astype(output_weight.dtype)
    writes = []
    for pair in range(samples // 2):
        own, other = keep.at[pair], got.at[pair]
        parts = []
        for h in range(heads):
            at_high = slice(breadth + h, breadth + h + 1)
            at_total = slice(breadth + heads + h, breadth + heads + h + 1)
            across = slice(h * width, (h + 1) * width)
            high = jnp.maximum(own[at_high], other[at_high])
            mine, theirs = jnp.exp2(own[at_high] - high), jnp.exp2(other[at_high] - high)
            total = own[at_total] * mine + other[at_total] * theirs
            parts.append((own[across] * mine + other[across] * theirs) / total)
        attended = jnp.concatenate(parts, axis=0).T.astype(jnp.bfloat16)
        projected = jnp.dot(
            attended, output_weight[...].astype(jnp.bfloat16), preferred_element_type=jnp.float32
        )
        for side in range(2):
            s = 2 * pair + side
            gate = jax.nn.sigmoid(output_gate[first + s].astype(jnp.float32))
            updated[s] = (
                activations[first + s].astype(jnp.float32)
                + gate * projected[side * rows : (side + 1) * rows]
            ).astype(jnp.bfloat16)
            writes.append(pltpu.make_async_copy(updated.at[s], updated_hbm.at[first + s], sems.at[s]))
            writes[-1].start()
    for write in writes:
        write.wait()


def swap_cores(array):
    return lax.ppermute(array, "row", [(i, i ^ 1) for i in range(lax.axis_size("row"))])


def ring_chip(position, steps):
    return 2 * position - 1 if 0 < position <= steps // 2 else 2 * ((steps - position) % steps)


def next_chip(array):
    steps = lax.axis_size("row") // 2
    order = [ring_chip(p, steps) for p in range(steps)]
    pairs = [
        (2 * order[p] + c, 2 * order[(p + 1) % steps] + c) for p in range(steps) for c in range(2)
    ]
    return lax.ppermute(array, "row", pairs)


def from_noise(array, k):
    if k == 0:
        return array
    return lax.ppermute(array, "noise", [(i, i ^ k) for i in range(lax.axis_size("noise"))])


def from_all_noise(own, direct, third, breadth):
    parts = [own] + [None] * (2 ** len(direct) - 1)
    for k in range(1, len(parts)):
        low = k & -k
        if k == 3:
            parts[k] = third
        elif low == k:
            parts[k] = direct[low.bit_length() - 1]
        else:
            parts[k] = from_noise(parts[k ^ low][:, :breadth], low)
    return parts


def body(
    activations,
    cond_scale,
    cond_shift,
    output_gate,
    pair_repr,
    bias_weight,
    query_weight,
    query_bias,
    key_weight,
    value_weight,
    output_weight,
    token_mask,
):
    samples, rows, features = activations.shape
    heads = bias_weight.shape[1]
    head_features = query_weight.shape[1]
    noise_size = lax.axis_size("noise")
    steps = lax.axis_size("row") // 2
    assert noise_size == steps and pair_repr.shape[1] == 2 * rows
    bf16, f32 = jnp.bfloat16, jnp.float32
    params = pltpu.CompilerParams(vmem_limit_bytes=vmem_bytes)
    struct = jax.ShapeDtypeStruct
    after = lax.optimization_barrier
    half = query_weight.shape[0] // 2

    in_hbm = pl.BlockSpec(memory_space=pltpu.HBM)
    packed_shape, extended_shape = (half, 2 * head_features), (half, 2 * head_features + features)
    assert output_weight.shape == (half, 2 * head_features)
    shifted, sent, packed, extended = pl.pallas_call(
        shift_kernel,
        in_specs=[in_hbm] * 7,
        out_specs=[in_hbm] * 4,
        out_shape=[struct(activations.shape, bf16)] * 2
        + [struct(packed_shape, bf16), struct(extended_shape, bf16)],
        scratch_shapes=[pltpu.VMEM(activations.shape, bf16)] * 2
        + [pltpu.VMEM(extended_shape, bf16)]
        + [pltpu.VMEM(activations.shape, bf16)] * 3
        + [pltpu.VMEM(token_mask.shape, jnp.int32)]
        + [pltpu.VMEM(query_weight.shape, bf16)] * 2
        + [pltpu.VMEM(output_weight.shape, bf16)]
        + [pltpu.SemaphoreType.DMA((3 * samples + 4,)), pltpu.SemaphoreType.DMA((2 * samples + 2,))],
        compiler_params=pltpu.CompilerParams(vmem_limit_bytes=wide_bytes),
        name="shift",
    )(activations, cond_scale, cond_shift, token_mask, query_weight, key_weight, output_weight)

    ring = [sent, next_chip(sent)]
    direct = [from_noise(extended, 1)] + [from_noise(packed, 2**k) for k in range(1, noise_size.bit_length() - 1)]
    head_weights, _ = after((bias_weight.T, packed))
    columns = pair_repr.shape[1]
    tile_rows, piece_rows = heads * rows, head_features // columns * half
    assert output_weight.shape == (half, 2 * head_features)
    parcel = pl.pallas_call(
        bias_kernel,
        out_shape=struct((tile_rows + piece_rows, columns), bf16),
        scratch_shapes=[pltpu.VMEM((rows * 2 * heads, columns), f32)],
        compiler_params=params,
        name="bias",
    )(pair_repr, value_weight, head_weights)
    shifted_other = swap_cores(shifted)
    ring[1], direct, parcel, shifted_other = after((ring[1], direct, parcel, shifted_other))
    ring.append(next_chip(ring[1]))
    joined = pl.pallas_call(
        join_kernel,
        out_shape=struct((parcel.shape[0] + 2 * piece_rows, columns), bf16),
        compiler_params=params,
        name="join",
    )(parcel, direct[1])
    parcels = [parcel, from_noise(joined, 1)] + [from_noise(parcel, k) for k in range(2, noise_size)]
    weights = from_all_noise(extended, direct, parcels[1], 2 * head_features)
    part_shape = (noise_size, half, head_features)
    query_mine, key_mine = pl.pallas_call(
        functools.partial(stack_kernel, 0),
        out_shape=[struct(part_shape, bf16)] * 2,
        compiler_params=params,
        name="stack",
    )(*weights)
    query_other, key_other = swap_cores(query_mine), swap_cores(key_mine)
    output_mine = pl.pallas_call(
        functools.partial(stack_kernel, 1),
        out_shape=struct((2, half, features), bf16),
        compiler_params=params,
        name="stack_output",
    )(extended, direct[0])
    output_mine, _ = after((output_mine, ring[2]))

    for _ in range(steps - 3):
        ring.append(next_chip(ring[-1]))
    last = ring.pop()
    tile_shape, piece_shape = (noise_size, tile_rows // 2, columns), (noise_size, piece_rows, columns)
    own_bias, other_bias, own_value = pl.pallas_call(
        sort_kernel,
        out_shape=[struct(shape, bf16) for shape in (tile_shape, tile_shape, piece_shape)],
        compiler_params=params,
        name="sort",
    )(*parcels)
    swapped = swap_cores(other_bias)
    swapped_value = swap_cores(own_value)

    bias_row = query_bias.reshape(1, head_features)
    record = head_features + 2 * heads
    full_type = f32 if half % 16 else bf16
    output_type = f32 if output_weight.shape[0] % 16 else bf16
    spread = pltpu.VMEM((heads * 2 * rows, 256), bf16)
    partial, queries, key_full, value_full = pl.pallas_call(
        functools.partial(early_kernel, steps, heads),
        out_shape=[
            struct((samples, record, 2 * rows), f32),
            struct((samples, 2 * rows, head_features), bf16),
            struct((features, head_features), bf16),
            struct((head_features, features), bf16),
        ],
        scratch_shapes=[
            pltpu.VMEM((features, 2 * head_features), full_type),
            pltpu.VMEM((features, head_features), full_type),
            spread,
        ],
        compiler_params=params,
        name="early",
    )(query_mine, key_mine, query_other, key_other, bias_row, shifted, shifted_other, own_bias, swapped, own_value, swapped_value, *ring)
    output_parts = [output_mine]
    for k in range(1, noise_size.bit_length() - 1):
        held = jnp.concatenate(output_parts, axis=0) if k > 1 else output_mine
        output_parts.append(from_noise(held, 2**k))
    keep, got = [], []
    chunks = 2
    each = samples // chunks
    for c in range(chunks):
        kept, give = pl.pallas_call(
            functools.partial(late_kernel, steps, heads, c * each),
            out_shape=[struct((each // 2, record, 2 * rows), f32)] * 2,
            scratch_shapes=[pltpu.VMEM((each, record, 2 * rows), f32), spread],
            compiler_params=params,
            name="late",
        )(partial, queries, key_full, value_full, own_bias, swapped, last)
        keep.append(kept)
        got.append(swap_cores(give))
    updated = []
    for c in range(chunks):
        operands = [activations, output_gate, keep[c], got[c], *output_parts, *updated]
        updated = [
            pl.pallas_call(
                functools.partial(finish_kernel, heads, c * each, len(output_parts)),
                in_specs=[pl.BlockSpec(memory_space=pltpu.VMEM)] * (4 + len(output_parts)) + [in_hbm] * len(updated),
                out_specs=in_hbm,
                out_shape=struct(activations.shape, bf16),
                input_output_aliases={4 + len(output_parts): 0} if updated else {},
                scratch_shapes=[
                    pltpu.VMEM((each, rows, features), bf16),
                    pltpu.VMEM((head_features, features), output_type),
                    pltpu.SemaphoreType.DMA((each,)),
                ],
                compiler_params=params,
                name="finish",
            )(*operands)
        ]
    return updated[0]


def solution(mesh):
    return jax.shard_map(
        body,
        mesh=mesh,
        in_specs=(
            P("noise", "row", None),
            P("noise", "row", None),
            P("noise", "row", None),
            P("noise", "row", None),
            P("row", "noise", None),
            P(),
            P("noise", None),
            P(),
            P("noise", None),
            P("noise", None),
            P("noise", None),
            P("noise", "row"),
        ),
        out_specs=P("noise", "row", None),
        check_vma=False,
    )
```

```python
import functools
import math

import jax
import jax.numpy as jnp
from jax import lax
from jax.experimental import pallas as pl
from jax.experimental.pallas import tpu as pltpu
from jax.sharding import PartitionSpec as P

epsilon = 1e-05
masked_score = -1e30
absent = 32768.0
log2_e = math.log2(math.e)
vmem_bytes = 40 * 2**20
wide_bytes = 60 * 2**20


def layer_norm(tensor):
    average = jnp.mean(tensor, axis=-1, keepdims=True)
    centred = tensor - average
    variance = jnp.mean(centred * centred, axis=-1, keepdims=True)
    return centred * lax.rsqrt(variance + epsilon)


def shift_kernel(
    activations_hbm,
    scale_hbm,
    shift_hbm,
    mask_hbm,
    query_hbm,
    key_hbm,
    output_hbm,
    shifted_hbm,
    sent_hbm,
    extended_hbm,
    shifted,
    sent,
    extended,
    activations,
    cond_scale,
    cond_shift,
    token_mask,
    query_weight,
    key_weight,
    output_weight,
    sems,
    sems_out,
):
    samples, rows, features = activations.shape
    weights = ((query_hbm, query_weight), (key_hbm, key_weight), (output_hbm, output_weight))
    weight_copies = [
        pltpu.make_async_copy(source, target, sems.at[1 + 3 * samples + w])
        for w, (source, target) in enumerate(weights)
    ]
    copies = [pltpu.make_async_copy(mask_hbm, token_mask, sems.at[0])]
    for s in range(samples):
        for t, (source, target) in enumerate(
            ((activations_hbm, activations), (scale_hbm, cond_scale), (shift_hbm, cond_shift))
        ):
            copies.append(pltpu.make_async_copy(source.at[s], target.at[s], sems.at[1 + 3 * s + t]))
    for copy in weight_copies + copies:
        copy.start()
    diagonal = lax.broadcasted_iota(jnp.int32, (rows, rows), 0) == lax.broadcasted_iota(
        jnp.int32, (rows, rows), 1
    )
    core = lax.rem(lax.axis_index("row"), 2)
    half, breadth = extended.shape[0], query_weight.shape[1]
    for copy in weight_copies:
        copy.wait()
    for w, weight in enumerate((query_weight, key_weight)):
        whole = weight[...].astype(jnp.float32)
        extended[:, w * breadth : (w + 1) * breadth] = jnp.where(
            core == 0, whole[:half], whole[half:]
        ).astype(jnp.bfloat16)
    extended[:, 2 * breadth :] = output_weight[...]
    written = [pltpu.make_async_copy(extended, extended_hbm, sems_out.at[2 * samples])]
    written[0].start()
    copies[0].wait()
    for s in range(samples):
        for copy in copies[1 + 3 * s : 4 + 3 * s]:
            copy.wait()
        normed = layer_norm(activations[s].astype(jnp.float32))
        result = cond_scale[s].astype(jnp.float32) * normed + cond_shift[s].astype(jnp.float32)
        flags = jnp.where(diagonal, token_mask[s : s + 1, :].astype(jnp.float32), 0.0)
        valid = jnp.sum(flags, axis=1, keepdims=True) > 0.0
        shifted[s] = result.astype(jnp.bfloat16)
        sent[s] = jnp.where(valid, result, absent).astype(jnp.bfloat16)
        for t, (source, target) in enumerate(((sent, sent_hbm), (shifted, shifted_hbm))):
            written.append(pltpu.make_async_copy(source.at[s], target.at[s], sems_out.at[2 * s + t]))
            written[-1].start()
    for copy in written:
        copy.wait()


def bias_kernel(pair, value_weight, weights, parcel, collected):
    rows, columns, channels = pair.shape
    heads = weights.shape[0]
    per = 8
    record = 2 * heads
    extended = jnp.concatenate(
        [weights[...], jnp.full((heads, channels), 1.0 / channels, jnp.bfloat16)], axis=0
    )
    square = (channels, channels)
    diagonal = lax.broadcasted_iota(jnp.int32, square, 0) == lax.broadcasted_iota(jnp.int32, square, 1)
    centring = (jnp.where(diagonal, 1.0, 0.0) - 1.0 / channels).astype(jnp.bfloat16)
    lane = lax.broadcasted_iota(jnp.int32, (1, rows), 1)
    squares = jnp.zeros((columns, rows), jnp.float32)
    for i in range(rows // per):
        block = pair[i * per : (i + 1) * per].reshape(per * columns, channels)
        centred = jnp.dot(block, centring, preferred_element_type=jnp.float32)
        summed = jnp.sum(centred * centred, axis=1, keepdims=True)
        result = lax.dot_general(
            extended, block, (((1,), (1,)), ((), ())), preferred_element_type=jnp.float32
        )
        for r in range(per):
            row = i * per + r
            collected[row * record : (row + 1) * record, :] = result[:, r * columns : (r + 1) * columns]
            squares = jnp.where(lane == row, summed[r * columns : (r + 1) * columns], squares)
    core = lax.rem(lax.axis_index("row"), 2)
    half = columns // 2
    average = collected[pl.ds(heads, rows, stride=record), :].T
    inverse = lax.rsqrt(squares / channels + epsilon)
    for p in range(heads // 2):
        own, other = [], []
        for h in (2 * p, 2 * p + 1):
            summed = jnp.sum(weights[h : h + 1, :].astype(jnp.float32), axis=1, keepdims=True)
            turned = (collected[pl.ds(h, rows, stride=record), :].T - average * summed) * inverse
            low, up = turned[:half], turned[half:]
            own.append(jnp.where(core == 0, low, up))
            other.append(jnp.where(core == 0, up, low))
        at = p * half
        parcel[at : at + half, :] = jnp.concatenate(own, axis=1).astype(jnp.bfloat16)
        at += heads // 2 * half
        parcel[at : at + half, :] = jnp.concatenate(other[::-1], axis=1).astype(jnp.bfloat16)
    depth, breadth = value_weight.shape
    whole = value_weight[...].astype(jnp.float32)
    kept = jnp.where(core == 0, whole[: depth // 2], whole[depth // 2 :]).astype(jnp.bfloat16)
    at = heads * half
    for t in range(breadth // columns):
        parcel[at : at + depth // 2, :] = kept[:, t * columns : (t + 1) * columns]
        at += depth // 2


def sort_kernel(*refs):
    stacks = refs[-3:]
    for k, parcel in enumerate(refs[:-3]):
        at = 0
        for stack in stacks:
            stack[k] = parcel[at : at + stack.shape[1]]
            at += stack.shape[1]


def stack_kernel(first, *refs):
    stacks = [ref for ref in refs if len(ref.shape) == 3]
    for k, part in enumerate(refs[: -len(stacks)]):
        for t, stack in enumerate(stacks):
            breadth = stack.shape[2]
            stack[k] = part[:, (first + t) * breadth : (first + t + 1) * breadth]


def spread_queries(heads, queries, spread):
    count, head_features = queries.shape
    width = head_features // heads
    reach = spread.shape[1]
    lane = lax.broadcasted_iota(jnp.int32, (1, reach), 1)
    turned = jnp.concatenate([queries[count // 2 :], queries[: count // 2]], axis=0)
    for h in range(heads):
        start, free = (0, reach - 1) if h < heads // 2 else (head_features - reach, 0)
        inside = ((lane >= h * width - start) & (lane < (h + 1) * width - start)).astype(jnp.bfloat16)
        extra = (lane == free).astype(jnp.bfloat16)
        own = (turned if h % 2 else queries)[:, start : start + reach]
        spread[h * count : (h + 1) * count, :] = own * inside + extra


def attend_keys(heads, tokens, keys, values, bias_of, spread):
    head_features = values.shape[0]
    width = head_features // heads
    count, reach = spread.shape[0] // heads, spread.shape[1]
    used = heads // 2 * width
    penalty = jnp.where(tokens[:, 0:1].astype(jnp.float32) > absent / 2, masked_score, 0.0)
    lane = lax.broadcasted_iota(jnp.int32, (1, reach), 1)
    scores = []
    for part in range(2):
        start = part * (head_features - reach)
        inside = lane < used if part == 0 else lane >= reach - used
        extended = jnp.where(inside, keys[:, start : start + reach], penalty).astype(jnp.bfloat16)
        scores.append(
            lax.dot_general(
                extended,
                spread[part * heads // 2 * count : (part + 1) * heads // 2 * count, :],
                (((1,), (1,)), ((), ())),
                preferred_element_type=jnp.float32,
            )
        )
    sums, highs, totals = [], [], []
    for h in range(heads):
        at = h % (heads // 2) * count
        score = scores[h // (heads // 2)][:, at : at + count] * (log2_e / math.sqrt(width))
        score = score + bias_of(h) * log2_e
        high = jnp.max(score, axis=0, keepdims=True)
        probs = jnp.exp2(score - high)
        totals.append(jnp.sum(probs, axis=0, keepdims=True))
        highs.append(high)
        sums.append(
            jnp.dot(
                values[h * width : (h + 1) * width],
                probs.astype(jnp.bfloat16),
                preferred_element_type=jnp.float32,
            )
        )
    return sums, highs, totals


def bias_picker(parcel, swapped, steps, first, rows):
    chip = lax.axis_index("row") // 2
    place = lax.axis_index("noise")
    left = lax.broadcasted_iota(jnp.int32, (1, 2 * rows), 1) < rows

    here = jnp.where(chip % 2 == 1, (chip + 1) // 2, lax.rem(steps - chip // 2, steps))

    def pick(b, h):
        position = lax.rem(here - (first + b) + steps, steps)
        outward = (position > 0) & (position <= steps // 2)
        origin = jnp.where(outward, 2 * position - 1, 2 * lax.rem(steps - position, steps))
        part = origin ^ place
        at = slice(h // 2 * rows, (h // 2 + 1) * rows)
        pairs = parcel[part, at].astype(jnp.float32), swapped[part, at].astype(jnp.float32)
        return jnp.where(left, pairs[h % 2], pairs[1 - h % 2])

    return pick


def early_kernel(steps, heads, query_mine, key_mine, query_other, key_other, query_bias, shifted, shifted_other, own_bias, swapped, own_value, swapped_value, *refs):
    blocks = refs[: steps - 1]
    partial, queries, key_weight, value_weight, full, full_value, spread = refs[steps - 1 :]
    samples, rows, features = shifted.shape
    noise_size, half, _ = query_mine.shape
    breadth = key_weight.shape[1]
    width = breadth // heads
    core = lax.rem(lax.axis_index("row"), 2)
    place = lax.axis_index("noise")
    for query, key, value, of_core in (
        (query_mine, key_mine, own_value, core),
        (query_other, key_other, swapped_value, 1 - core),
    ):
        for k in range(noise_size):
            start = ((place ^ k) * 2 + of_core) * half
            down = pl.ds(pl.multiple_of(start, math.gcd(half, 32)), half)
            full[down, 0:breadth] = query[k].astype(full.dtype)
            full[down, breadth:] = key[k].astype(full.dtype)
            for t in range(breadth // 128):
                at = t * half
                full_value[down, t * 128 : (t + 1) * 128] = value[k, at : at + half].astype(full.dtype)
    key_weight[...] = full[:, breadth : 2 * breadth].astype(jnp.bfloat16)
    value_weight[...] = full_value[...].astype(jnp.float32).T.astype(jnp.bfloat16)
    for side, tokens in enumerate((shifted, shifted_other)):
        result = jnp.dot(
            tokens[...].reshape(samples * rows, features),
            full[:, 0:breadth].astype(jnp.bfloat16),
            preferred_element_type=jnp.float32,
        ) + query_bias[...].astype(jnp.float32)
        queries[:, side * rows : (side + 1) * rows] = result.astype(jnp.bfloat16).reshape(
            samples, rows, breadth
        )
    pick = bias_picker(own_bias, swapped, steps, 0, rows)
    for s in range(samples):
        tokens = jnp.concatenate([block[s] for block in blocks], axis=0)
        keys = jnp.dot(tokens, key_weight[...], preferred_element_type=jnp.float32)
        values = lax.dot_general(
            value_weight[...], tokens, (((1,), (1,)), ((), ())), preferred_element_type=jnp.float32
        ).astype(jnp.bfloat16)
        spread_queries(heads, queries[s], spread)
        sums, highs, totals = attend_keys(
            heads,
            tokens,
            keys,
            values,
            lambda h: jnp.concatenate([pick(b, h) for b in range(steps - 1)], axis=0),
            spread,
        )
        for h in range(heads):
            partial[s, h * width : (h + 1) * width] = sums[h]
            partial[s, breadth + h : breadth + h + 1] = highs[h]
            partial[s, breadth + heads + h : breadth + heads + h + 1] = totals[h]


def late_kernel(steps, heads, first, partial, queries, key_weight, value_weight, own_bias, swapped, block, keep, give, merged, spread):
    samples = merged.shape[0]
    rows = block.shape[1]
    breadth = key_weight.shape[1]
    width = breadth // heads
    pick = bias_picker(own_bias, swapped, steps, steps - 1, rows)
    tokens = block[first : first + samples].reshape(samples * rows, block.shape[2])
    keys = jnp.dot(tokens, key_weight[...], preferred_element_type=jnp.float32)
    values = lax.dot_general(
        value_weight[...], tokens, (((1,), (1,)), ((), ())), preferred_element_type=jnp.float32
    ).astype(jnp.bfloat16)
    for s in range(samples):
        here = slice(s * rows, (s + 1) * rows)
        spread_queries(heads, queries[first + s], spread)
        sums, highs, totals = attend_keys(
            heads, tokens[here], keys[here], values[:, here], lambda h: pick(0, h), spread
        )
        before = partial.at[first + s]
        for h in range(heads):
            at_high = slice(breadth + h, breadth + h + 1)
            at_total = slice(breadth + heads + h, breadth + heads + h + 1)
            high = jnp.maximum(before[at_high], highs[h])
            old, new = jnp.exp2(before[at_high] - high), jnp.exp2(highs[h] - high)
            across = slice(h * width, (h + 1) * width)
            merged[s, across] = before[across] * old + sums[h] * new
            merged[s, at_high] = high
            merged[s, at_total] = before[at_total] * old + totals[h] * new
    half = merged.shape[2] // 2
    left = lax.broadcasted_iota(jnp.int32, (1, 2 * half), 1) < half
    row = lax.broadcasted_iota(jnp.int32, (merged.shape[1], 1), 0)
    head = jnp.where(row < breadth, row // width, (row - breadth) % heads)
    even = head % 2 == 0
    for pair in range(samples // 2):
        a, b = merged[2 * pair], merged[2 * pair + 1]
        lefts = jnp.where(left, a, pltpu.roll(b, half, 1))
        rights = jnp.where(left, pltpu.roll(a, half, 1), b)
        keep[pair] = jnp.where(even, lefts, rights)
        give[pair] = jnp.where(even, rights, lefts)


def finish_kernel(heads, first, groups, activations, output_gate, keep, got, *refs):
    direct, *arrived = refs[:groups]
    updated_hbm, updated, output_weight, sems = refs[-4:]
    output_parts = [direct.at[0]]
    for k in range(1, 2 ** (direct.shape[0] - 1)):
        output_parts.append(arrived.pop(0) if k & (k - 1) else direct.at[k.bit_length()])
    part_rows = output_parts[0].shape[0]
    breadth = output_weight.shape[0]
    width = breadth // heads
    samples, rows, _ = updated.shape
    place = lax.axis_index("noise")
    for k, part in enumerate(output_parts):
        down = pl.ds(pl.multiple_of((place ^ k) * part_rows, math.gcd(part_rows, 32)), part_rows)
        output_weight[down, :] = part[...].astype(output_weight.dtype)
    writes = []
    for pair in range(samples // 2):
        own, other = keep.at[pair], got.at[pair]
        parts = []
        for h in range(heads):
            at_high = slice(breadth + h, breadth + h + 1)
            at_total = slice(breadth + heads + h, breadth + heads + h + 1)
            across = slice(h * width, (h + 1) * width)
            high = jnp.maximum(own[at_high], other[at_high])
            mine, theirs = jnp.exp2(own[at_high] - high), jnp.exp2(other[at_high] - high)
            total = own[at_total] * mine + other[at_total] * theirs
            parts.append((own[across] * mine + other[across] * theirs) / total)
        attended = jnp.concatenate(parts, axis=0).T.astype(jnp.bfloat16)
        projected = jnp.dot(
            attended, output_weight[...].astype(jnp.bfloat16), preferred_element_type=jnp.float32
        )
        for side in range(2):
            s = 2 * pair + side
            gate = jax.nn.sigmoid(output_gate[first + s].astype(jnp.float32))
            updated[s] = (
                activations[first + s].astype(jnp.float32)
                + gate * projected[side * rows : (side + 1) * rows]
            ).astype(jnp.bfloat16)
            writes.append(pltpu.make_async_copy(updated.at[s], updated_hbm.at[first + s], sems.at[s]))
            writes[-1].start()
    for write in writes:
        write.wait()


def swap_cores(array):
    return lax.ppermute(array, "row", [(i, i ^ 1) for i in range(lax.axis_size("row"))])


def ring_chip(position, steps):
    return 2 * position - 1 if 0 < position <= steps // 2 else 2 * ((steps - position) % steps)


def next_chip(array):
    steps = lax.axis_size("row") // 2
    order = [ring_chip(p, steps) for p in range(steps)]
    pairs = [
        (2 * order[p] + c, 2 * order[(p + 1) % steps] + c) for p in range(steps) for c in range(2)
    ]
    return lax.ppermute(array, "row", pairs)


def from_noise(array, k):
    if k == 0:
        return array
    return lax.ppermute(array, "noise", [(i, i ^ k) for i in range(lax.axis_size("noise"))])


def from_all_noise(own, direct, breadth):
    parts = [own] + [None] * (2 ** len(direct) - 1)
    for k in range(1, len(parts)):
        low = k & -k
        if low == k:
            parts[k] = direct[low.bit_length() - 1]
        else:
            parts[k] = from_noise(parts[k ^ low][:, :breadth], low)
    return parts


def body(
    activations,
    cond_scale,
    cond_shift,
    output_gate,
    pair_repr,
    bias_weight,
    query_weight,
    query_bias,
    key_weight,
    value_weight,
    output_weight,
    token_mask,
):
    samples, rows, features = activations.shape
    heads = bias_weight.shape[1]
    head_features = query_weight.shape[1]
    noise_size = lax.axis_size("noise")
    steps = lax.axis_size("row") // 2
    assert noise_size == steps and pair_repr.shape[1] == 2 * rows
    bf16, f32 = jnp.bfloat16, jnp.float32
    params = pltpu.CompilerParams(vmem_limit_bytes=vmem_bytes)
    struct = jax.ShapeDtypeStruct
    after = lax.optimization_barrier
    half = query_weight.shape[0] // 2

    in_hbm = pl.BlockSpec(memory_space=pltpu.HBM)
    extended_shape = (half, 2 * head_features + features)
    assert output_weight.shape == (half, 2 * head_features)
    shifted, sent, extended = pl.pallas_call(
        shift_kernel,
        in_specs=[in_hbm] * 7,
        out_specs=[in_hbm] * 3,
        out_shape=[struct(activations.shape, bf16)] * 2
        + [struct(extended_shape, bf16)],
        scratch_shapes=[pltpu.VMEM(activations.shape, bf16)] * 2
        + [pltpu.VMEM(extended_shape, bf16)]
        + [pltpu.VMEM(activations.shape, bf16)] * 3
        + [pltpu.VMEM(token_mask.shape, jnp.int32)]
        + [pltpu.VMEM(query_weight.shape, bf16)] * 2
        + [pltpu.VMEM(output_weight.shape, bf16)]
        + [pltpu.SemaphoreType.DMA((3 * samples + 4,)), pltpu.SemaphoreType.DMA((2 * samples + 1,))],
        compiler_params=pltpu.CompilerParams(vmem_limit_bytes=wide_bytes),
        name="shift",
    )(activations, cond_scale, cond_shift, token_mask, query_weight, key_weight, output_weight)

    ring = [sent, next_chip(sent)]
    direct = [from_noise(extended, 2**k) for k in range(noise_size.bit_length() - 1)]
    head_weights, _ = after((bias_weight.T, extended))
    columns = pair_repr.shape[1]
    tile_rows, piece_rows = heads * rows, head_features // columns * half
    assert output_weight.shape == (half, 2 * head_features)
    parcel = pl.pallas_call(
        bias_kernel,
        out_shape=struct((tile_rows + piece_rows, columns), bf16),
        scratch_shapes=[pltpu.VMEM((rows * 2 * heads, columns), f32)],
        compiler_params=params,
        name="bias",
    )(pair_repr, value_weight, head_weights)
    shifted_other = swap_cores(shifted)
    ring[1], direct, parcel, shifted_other = after((ring[1], direct, parcel, shifted_other))
    ring.append(next_chip(ring[1]))
    parcels = [from_noise(parcel, k) for k in range(noise_size)]
    weights = from_all_noise(extended, direct, 2 * head_features)
    part_shape = (noise_size, half, head_features)
    query_mine, key_mine = pl.pallas_call(
        functools.partial(stack_kernel, 0),
        out_shape=[struct(part_shape, bf16)] * 2,
        compiler_params=params,
        name="stack",
    )(*weights)
    query_other, key_other = swap_cores(query_mine), swap_cores(key_mine)
    output_direct = pl.pallas_call(
        functools.partial(stack_kernel, 1),
        out_shape=struct((1 + len(direct), half, features), bf16),
        compiler_params=params,
        name="stack_output",
    )(extended, *direct)
    output_direct, _ = after((output_direct, ring[2]))

    for _ in range(steps - 3):
        ring.append(next_chip(ring[-1]))
    last = ring.pop()
    tile_shape, piece_shape = (noise_size, tile_rows // 2, columns), (noise_size, piece_rows, columns)
    own_bias, other_bias, own_value = pl.pallas_call(
        sort_kernel,
        out_shape=[struct(shape, bf16) for shape in (tile_shape, tile_shape, piece_shape)],
        compiler_params=params,
        name="sort",
    )(*parcels)
    swapped = swap_cores(other_bias)
    swapped_value = swap_cores(own_value)

    bias_row = query_bias.reshape(1, head_features)
    record = head_features + 2 * heads
    full_type = f32 if half % 16 else bf16
    output_type = f32 if output_weight.shape[0] % 16 else bf16
    spread = pltpu.VMEM((heads * 2 * rows, 256), bf16)
    partial, queries, key_full, value_full = pl.pallas_call(
        functools.partial(early_kernel, steps, heads),
        out_shape=[
            struct((samples, record, 2 * rows), f32),
            struct((samples, 2 * rows, head_features), bf16),
            struct((features, head_features), bf16),
            struct((head_features, features), bf16),
        ],
        scratch_shapes=[
            pltpu.VMEM((features, 2 * head_features), full_type),
            pltpu.VMEM((features, head_features), full_type),
            spread,
        ],
        compiler_params=params,
        name="early",
    )(query_mine, key_mine, query_other, key_other, bias_row, shifted, shifted_other, own_bias, swapped, own_value, swapped_value, *ring)
    output_parts = [output_direct[i] for i in range(1 + len(direct))]
    output_parts = from_all_noise(output_parts[0], output_parts[1:], features)
    forwarded = [k for k in range(noise_size) if k & (k - 1)]
    partial, *arrived = after((partial, *[output_parts[k] for k in forwarded]))
    forwarded = [output_direct] + arrived
    keep, got = [], []
    chunks = 2
    each = samples // chunks
    for c in range(chunks):
        kept, give = pl.pallas_call(
            functools.partial(late_kernel, steps, heads, c * each),
            out_shape=[struct((each // 2, record, 2 * rows), f32)] * 2,
            scratch_shapes=[pltpu.VMEM((each, record, 2 * rows), f32), spread],
            compiler_params=params,
            name="late",
        )(partial, queries, key_full, value_full, own_bias, swapped, last)
        keep.append(kept)
        got.append(swap_cores(give))
    updated = []
    for c in range(chunks):
        operands = [activations, output_gate, keep[c], got[c], *forwarded, *updated]
        updated = [
            pl.pallas_call(
                functools.partial(finish_kernel, heads, c * each, len(forwarded)),
                in_specs=[pl.BlockSpec(memory_space=pltpu.VMEM)] * (4 + len(forwarded)) + [in_hbm] * len(updated),
                out_specs=in_hbm,
                out_shape=struct(activations.shape, bf16),
                input_output_aliases={4 + len(forwarded): 0} if updated else {},
                scratch_shapes=[
                    pltpu.VMEM((each, rows, features), bf16),
                    pltpu.VMEM((head_features, features), output_type),
                    pltpu.SemaphoreType.DMA((each,)),
                ],
                compiler_params=params,
                name="finish",
            )(*operands)
        ]
    return updated[0]


def solution(mesh):
    return jax.shard_map(
        body,
        mesh=mesh,
        in_specs=(
            P("noise", "row", None),
            P("noise", "row", None),
            P("noise", "row", None),
            P("noise", "row", None),
            P("row", "noise", None),
            P(),
            P("noise", None),
            P(),
            P("noise", None),
            P("noise", None),
            P("noise", None),
            P("noise", "row"),
        ),
        out_specs=P("noise", "row", None),
        check_vma=False,
    )
```

```python
import functools
import math

import jax
import jax.numpy as jnp
from jax import lax
from jax.experimental import pallas as pl
from jax.experimental.pallas import tpu as pltpu
from jax.sharding import PartitionSpec as P

epsilon = 1e-05
masked_score = -1e30
absent = 32768.0
log2_e = math.log2(math.e)
vmem_bytes = 40 * 2**20
wide_bytes = 60 * 2**20


def layer_norm(tensor):
    average = jnp.mean(tensor, axis=-1, keepdims=True)
    centred = tensor - average
    variance = jnp.mean(centred * centred, axis=-1, keepdims=True)
    return centred * lax.rsqrt(variance + epsilon)


def shift_kernel(
    activations_hbm,
    scale_hbm,
    shift_hbm,
    mask_hbm,
    query_hbm,
    key_hbm,
    output_hbm,
    shifted_hbm,
    sent_hbm,
    extended_hbm,
    shifted,
    sent,
    extended,
    activations,
    cond_scale,
    cond_shift,
    token_mask,
    query_weight,
    key_weight,
    output_weight,
    sems,
    sems_out,
):
    samples, rows, features = activations.shape
    weights = ((query_hbm, query_weight), (key_hbm, key_weight), (output_hbm, output_weight))
    weight_copies = [
        pltpu.make_async_copy(source, target, sems.at[1 + 3 * samples + w])
        for w, (source, target) in enumerate(weights)
    ]
    copies = [pltpu.make_async_copy(mask_hbm, token_mask, sems.at[0])]
    for s in range(samples):
        for t, (source, target) in enumerate(
            ((activations_hbm, activations), (scale_hbm, cond_scale), (shift_hbm, cond_shift))
        ):
            copies.append(pltpu.make_async_copy(source.at[s], target.at[s], sems.at[1 + 3 * s + t]))
    for copy in weight_copies + copies:
        copy.start()
    diagonal = lax.broadcasted_iota(jnp.int32, (rows, rows), 0) == lax.broadcasted_iota(
        jnp.int32, (rows, rows), 1
    )
    core = lax.rem(lax.axis_index("row"), 2)
    half, breadth = extended.shape[0], query_weight.shape[1]
    for copy in weight_copies:
        copy.wait()
    for w, weight in enumerate((query_weight, key_weight)):
        whole = weight[...].astype(jnp.float32)
        extended[:, w * breadth : (w + 1) * breadth] = jnp.where(
            core == 0, whole[:half], whole[half:]
        ).astype(jnp.bfloat16)
    extended[:, 2 * breadth :] = output_weight[...]
    written = [pltpu.make_async_copy(extended, extended_hbm, sems_out.at[2 * samples])]
    written[0].start()
    copies[0].wait()
    for s in range(samples):
        for copy in copies[1 + 3 * s : 4 + 3 * s]:
            copy.wait()
        normed = layer_norm(activations[s].astype(jnp.float32))
        result = cond_scale[s].astype(jnp.float32) * normed + cond_shift[s].astype(jnp.float32)
        flags = jnp.where(diagonal, token_mask[s : s + 1, :].astype(jnp.float32), 0.0)
        valid = jnp.sum(flags, axis=1, keepdims=True) > 0.0
        shifted[s] = result.astype(jnp.bfloat16)
        sent[s] = jnp.where(valid, result, absent).astype(jnp.bfloat16)
        for t, (source, target) in enumerate(((sent, sent_hbm), (shifted, shifted_hbm))):
            written.append(pltpu.make_async_copy(source.at[s], target.at[s], sems_out.at[2 * s + t]))
            written[-1].start()
    for copy in written:
        copy.wait()


def bias_kernel(pair, value_weight, weights, parcel, collected):
    rows, columns, channels = pair.shape
    heads = weights.shape[0]
    per = 8
    record = 2 * heads
    extended = jnp.concatenate(
        [weights[...], jnp.full((heads, channels), 1.0 / channels, jnp.bfloat16)], axis=0
    )
    square = (channels, channels)
    diagonal = lax.broadcasted_iota(jnp.int32, square, 0) == lax.broadcasted_iota(jnp.int32, square, 1)
    centring = (jnp.where(diagonal, 1.0, 0.0) - 1.0 / channels).astype(jnp.bfloat16)
    lane = lax.broadcasted_iota(jnp.int32, (1, rows), 1)
    squares = jnp.zeros((columns, rows), jnp.float32)
    for i in range(rows // per):
        block = pair[i * per : (i + 1) * per].reshape(per * columns, channels)
        centred = jnp.dot(block, centring, preferred_element_type=jnp.float32)
        summed = jnp.sum(centred * centred, axis=1, keepdims=True)
        result = lax.dot_general(
            extended, block, (((1,), (1,)), ((), ())), preferred_element_type=jnp.float32
        )
        for r in range(per):
            row = i * per + r
            collected[row * record : (row + 1) * record, :] = result[:, r * columns : (r + 1) * columns]
            squares = jnp.where(lane == row, summed[r * columns : (r + 1) * columns], squares)
    core = lax.rem(lax.axis_index("row"), 2)
    half = columns // 2
    average = collected[pl.ds(heads, rows, stride=record), :].T
    inverse = lax.rsqrt(squares / channels + epsilon)
    for p in range(heads // 2):
        own, other = [], []
        for h in (2 * p, 2 * p + 1):
            summed = jnp.sum(weights[h : h + 1, :].astype(jnp.float32), axis=1, keepdims=True)
            turned = (collected[pl.ds(h, rows, stride=record), :].T - average * summed) * inverse
            low, up = turned[:half], turned[half:]
            own.append(jnp.where(core == 0, low, up))
            other.append(jnp.where(core == 0, up, low))
        at = p * half
        parcel[at : at + half, :] = jnp.concatenate(own, axis=1).astype(jnp.bfloat16)
        at += heads // 2 * half
        parcel[at : at + half, :] = jnp.concatenate(other[::-1], axis=1).astype(jnp.bfloat16)
    depth, breadth = value_weight.shape
    whole = value_weight[...].astype(jnp.float32)
    kept = jnp.where(core == 0, whole[: depth // 2], whole[depth // 2 :]).astype(jnp.bfloat16)
    at = heads * half
    for t in range(breadth // columns):
        parcel[at : at + depth // 2, :] = kept[:, t * columns : (t + 1) * columns]
        at += depth // 2


def sort_kernel(*refs):
    stacks = refs[-3:]
    for k, parcel in enumerate(refs[:-3][::-1]):
        at = 0
        for stack in stacks:
            stack[k] = parcel[at : at + stack.shape[1]]
            at += stack.shape[1]


def stack_kernel(first, *refs):
    stacks = [ref for ref in refs if len(ref.shape) == 3]
    for k, part in enumerate(refs[: -len(stacks)]):
        for t, stack in enumerate(stacks):
            breadth = stack.shape[2]
            stack[k] = part[:, (first + t) * breadth : (first + t + 1) * breadth]


def spread_queries(heads, queries, spread):
    count, head_features = queries.shape
    width = head_features // heads
    reach = spread.shape[1]
    lane = lax.broadcasted_iota(jnp.int32, (1, reach), 1)
    turned = jnp.concatenate([queries[count // 2 :], queries[: count // 2]], axis=0)
    for h in range(heads):
        start, free = (0, reach - 1) if h < heads // 2 else (head_features - reach, 0)
        inside = ((lane >= h * width - start) & (lane < (h + 1) * width - start)).astype(jnp.bfloat16)
        extra = (lane == free).astype(jnp.bfloat16)
        own = (turned if h % 2 else queries)[:, start : start + reach]
        spread[h * count : (h + 1) * count, :] = own * inside + extra


def attend_keys(heads, tokens, keys, values, bias_of, spread):
    head_features = values.shape[0]
    width = head_features // heads
    count, reach = spread.shape[0] // heads, spread.shape[1]
    used = heads // 2 * width
    penalty = jnp.where(tokens[:, 0:1].astype(jnp.float32) > absent / 2, masked_score, 0.0)
    lane = lax.broadcasted_iota(jnp.int32, (1, reach), 1)
    scores = []
    for part in range(2):
        start = part * (head_features - reach)
        inside = lane < used if part == 0 else lane >= reach - used
        extended = jnp.where(inside, keys[:, start : start + reach], penalty).astype(jnp.bfloat16)
        scores.append(
            lax.dot_general(
                extended,
                spread[part * heads // 2 * count : (part + 1) * heads // 2 * count, :],
                (((1,), (1,)), ((), ())),
                preferred_element_type=jnp.float32,
            )
        )
    sums, highs, totals = [], [], []
    for h in range(heads):
        at = h % (heads // 2) * count
        score = scores[h // (heads // 2)][:, at : at + count] * (log2_e / math.sqrt(width))
        score = score + bias_of(h) * log2_e
        high = jnp.max(score, axis=0, keepdims=True)
        probs = jnp.exp2(score - high)
        totals.append(jnp.sum(probs, axis=0, keepdims=True))
        highs.append(high)
        sums.append(
            jnp.dot(
                values[h * width : (h + 1) * width],
                probs.astype(jnp.bfloat16),
                preferred_element_type=jnp.float32,
            )
        )
    return sums, highs, totals


def bias_picker(parcel, swapped, steps, first, rows):
    chip = lax.axis_index("row") // 2
    place = lax.axis_index("noise")
    left = lax.broadcasted_iota(jnp.int32, (1, 2 * rows), 1) < rows

    here = jnp.where(chip % 2 == 1, (chip + 1) // 2, lax.rem(steps - chip // 2, steps))

    def pick(b, h):
        position = lax.rem(here - (first + b) + steps, steps)
        outward = (position > 0) & (position <= steps // 2)
        origin = jnp.where(outward, 2 * position - 1, 2 * lax.rem(steps - position, steps))
        part = origin ^ place
        at = slice(h // 2 * rows, (h // 2 + 1) * rows)
        pairs = parcel[part, at].astype(jnp.float32), swapped[part, at].astype(jnp.float32)
        return jnp.where(left, pairs[h % 2], pairs[1 - h % 2])

    return pick


def early_kernel(steps, heads, query_mine, key_mine, query_other, key_other, query_bias, shifted, shifted_other, own_bias, swapped, own_value, swapped_value, *refs):
    blocks = refs[: steps - 1]
    partial, queries, key_weight, value_weight, full, full_value, spread = refs[steps - 1 :]
    samples, rows, features = shifted.shape
    noise_size, half, _ = query_mine.shape
    breadth = key_weight.shape[1]
    width = breadth // heads
    core = lax.rem(lax.axis_index("row"), 2)
    place = lax.axis_index("noise")
    for query, key, value, of_core in (
        (query_mine, key_mine, own_value, core),
        (query_other, key_other, swapped_value, 1 - core),
    ):
        for k in range(noise_size):
            start = ((place ^ k) * 2 + of_core) * half
            down = pl.ds(pl.multiple_of(start, math.gcd(half, 32)), half)
            full[down, 0:breadth] = query[k].astype(full.dtype)
            full[down, breadth:] = key[k].astype(full.dtype)
            for t in range(breadth // 128):
                at = t * half
                full_value[down, t * 128 : (t + 1) * 128] = value[k, at : at + half].astype(full.dtype)
    key_weight[...] = full[:, breadth : 2 * breadth].astype(jnp.bfloat16)
    value_weight[...] = full_value[...].astype(jnp.float32).T.astype(jnp.bfloat16)
    for side, tokens in enumerate((shifted, shifted_other)):
        result = jnp.dot(
            tokens[...].reshape(samples * rows, features),
            full[:, 0:breadth].astype(jnp.bfloat16),
            preferred_element_type=jnp.float32,
        ) + query_bias[...].astype(jnp.float32)
        queries[:, side * rows : (side + 1) * rows] = result.astype(jnp.bfloat16).reshape(
            samples, rows, breadth
        )
    pick = bias_picker(own_bias, swapped, steps, 0, rows)
    for s in range(samples):
        tokens = jnp.concatenate([block[s] for block in blocks], axis=0)
        keys = jnp.dot(tokens, key_weight[...], preferred_element_type=jnp.float32)
        values = lax.dot_general(
            value_weight[...], tokens, (((1,), (1,)), ((), ())), preferred_element_type=jnp.float32
        ).astype(jnp.bfloat16)
        spread_queries(heads, queries[s], spread)
        sums, highs, totals = attend_keys(
            heads,
            tokens,
            keys,
            values,
            lambda h: jnp.concatenate([pick(b, h) for b in range(steps - 1)], axis=0),
            spread,
        )
        for h in range(heads):
            partial[s, h * width : (h + 1) * width] = sums[h]
            partial[s, breadth + h : breadth + h + 1] = highs[h]
            partial[s, breadth + heads + h : breadth + heads + h + 1] = totals[h]


def late_kernel(steps, heads, first, partial, queries, key_weight, value_weight, own_bias, swapped, block, keep, give, merged, spread):
    samples = merged.shape[0]
    rows = block.shape[1]
    breadth = key_weight.shape[1]
    width = breadth // heads
    pick = bias_picker(own_bias, swapped, steps, steps - 1, rows)
    tokens = block[first : first + samples].reshape(samples * rows, block.shape[2])
    keys = jnp.dot(tokens, key_weight[...], preferred_element_type=jnp.float32)
    values = lax.dot_general(
        value_weight[...], tokens, (((1,), (1,)), ((), ())), preferred_element_type=jnp.float32
    ).astype(jnp.bfloat16)
    for s in range(samples):
        here = slice(s * rows, (s + 1) * rows)
        spread_queries(heads, queries[first + s], spread)
        sums, highs, totals = attend_keys(
            heads, tokens[here], keys[here], values[:, here], lambda h: pick(0, h), spread
        )
        before = partial.at[first + s]
        for h in range(heads):
            at_high = slice(breadth + h, breadth + h + 1)
            at_total = slice(breadth + heads + h, breadth + heads + h + 1)
            high = jnp.maximum(before[at_high], highs[h])
            old, new = jnp.exp2(before[at_high] - high), jnp.exp2(highs[h] - high)
            across = slice(h * width, (h + 1) * width)
            merged[s, across] = before[across] * old + sums[h] * new
            merged[s, at_high] = high
            merged[s, at_total] = before[at_total] * old + totals[h] * new
    half = merged.shape[2] // 2
    left = lax.broadcasted_iota(jnp.int32, (1, 2 * half), 1) < half
    row = lax.broadcasted_iota(jnp.int32, (merged.shape[1], 1), 0)
    head = jnp.where(row < breadth, row // width, (row - breadth) % heads)
    even = head % 2 == 0
    for pair in range(samples // 2):
        a, b = merged[2 * pair], merged[2 * pair + 1]
        lefts = jnp.where(left, a, pltpu.roll(b, half, 1))
        rights = jnp.where(left, pltpu.roll(a, half, 1), b)
        keep[pair] = jnp.where(even, lefts, rights)
        give[pair] = jnp.where(even, rights, lefts)


def finish_kernel(heads, first, groups, activations, output_gate, keep, got, *refs):
    direct, *arrived = refs[:groups]
    updated_hbm, updated, output_weight, sems = refs[-4:]
    output_parts = [direct.at[0]]
    for k in range(1, 2 ** (direct.shape[0] - 1)):
        output_parts.append(arrived.pop(0) if k & (k - 1) else direct.at[k.bit_length()])
    part_rows = output_parts[0].shape[0]
    breadth = output_weight.shape[0]
    width = breadth // heads
    samples, rows, _ = updated.shape
    place = lax.axis_index("noise")
    for k, part in enumerate(output_parts):
        down = pl.ds(pl.multiple_of((place ^ k) * part_rows, math.gcd(part_rows, 32)), part_rows)
        output_weight[down, :] = part[...].astype(output_weight.dtype)
    writes = []
    for pair in range(samples // 2):
        own, other = keep.at[pair], got.at[pair]
        parts = []
        for h in range(heads):
            at_high = slice(breadth + h, breadth + h + 1)
            at_total = slice(breadth + heads + h, breadth + heads + h + 1)
            across = slice(h * width, (h + 1) * width)
            high = jnp.maximum(own[at_high], other[at_high])
            mine, theirs = jnp.exp2(own[at_high] - high), jnp.exp2(other[at_high] - high)
            total = own[at_total] * mine + other[at_total] * theirs
            parts.append((own[across] * mine + other[across] * theirs) / total)
        attended = jnp.concatenate(parts, axis=0).T.astype(jnp.bfloat16)
        projected = jnp.dot(
            attended, output_weight[...].astype(jnp.bfloat16), preferred_element_type=jnp.float32
        )
        for side in range(2):
            s = 2 * pair + side
            gate = jax.nn.sigmoid(output_gate[first + s].astype(jnp.float32))
            updated[s] = (
                activations[first + s].astype(jnp.float32)
                + gate * projected[side * rows : (side + 1) * rows]
            ).astype(jnp.bfloat16)
            writes.append(pltpu.make_async_copy(updated.at[s], updated_hbm.at[first + s], sems.at[s]))
            writes[-1].start()
    for write in writes:
        write.wait()


def swap_cores(array):
    return lax.ppermute(array, "row", [(i, i ^ 1) for i in range(lax.axis_size("row"))])


def ring_chip(position, steps):
    return 2 * position - 1 if 0 < position <= steps // 2 else 2 * ((steps - position) % steps)


def next_chip(array):
    steps = lax.axis_size("row") // 2
    order = [ring_chip(p, steps) for p in range(steps)]
    pairs = [
        (2 * order[p] + c, 2 * order[(p + 1) % steps] + c) for p in range(steps) for c in range(2)
    ]
    return lax.ppermute(array, "row", pairs)


def from_noise(array, k):
    if k == 0:
        return array
    return lax.ppermute(array, "noise", [(i, i ^ k) for i in range(lax.axis_size("noise"))])


def from_all_noise(own, direct, breadth):
    parts = [own] + [None] * (2 ** len(direct) - 1)
    for k in range(1, len(parts)):
        low = k & -k
        if low == k:
            parts[k] = direct[low.bit_length() - 1]
        else:
            parts[k] = from_noise(parts[k ^ low][:, :breadth], low)
    return parts


def body(
    activations,
    cond_scale,
    cond_shift,
    output_gate,
    pair_repr,
    bias_weight,
    query_weight,
    query_bias,
    key_weight,
    value_weight,
    output_weight,
    token_mask,
):
    samples, rows, features = activations.shape
    heads = bias_weight.shape[1]
    head_features = query_weight.shape[1]
    noise_size = lax.axis_size("noise")
    steps = lax.axis_size("row") // 2
    assert noise_size == steps and pair_repr.shape[1] == 2 * rows
    bf16, f32 = jnp.bfloat16, jnp.float32
    params = pltpu.CompilerParams(vmem_limit_bytes=vmem_bytes)
    struct = jax.ShapeDtypeStruct
    after = lax.optimization_barrier
    half = query_weight.shape[0] // 2

    in_hbm = pl.BlockSpec(memory_space=pltpu.HBM)
    extended_shape = (half, 2 * head_features + features)
    assert output_weight.shape == (half, 2 * head_features)
    shifted, sent, extended = pl.pallas_call(
        shift_kernel,
        in_specs=[in_hbm] * 7,
        out_specs=[in_hbm] * 3,
        out_shape=[struct(activations.shape, bf16)] * 2
        + [struct(extended_shape, bf16)],
        scratch_shapes=[pltpu.VMEM(activations.shape, bf16)] * 2
        + [pltpu.VMEM(extended_shape, bf16)]
        + [pltpu.VMEM(activations.shape, bf16)] * 3
        + [pltpu.VMEM(token_mask.shape, jnp.int32)]
        + [pltpu.VMEM(query_weight.shape, bf16)] * 2
        + [pltpu.VMEM(output_weight.shape, bf16)]
        + [pltpu.SemaphoreType.DMA((3 * samples + 4,)), pltpu.SemaphoreType.DMA((2 * samples + 1,))],
        compiler_params=pltpu.CompilerParams(vmem_limit_bytes=wide_bytes),
        name="shift",
    )(activations, cond_scale, cond_shift, token_mask, query_weight, key_weight, output_weight)

    ring = [sent, next_chip(sent)]
    direct = [from_noise(extended, 2**k) for k in range(noise_size.bit_length() - 1)]
    head_weights, _ = after((bias_weight.T, extended))
    columns = pair_repr.shape[1]
    tile_rows, piece_rows = heads * rows, head_features // columns * half
    assert output_weight.shape == (half, 2 * head_features)
    parcel = pl.pallas_call(
        bias_kernel,
        out_shape=struct((tile_rows + piece_rows, columns), bf16),
        scratch_shapes=[pltpu.VMEM((rows * 2 * heads, columns), f32)],
        compiler_params=params,
        name="bias",
    )(pair_repr, value_weight, head_weights)
    shifted_other = swap_cores(shifted)
    ring[1], direct, parcel, shifted_other = after((ring[1], direct, parcel, shifted_other))
    ring.append(next_chip(ring[1]))
    parcels = [from_noise(parcel, k) for k in range(noise_size)]
    weights = from_all_noise(extended, direct, 2 * head_features)
    part_shape = (noise_size, half, head_features)
    query_mine, key_mine = pl.pallas_call(
        functools.partial(stack_kernel, 0),
        out_shape=[struct(part_shape, bf16)] * 2,
        compiler_params=params,
        name="stack",
    )(*weights)
    query_other, key_other = swap_cores(query_mine), swap_cores(key_mine)
    output_direct = pl.pallas_call(
        functools.partial(stack_kernel, 1),
        out_shape=struct((1 + len(direct), half, features), bf16),
        compiler_params=params,
        name="stack_output",
    )(extended, *direct)
    output_direct, _ = after((output_direct, ring[2]))

    for _ in range(steps - 3):
        ring.append(next_chip(ring[-1]))
    last = ring.pop()
    tile_shape, piece_shape = (noise_size, tile_rows // 2, columns), (noise_size, piece_rows, columns)
    own_bias, other_bias, own_value = pl.pallas_call(
        sort_kernel,
        out_shape=[struct(shape, bf16) for shape in (tile_shape, tile_shape, piece_shape)],
        compiler_params=params,
        name="sort",
    )(*parcels[::-1])
    swapped = swap_cores(other_bias)
    swapped_value = swap_cores(own_value)

    bias_row = query_bias.reshape(1, head_features)
    record = head_features + 2 * heads
    full_type = f32 if half % 16 else bf16
    output_type = f32 if output_weight.shape[0] % 16 else bf16
    spread = pltpu.VMEM((heads * 2 * rows, 256), bf16)
    partial, queries, key_full, value_full = pl.pallas_call(
        functools.partial(early_kernel, steps, heads),
        out_shape=[
            struct((samples, record, 2 * rows), f32),
            struct((samples, 2 * rows, head_features), bf16),
            struct((features, head_features), bf16),
            struct((head_features, features), bf16),
        ],
        scratch_shapes=[
            pltpu.VMEM((features, 2 * head_features), full_type),
            pltpu.VMEM((features, head_features), full_type),
            spread,
        ],
        compiler_params=params,
        name="early",
    )(query_mine, key_mine, query_other, key_other, bias_row, shifted, shifted_other, own_bias, swapped, own_value, swapped_value, *ring)
    output_parts = [output_direct[i] for i in range(1 + len(direct))]
    output_parts = from_all_noise(output_parts[0], output_parts[1:], features)
    forwarded = [k for k in range(noise_size) if k & (k - 1)]
    partial, *arrived = after((partial, *[output_parts[k] for k in forwarded]))
    forwarded = [output_direct] + arrived
    keep, got = [], []
    chunks = 2
    each = samples // chunks
    for c in range(chunks):
        kept, give = pl.pallas_call(
            functools.partial(late_kernel, steps, heads, c * each),
            out_shape=[struct((each // 2, record, 2 * rows), f32)] * 2,
            scratch_shapes=[pltpu.VMEM((each, record, 2 * rows), f32), spread],
            compiler_params=params,
            name="late",
        )(partial, queries, key_full, value_full, own_bias, swapped, last)
        keep.append(kept)
        got.append(swap_cores(give))
    updated = []
    for c in range(chunks):
        operands = [activations, output_gate, keep[c], got[c], *forwarded, *updated]
        updated = [
            pl.pallas_call(
                functools.partial(finish_kernel, heads, c * each, len(forwarded)),
                in_specs=[pl.BlockSpec(memory_space=pltpu.VMEM)] * (4 + len(forwarded)) + [in_hbm] * len(updated),
                out_specs=in_hbm,
                out_shape=struct(activations.shape, bf16),
                input_output_aliases={4 + len(forwarded): 0} if updated else {},
                scratch_shapes=[
                    pltpu.VMEM((each, rows, features), bf16),
                    pltpu.VMEM((head_features, features), output_type),
                    pltpu.SemaphoreType.DMA((each,)),
                ],
                compiler_params=params,
                name="finish",
            )(*operands)
        ]
    return updated[0]


def solution(mesh):
    return jax.shard_map(
        body,
        mesh=mesh,
        in_specs=(
            P("noise", "row", None),
            P("noise", "row", None),
            P("noise", "row", None),
            P("noise", "row", None),
            P("row", "noise", None),
            P(),
            P("noise", None),
            P(),
            P("noise", None),
            P("noise", None),
            P("noise", None),
            P("noise", "row"),
        ),
        out_specs=P("noise", "row", None),
        check_vma=False,
    )
```
